32 devices in a mesh: tm: 8 (over z, x), mp: 4 (over y, core).
Axes of the slice: x: 2, y: 2, z: 4, core: 2. Of those that a mesh axis runs over, the one named last changes fastest.
Arguments:
- inputs: bfloat16 [1, 2048, 2304], P(None, 'tm', 'mp'), may hold values from -6 to 6
- first_weight: bfloat16 [4608, 3, 2304], P('tm', None, 'mp'), may hold values from -0.09375 to 0.09375
- first_bias: float32 [3, 2304], P(None, 'mp'), may hold values from -2 to 8, as said below
- second_weight: bfloat16 [4608, 3, 2304], P('tm', None, 'mp'), may hold values from -0.09375 to 0.09375
- second_bias: float32 [3, 2304], P(None, 'mp'), may hold values from -2 to 8, as said below
- cotangent: bfloat16 [1, 2048, 2304], P(None, 'tm', 'mp'), may hold values from -6 to 6
Outputs:
- outputs: bfloat16 [1, 2048, 2304], P(None, 'tm', 'mp')
- input_grad: float32 [1, 2048, 2304], P(None, 'tm', 'mp')
- first_weightgrad: float32 [4608, 3, 2304], P('tm', None, 'mp')
- first_biasgrad: float32 [3, 2304], P(None, 'mp')
- second_weightgrad: float32 [4608, 3, 2304], P('tm', None, 'mp')
- second_biasgrad: float32 [3, 2304], P(None, 'mp')
The draws below stay inside these ranges and needn't reach their ends.
Inputs may be any that keep to these rules, and one draw needn't show every extreme that they name: `first_bias`: gate biases in the rows candidate, forget, output. `second_bias`: gate biases in the rows candidate, forget, output.
All inputs are finite; a program needn't handle non-finite values.
Results may differ from the reference program's by a relative error of at most 0.0047.
Values may be sent and summed in bfloat16 or wider, within the bound.
No kernel may reach another device: no remote copies, remote signals or barrier semaphores. Data moves between devices by JAX's collectives and lax.ppermute only.
A program may use at most 256 MiB of HBM per device.

```python
import math
import jax
import jax.numpy as jnp
from jax import lax

D = 2304
SEQ_LEN = 2048
SEQS = 1


def bias_rows(key, forget_low):
    subkeys = jax.random.split(key, 3)
    candidate = jax.random.uniform(subkeys[0], (1, D), jnp.float32, -2.0, 2.0)
    forget = jax.random.uniform(subkeys[1], (1, D), jnp.float32, forget_low, 8.0)
    outgate = jax.random.uniform(subkeys[2], (1, D), jnp.float32, -1.0, 2.0)
    return jnp.concatenate([candidate, forget, outgate], axis=0)


def draw_first_bias(key, part):
    key = jax.random.fold_in(key, 11)
    forget_low = 2.5
    return bias_rows(key, forget_low)


def draw_second_bias(key, part):
    key = jax.random.fold_in(key, 23)
    forget_low = 2.5
    return bias_rows(key, forget_low)


def block_levels(own_key, extent, cuts, least, high):
    gain = 1.0
    for axis_at, blocks in cuts:
        heights = jax.random.uniform(jax.random.fold_in(jax.random.fold_in(own_key, 6), axis_at), (blocks,), jnp.float32, least / len(cuts), high / len(cuts))
        gain = gain * jnp.repeat(jnp.exp(heights), extent[axis_at] // blocks).reshape((-1,) + (1,) * (len(extent) - 1 - axis_at))
    return gain


def bell_draw(stream_key, shape, scale, limit, cuts=(), kind=jnp.bfloat16):
    entries = scale * jax.random.normal(stream_key, shape, jnp.float32)
    if cuts:
        entries = entries * block_levels(stream_key, shape, cuts, -0.22, 0.18)
    return jnp.clip(entries, -limit, limit).astype(kind)


def setup_inputs(seed: int = 0) -> dict:
    key_of = jax.random.split(jax.random.key(seed), 7)
    inputs = bell_draw(key_of[0], (SEQS, SEQ_LEN, D), 1.0, 6.0, ((1, 8), (2, 4)))
    first_weight = bell_draw(key_of[1], (2 * D, 3, D), (2 * D) ** -0.5, 0.09375, ((0, 8), (2, 4)))
    first_bias = draw_first_bias(jax.random.fold_in(key_of[6], 71), 0)
    second_weight = bell_draw(key_of[3], (2 * D, 3, D), (2 * D) ** -0.5, 0.09375, ((0, 8), (2, 4)))
    second_bias = draw_second_bias(jax.random.fold_in(key_of[6], 71), 0)
    cotangent = bell_draw(key_of[5], (SEQS, SEQ_LEN, D), 1.0, 6.0, ((1, 8), (2, 4)))
    return {"inputs": inputs, "first_weight": first_weight, "first_bias": first_bias, "second_weight": second_weight, "second_bias": second_bias, "cotangent": cotangent}


@jax.custom_vjp
def low(v):
    return lax.optimization_barrier(v.astype(jnp.bfloat16)).astype(jnp.float32)

@jax.custom_vjp
def low_back(v):
    return v

def low_keep(v):
    return (low(v), None)

def low_pass(kept, grad):
    return (grad,)

def back_keep(v):
    return (v, None)

def back_low(kept, grad):
    return (low(grad),)
low.defvjp(low_keep, low_pass)
low_back.defvjp(back_keep, back_low)

def qrnn_layer(layer_in, weight, bias):
    previous = jnp.concatenate([jnp.zeros_like(layer_in[:, :1]), layer_in[:, :-1]], axis=1)
    stacked = jnp.concatenate([previous, layer_in], axis=2)
    gates = jnp.einsum('stk,kgd->stgd', stacked, weight, precision=lax.Precision.HIGHEST) + bias
    gates = low_back(gates)
    candidate = jnp.tanh(gates[:, :, 0])
    forget = jax.nn.sigmoid(gates[:, :, 1])
    outgate = jax.nn.sigmoid(gates[:, :, 2])

    def advance(cells_now, pieces):
        forget_now, candidate_now = pieces
        updated = forget_now * cells_now + (1.0 - forget_now) * candidate_now
        return (updated, updated)
    start_cells = jnp.zeros((layer_in.shape[0], weight.shape[2]), jnp.float32)
    finals, cells = lax.scan(advance, start_cells, (jnp.swapaxes(forget, 0, 1), jnp.swapaxes(candidate, 0, 1)))
    cells = jnp.swapaxes(cells, 0, 1)
    return outgate * cells

def two_layers(layer_in, weight_one, bias_one, weight_two, bias_two):
    hidden = low(qrnn_layer(layer_in, weight_one, bias_one))
    return qrnn_layer(hidden, weight_two, bias_two)

def reference(inputs, first_weight, first_bias, second_weight, second_bias, cotangent):
    group = math.gcd(SEQS, 2)
    blocks_in = inputs.astype(jnp.float32).reshape(SEQS // group, group, SEQ_LEN, D)
    blocks_cot = cotangent.astype(jnp.float32).reshape(SEQS // group, group, SEQ_LEN, D)
    weight_one = first_weight.astype(jnp.float32)
    weight_two = second_weight.astype(jnp.float32)
    bias_one = first_bias.astype(jnp.float32)
    bias_two = second_bias.astype(jnp.float32)

    def one_group(totals, pieces):
        block_in, block_cot = pieces
        result, pullback = jax.vjp(two_layers, block_in, weight_one, bias_one, weight_two, bias_two)
        grads = pullback(block_cot)
        summed = tuple((running + extra for running, extra in zip(totals, grads[1:])))
        return (summed, (result, grads[0]))
    start = (jnp.zeros_like(weight_one), jnp.zeros_like(bias_one), jnp.zeros_like(weight_two), jnp.zeros_like(bias_two))
    totals, (results, in_grads) = lax.scan(one_group, start, (blocks_in, blocks_cot))
    outputs = results.reshape(SEQS, SEQ_LEN, D).astype(jnp.bfloat16)
    input_grad = in_grads.reshape(SEQS, SEQ_LEN, D)
    return (outputs, input_grad, totals[0], totals[1], totals[2], totals[3])
```

```python
import jax
import jax.numpy as jnp
from jax import lax
from jax.experimental import pallas as pl
from jax.experimental.pallas import tpu as pltpu
from jax.sharding import PartitionSpec as P

BF = jnp.bfloat16
F32 = jnp.float32
LANES = 128
MIB = 2**20

NZ = 4


def mod(value):
    return lax.rem(value + NZ, NZ)


def flip(bit, by):
    return bit if by == 0 else 1 - bit


def moved(array, target):
    pairs = []
    for z in range(NZ):
        for x in range(2):
            for y in range(2):
                for c in range(2):
                    tz, tx, ty, tc = target(z, x, y, c)
                    pairs.append(((z * 2 + x) * 4 + y * 2 + c, (tz * 2 + tx) * 4 + ty * 2 + tc))
    return lax.ppermute(array, ("tm", "mp"), pairs)


def over_x(array):
    return moved(array, lambda z, x, y, c: (z, 1 - x, y, c))


def over_y(array):
    return moved(array, lambda z, x, y, c: (z, x, 1 - y, c))


def over_core(array):
    return moved(array, lambda z, x, y, c: (z, x, y, 1 - c))


def over_z(array):
    return moved(array, lambda z, x, y, c: ((z + 1) % NZ, x, y, c))


def call(body, outs, args, scratch=(), vmem=48):
    whole = pl.BlockSpec(memory_space=pltpu.VMEM)
    specs = [pl.BlockSpec(memory_space=pltpu.SMEM)] + [whole] * (len(args) - 1)
    return pl.pallas_call(
        body,
        out_shape=[jax.ShapeDtypeStruct(shape, kind) for shape, kind in outs],
        in_specs=specs,
        out_specs=[whole] * len(outs),
        scratch_shapes=list(scratch),
        compiler_params=pltpu.CompilerParams(vmem_limit_bytes=vmem * MIB),
    )(*args)


def pack_weight(ids, weight):
    rows, gates, columns = weight.shape
    own = columns // 8

    def body(ids, w, *rest):
        outs, turned = rest[:8], rest[8]
        z, c = ids[0], ids[3]
        for g in range(gates):
            turned[...] = w[g].astype(F32).T
            for dz in range(NZ):
                for r in range(2):
                    i = mod(z + dz) * 2 + flip(c, r)
                    outs[dz * 2 + r][g] = turned[pl.ds(pl.multiple_of(i * own, 8), own)].astype(BF)

    return call(
        body,
        [((gates, own, rows), BF)] * 8,
        [ids, jnp.transpose(weight, (1, 0, 2))],
        [pltpu.VMEM((columns, rows), F32)],
    )


def send_blocks(blocks):
    return [
        moved(blocks[dz * 2 + r], lambda z, x, y, c, dz=dz, r=r: ((z + dz) % NZ, c ^ r, y, x))
        for dz in range(NZ)
        for r in range(2)
    ]


def return_blocks(blocks):
    def back(dz, r):
        return lambda z, x, y, c: ((z - dz) % NZ, c, y, x ^ r)

    return [moved(blocks[dz * 2 + r], back(dz, r)) for dz in range(NZ) for r in range(2)]


def join_weight(ids, blocks):
    gates, own, rows = blocks[0].shape
    part = gates * own

    def body(ids, *rest):
        ins, (wide, tall), joined = rest[:8], rest[8:10], rest[10]
        z, x = ids[0], ids[1]
        for dz in range(NZ):
            for r in range(2):
                source = mod(z - dz)
                base = (flip(x, r) * 2 + source // 2) * part
                for g in range(gates):
                    at = pl.ds(pl.multiple_of(base + g * own, 8), own)
                    joined[lax.rem(source, 2), at, :] = ins[dz * 2 + r][g].astype(F32)
        for half in range(2):
            at = pl.ds(half * 2 * part, 2 * part)
            both = jnp.concatenate([joined[0, at, :], joined[1, at, :]], axis=1)
            wide[at, :] = both.astype(BF)
        for y in range(2):
            tall[pl.ds(y * rows, rows), :] = joined[y].T.astype(BF)

    return call(
        body,
        [((4 * part, 2 * rows), BF), ((2 * rows, 4 * part), BF)],
        [ids, *blocks],
        [pltpu.VMEM((2, 4 * part, rows), F32)],
    )


def halves(array, axis):
    half = array.shape[axis] // 2
    return lax.slice_in_dim(array, 0, half, axis=axis), lax.slice_in_dim(array, half, 2 * half, axis=axis)


def gather_chips(piece, axis):
    found = []
    for dz in range(NZ):
        if dz:
            piece = over_z(piece)
        from_x, from_y = over_x(piece), over_y(piece)
        found += [piece, from_x, from_y, over_y(halves(from_x, axis)[0]), over_x(halves(from_y, axis)[1])]
    return found


def sum_chips(parts, axis):
    running = None
    for step in range(NZ):
        own, to_x, to_y, diag_a, diag_b = parts[5 * step : 5 * step + 5]
        at_x, at_y = over_y(diag_a), over_x(diag_b)
        xa, xb = halves(to_x, axis)
        ya, yb = halves(to_y, axis)
        sent_x = jnp.concatenate([(xa + at_x).astype(BF), xb.astype(BF)], axis=axis)
        sent_y = jnp.concatenate([ya.astype(BF), (yb + at_y).astype(BF)], axis=axis)
        plane = own + over_x(sent_x) + over_y(sent_y)
        if running is not None:
            plane = plane + over_z(running.astype(BF))
        running = plane
    return running


def partial_gates(ids, wide, found, channel_pieces):
    total, depth = wide.shape
    part = total // 4
    rows = depth // 2
    if channel_pieces:
        own, length = found[0].shape
    else:
        length = found[0].shape[1] * 8
    span = 512

    def body(ids, w, *rest):
        ins, (u, mine, theirs), (prev, cur) = rest[:20], rest[20:23], rest[23:]
        z, x, y, c = ids[0], ids[1], ids[2], ids[3]
        for dz in range(NZ):
            near, at_x, at_y, diag_a, diag_b = ins[5 * dz : 5 * dz + 5]
            source = mod(z - dz)
            if channel_pieces:
                half = length // 2
                for other in range(2):
                    row = pl.multiple_of(flip(y, other) * rows + source * 2 * own, 16)
                    for k in range(2):
                        cols = pl.ds(k * half, half)
                        if other:
                            a, b = at_y[:, cols], (diag_a, diag_b)[k][...]
                        else:
                            a, b = near[:, cols], at_x[:, cols]
                        a, b = a.astype(F32), b.astype(F32)
                        pair = jnp.concatenate([jnp.where(x == 0, a, b), jnp.where(x == 0, b, a)], axis=0)
                        u[pl.ds(row, 2 * own), cols] = pair.astype(BF)
            else:
                block = length // 8
                here = pl.ds(pl.multiple_of((source * 2 + x) * block, block), block)
                there = pl.ds(pl.multiple_of((source * 2 + 1 - x) * block, block), block)
                top = pl.multiple_of(y * rows, 16)
                low = pl.multiple_of((1 - y) * rows, 16)
                u[pl.ds(top, rows), here] = near[...]
                u[pl.ds(top, rows), there] = at_x[...]
                u[pl.ds(low, rows), here] = at_y[...]
                u[pl.ds(low, rows // 2), there] = diag_a[...]
                u[pl.ds(pl.multiple_of(low + rows // 2, 16), rows // 2), there] = diag_b[...]
        for start in range(0, length, span):
            cols = pl.ds(start, span)
            made = jnp.dot(w[...], u[:, cols], preferred_element_type=F32)
            for core in range(2):
                prev[core, :, cols] = made[2 * core * part : (2 * core + 1) * part]
                cur[core, :, cols] = made[(2 * core + 1) * part : (2 * core + 2) * part]
        first = lax.broadcasted_iota(jnp.int32, (part, length), 1) == 0
        for out, core in ((mine, c), (theirs, 1 - c)):
            out[...] = cur[core] + jnp.where(first, 0.0, pltpu.roll(prev[core], 1, 1))

    return call(
        body,
        [((depth, length), BF), ((part, length), F32), ((part, length), F32)],
        [ids, wide, *found],
        [pltpu.VMEM((2, part, length), F32), pltpu.VMEM((2, part, length), F32)],
    )


def scan_lanes(forget, driven, backward):
    own, length = driven.shape
    lane = lax.broadcasted_iota(jnp.int32, (own, LANES), 1)
    count = length // LANES
    blocks = [None] * count
    carry = jnp.zeros((own, 1), F32)
    for block in range(count)[:: -1 if backward else 1]:
        cols = slice(block * LANES, (block + 1) * LANES)
        reach, state = forget[:, cols], driven[:, cols]
        by = 1
        while by < LANES:
            shift = LANES - by if backward else by
            inside = lane < LANES - by if backward else lane >= by
            state = state + jnp.where(inside, reach * pltpu.roll(state, shift, 1), 0.0)
            reach = jnp.where(inside, reach * pltpu.roll(reach, shift, 1), reach)
            by *= 2
        state = state + reach * carry
        carry = state[:, :1] if backward else state[:, LANES - 1 :]
        blocks[block] = state
    return blocks


def squash(value):
    return 1.0 / (1.0 + jnp.exp(-value))


def activate(mine, theirs, bias, own):
    gates = [
        mine[pl.ds(g * own, own), :] + theirs[pl.ds(g * own, own), :] + bias[pl.ds(g * own, own), :]
        for g in range(3)
    ]
    return jnp.tanh(gates[0]), squash(gates[1]), squash(gates[2])


def put_blocks(ref, blocks):
    for at, block in enumerate(blocks):
        ref[:, pl.ds(at * LANES, LANES)] = block


def gate_gradients(grad, candidate, forget, outgate, cells, adjoint, wide, gate_grad, bias_grad):
    own, length = grad.shape
    driven = grad[...] * outgate[...]
    last = lax.broadcasted_iota(jnp.int32, (own, length), 1) == length - 1
    later = jnp.where(last, 0.0, pltpu.roll(forget[...], length - 1, 1))
    put_blocks(adjoint, scan_lanes(later, driven, True))
    f, a = forget[...], candidate[...]
    away = 1.0 - f
    before = jnp.where(
        lax.broadcasted_iota(jnp.int32, (own, length), 1) == 0, 0.0, pltpu.roll(cells[...], 1, 1)
    )
    wide[pl.ds(0, own), :] = adjoint[...] * away * (1.0 - a * a)
    wide[pl.ds(own, own), :] = adjoint[...] * (before - a) * f * away
    o = outgate[...]
    wide[pl.ds(2 * own, own), :] = grad[...] * cells[...] * o * (1.0 - o)
    rounded = wide[...].astype(BF)
    gate_grad[...] = rounded
    total = jnp.sum(rounded.astype(F32), axis=1, keepdims=True)
    bias_grad[...] = jnp.broadcast_to(total, bias_grad.shape)


def first_cells(ids, mine, theirs, bias):
    part, length = mine.shape
    own = part // 3

    def body(ids, mine, theirs, bias, hidden, cand, forg, outg, cells):
        candidate, forget, outgate = activate(mine, theirs, bias, own)
        cand[...], forg[...], outg[...] = candidate, forget, outgate
        put_blocks(cells, scan_lanes(forget, (1.0 - forget) * candidate, False))
        hidden[...] = (outgate * cells[...]).astype(BF)

    return call(
        body,
        [((own, length), BF)] + [((own, length), F32)] * 4,
        [ids, mine, theirs, bias],
    )


def first_gate_grad(ids, grad, saved):
    own, length = grad.shape

    def body(ids, grad, cand, forg, outg, cells, gate_grad, bias_grad, adjoint, wide):
        gate_gradients(grad, cand, forg, outg, cells, adjoint, wide, gate_grad, bias_grad)

    return call(
        body,
        [((3 * own, length), BF), ((3 * own, LANES), F32)],
        [ids, grad, *saved],
        [pltpu.VMEM((own, length), F32), pltpu.VMEM((3 * own, length), F32)],
    )


def second_cells(ids, mine, theirs, bias, cot_pieces):
    part, length = mine.shape
    own = part // 3
    block = length // 8

    def body(ids, mine, theirs, bias, *rest):
        cots, outs = rest[:8], rest[8:16]
        gate_grad, bias_grad = rest[16:18]
        grad, cand, forg, outg, cells, adjoint, wide = rest[18:]
        z, x = ids[0], ids[1]
        for dz in range(NZ):
            for dx in range(2):
                i = mod(z - dz) * 2 + flip(x, dx)
                grad[:, pl.ds(pl.multiple_of(i * block, block), block)] = cots[dz * 2 + dx][...].astype(F32)
        candidate, forget, outgate = activate(mine, theirs, bias, own)
        cand[...], forg[...], outg[...] = candidate, forget, outgate
        put_blocks(cells, scan_lanes(forget, (1.0 - forget) * candidate, False))
        adjoint[...] = outgate * cells[...]
        for dz in range(NZ):
            for dx in range(2):
                i = mod(z + dz) * 2 + flip(x, dx)
                piece = adjoint[:, pl.ds(pl.multiple_of(i * block, block), block)]
                outs[dz * 2 + dx][...] = piece.astype(BF)
        gate_gradients(grad, cand, forg, outg, cells, adjoint, wide, gate_grad, bias_grad)

    made = call(
        body,
        [((own, block), BF)] * 8 + [((part, length), BF), ((part, LANES), F32)],
        [ids, mine, theirs, bias, *cot_pieces],
        [pltpu.VMEM((own, length), F32)] * 6 + [pltpu.VMEM((part, length), F32)],
    )
    return made[:8], made[8], made[9]


def split_cotangent(ids, cotangent):
    channels, block = cotangent.shape
    own = channels // 8

    def body(ids, cot, *rest):
        outs, wide = rest[:8], rest[8]
        wide[...] = cot[...].astype(F32)
        for dz in range(NZ):
            for dx in range(2):
                i = mod(ids[0] + dz) * 2 + flip(ids[1], dx)
                outs[dz * 2 + dx][...] = wide[pl.ds(pl.multiple_of(i * own, 8), own), :].astype(BF)

    return call(body, [((own, block), BF)] * 8, [ids, cotangent], [pltpu.VMEM((channels, block), F32)])


def over_tm(pieces):
    return [
        pieces[dz * 2 + dx]
        if dz == 0 and dx == 0
        else moved(pieces[dz * 2 + dx], lambda z, x, y, c, dz=dz, dx=dx: ((z + dz) % NZ, x ^ dx, y, c))
        for dz in range(NZ)
        for dx in range(2)
    ]


def join_outputs(ids, pieces):
    own, block = pieces[0].shape

    def body(ids, *rest):
        ins, out, wide = rest[:8], rest[8], rest[9]
        for dz in range(NZ):
            for dx in range(2):
                i = mod(ids[0] - dz) * 2 + flip(ids[1], dx)
                wide[pl.ds(pl.multiple_of(i * own, 8), own), :] = ins[dz * 2 + dx][...].astype(F32)
        out[...] = wide[...].astype(BF)

    return call(body, [((8 * own, block), BF)], [ids, *pieces], [pltpu.VMEM((8 * own, block), F32)])[0]


def input_parts(ids, tall, mine, theirs, channel_pieces):
    depth, total = tall.shape
    part, length = mine.shape
    rows = depth // 2
    own = rows // 8
    block = length // 8
    span = 512
    shape = (own, length) if channel_pieces else (rows, block)
    half = (own, length // 2) if channel_pieces else (rows // 2, block)

    def body(ids, w, mine, theirs, grads, *rest):
        outs, v = rest[:20], rest[20]
        z, x, y, c = ids[0], ids[1], ids[2], ids[3]
        last = lax.broadcasted_iota(jnp.int32, (part, length), 1) == length - 1
        for core in range(2):
            now = jnp.where(c == core, mine[...].astype(F32), theirs[...].astype(F32))
            after = jnp.where(last, 0.0, pltpu.roll(now, length - 1, 1))
            grads[pl.ds(core * 2 * part, 2 * part), :] = jnp.concatenate([after, now], axis=0).astype(BF)
        for start in range(0, length, span):
            cols = pl.ds(start, span)
            v[:, cols] = jnp.dot(w[...], grads[:, cols], preferred_element_type=F32)
        for step in range(NZ):
            target = mod(z - 1 - step)

            def piece(dx, dy, k=None):
                i = target * 2 + flip(x, dx)
                if channel_pieces:
                    row = pl.multiple_of(flip(y, dy) * rows + i * own, 8)
                    cols = slice(None) if k is None else pl.ds(k * length // 2, length // 2)
                    return v[pl.ds(row, own), cols]
                cols = pl.ds(pl.multiple_of(i * block, block), block)
                row = flip(y, dy) * rows
                if k is None:
                    return v[pl.ds(pl.multiple_of(row, 8), rows), cols]
                return v[pl.ds(pl.multiple_of(row + k * rows // 2, 8), rows // 2), cols]

            o = outs[5 * step : 5 * step + 5]
            o[0][...] = piece(0, 0)
            o[1][...] = piece(1, 0)
            o[2][...] = piece(0, 1)
            o[3][...] = piece(1, 1, 0).astype(BF)
            o[4][...] = piece(1, 1, 1).astype(BF)

    made = call(
        body,
        [((total, length), BF)] + [(shape, F32), (shape, F32), (shape, F32), (half, BF), (half, BF)] * NZ,
        [ids, tall, mine, theirs],
        [pltpu.VMEM((depth, length), F32)],
    )
    return made[0], made[1:]


def weight_blocks(ids, grads, u, bias_mine, bias_theirs):
    total, length = grads.shape
    depth = u.shape[0]
    part, rows = total // 4, depth // 2
    lanes = -(-(rows + 2) // LANES) * LANES

    def body(ids, grads, u, bias_mine, bias_theirs, *rest):
        outs, made = rest[:8], rest[8]
        z, x, c = ids[0], ids[1], ids[3]
        for y in range(2):
            made[y, :, pl.ds(0, rows)] = lax.dot_general(
                grads[...], u[pl.ds(y * rows, rows), :], (((1,), (1,)), ((), ())), preferred_element_type=F32
            )
        lane = lax.broadcasted_iota(jnp.int32, (part, lanes), 1)
        for r in range(2):
            core = flip(x, r)
            bias = jnp.where(core == c, bias_mine[:, :1], bias_theirs[:, :1])
            high = bias.astype(BF).astype(F32)
            for dz in range(NZ):
                source = mod(z - dz)
                at = pl.ds(pl.multiple_of((core * 2 + source // 2) * part, 8), part)
                block = made[lax.rem(source, 2), at, :]
                block = jnp.where(lane < rows, block, jnp.where(lane == rows, high, bias - high))
                outs[dz * 2 + r][...] = block.astype(BF)

    return call(
        body,
        [((part, lanes), BF)] * 8,
        [ids, grads, u, bias_mine, bias_theirs],
        [pltpu.VMEM((2, total, lanes), F32)],
    )


def unpack_weight(ids, blocks, rows):
    part, lanes = blocks[0].shape
    own = part // 3
    columns = own * 8

    def body(ids, *rest):
        ins, (out, bias), joined = rest[:8], rest[8:10], rest[10]
        z, c = ids[0], ids[3]
        for dz in range(NZ):
            for r in range(2):
                i = mod(z + dz) * 2 + flip(c, r)
                for g in range(3):
                    at = pl.ds(pl.multiple_of(i * own, 8), own)
                    joined[g, at, :] = ins[dz * 2 + r][pl.ds(g * own, own), :].astype(F32)
        for g in range(3):
            turned = joined[g].T
            out[g] = turned[:rows]
            bias[pl.ds(g, 1), :] = turned[rows : rows + 1] + turned[rows + 1 : rows + 2]

    grad, bias = call(
        body,
        [((3, rows, columns), F32), ((3, columns), F32)],
        [ids, *blocks],
        [pltpu.VMEM((3, columns, lanes), F32)],
    )
    return jnp.transpose(grad, (1, 0, 2)), bias


def owned_bias(bias, own):
    i = lax.axis_index("tm")
    return lax.dynamic_slice_in_dim(bias, i * own, own, axis=1).reshape(3 * own, 1)


def owned_channels(inputs, first_weight, first_bias, second_weight, second_bias, cotangent):
    tm, mp = lax.axis_index("tm"), lax.axis_index("mp")
    ids = jnp.stack([tm // 2, tm % 2, mp // 2, mp % 2]).astype(jnp.int32)
    rows = first_weight.shape[0]
    own = first_weight.shape[2] // 8

    w1_sent = send_blocks(pack_weight(ids, first_weight))
    u_found = gather_chips(inputs[0].T, 0)
    wide_1, tall_1 = join_weight(ids, w1_sent)
    w2_sent = send_blocks(pack_weight(ids, second_weight))
    cot_pieces = over_tm(split_cotangent(ids, cotangent[0].T))

    u, mine, theirs = partial_gates(ids, wide_1, u_found, False)
    hidden, *saved = first_cells(ids, mine, over_core(theirs), owned_bias(first_bias, own))
    wide_2, tall_2 = join_weight(ids, w2_sent)
    h_found = gather_chips(hidden, 1)
    h, mine, theirs = partial_gates(ids, wide_2, h_found, True)
    out_pieces, gate_grad, bias_2 = second_cells(
        ids, mine, over_core(theirs), owned_bias(second_bias, own), cot_pieces
    )
    outputs = join_outputs(ids, over_tm(out_pieces))

    grads, parts = input_parts(ids, tall_2, gate_grad, over_core(gate_grad), True)
    hidden_grad = sum_chips(parts, 1)
    blocks = weight_blocks(ids, grads, h, bias_2, over_core(bias_2))
    second_grad, second_bias_grad = unpack_weight(ids, return_blocks(blocks), rows)

    gate_grad, bias_1 = first_gate_grad(ids, hidden_grad, saved)
    grads, parts = input_parts(ids, tall_1, gate_grad, over_core(gate_grad), False)
    input_grad = sum_chips(parts, 0)
    blocks = weight_blocks(ids, grads, u, bias_1, over_core(bias_1))
    first_grad, first_bias_grad = unpack_weight(ids, return_blocks(blocks), rows)
    return (
        outputs.T[None],
        input_grad.T[None],
        first_grad,
        first_bias_grad,
        second_grad,
        second_bias_grad,
    )


def prefix(value, axis, join, neutral, backward):
    count, mine = (lax.axis_size(axis), lax.axis_index(axis))
    pieces = jax.tree.map(lambda part: lax.all_gather(part, axis), value)
    if backward:
        pieces = jax.tree.map(lambda part: part[::-1], pieces)
        mine = count - 1 - mine
    total = jax.tree.map(
        lambda part, zero: jnp.full_like(part, 0) + jnp.asarray(zero, part.dtype), value, neutral
    )

    def hop(position, total):
        longer = join(total, jax.tree.map(lambda part: part[position], pieces))
        return jax.tree.map(lambda new, old: jnp.where(position < mine, new, old), longer, total)

    return lax.fori_loop(0, count - 1, hop, total)


def passed_along(array, axis, by):
    size = lax.axis_size(axis)
    pairs = [(i, i + by) for i in range(size) if 0 <= i + by < size]
    return lax.ppermute(array, axis, pairs)


def affine_join(earlier, later):
    return (earlier[0] * later[0], later[0] * earlier[1] + later[1])


def weight_view(gathered):
    return gathered.reshape(2, gathered.shape[0] // 2, gathered.shape[1] * gathered.shape[2])


def span_prefix(product, offset):
    identity = (jnp.ones_like(product), jnp.zeros_like(offset))
    result = prefix((product, offset), "tm", affine_join, identity, False)
    return result[1]


def span_suffix(product, offset):
    identity = (jnp.ones_like(product), jnp.zeros_like(offset))
    result = prefix((product, offset), "tm", affine_join, identity, True)
    return result[1]


def forward_layer(layer_in, view, bias):
    seq_count, length, channels = layer_in.shape
    prev_row = passed_along(layer_in[:, length - 1 :], "tm", 1)
    previous = jnp.concatenate([prev_row, layer_in[:, : length - 1]], axis=1)
    stacked = jnp.stack([previous, layer_in])
    summed = jnp.einsum(
        "jsck,jkn->scn",
        lax.all_gather(stacked, "mp", axis=3, tiled=True),
        view,
        preferred_element_type=jnp.float32,
    )
    gates = summed.reshape(seq_count, length, 3, channels) + bias
    candidate = jnp.tanh(gates[:, :, 0])
    forget = jax.nn.sigmoid(gates[:, :, 1])
    outgate = jax.nn.sigmoid(gates[:, :, 2])
    product, offset = lax.associative_scan(
        affine_join, (forget, (1.0 - forget) * candidate), axis=1
    )
    carry_in = span_prefix(product[:, length - 1], offset[:, length - 1])
    cells = offset + product * carry_in[:, None]
    cells_prev = jnp.concatenate([carry_in[:, None], cells[:, : length - 1]], axis=1)
    return (outgate * cells, (stacked, candidate, forget, outgate, cells, cells_prev))


def backward_layer(grad_in, saved, view):
    stacked, candidate, forget, outgate, cells, cells_prev = saved
    seq_count, length, channels = grad_in.shape
    driven = grad_in * outgate
    next_forget = jnp.concatenate([forget[:, 1:], jnp.ones_like(forget[:, :1])], axis=1)
    reach, local_adj = lax.associative_scan(
        affine_join, (next_forget[:, ::-1], driven[:, ::-1]), axis=1
    )
    reach = reach[:, ::-1]
    local_adj = local_adj[:, ::-1]
    first_forget = forget[:, 0]
    incoming = span_suffix(first_forget * reach[:, 0], first_forget * local_adj[:, 0])
    adjoint = local_adj + reach * incoming[:, None]
    grad_cand = adjoint * (1.0 - forget) * (1.0 - candidate * candidate)
    grad_forget = adjoint * (cells_prev - candidate) * forget * (1.0 - forget)
    grad_outgate = grad_in * cells * outgate * (1.0 - outgate)
    gate_grad = jnp.stack([grad_cand, grad_forget, grad_outgate], axis=2).astype(jnp.bfloat16)
    flat_grad = gate_grad.reshape(seq_count, length, 3 * channels)
    bias_part = jnp.sum(gate_grad, axis=(0, 1), dtype=jnp.float32)
    back_both = jnp.einsum("scn,jkn->jsck", flat_grad, view, preferred_element_type=jnp.float32)
    from_prev = back_both[0]
    from_current = back_both[1]
    local_grad = from_current + jnp.concatenate(
        [from_prev[:, 1:], jnp.zeros_like(from_prev[:, :1])], axis=1
    )
    tail_rows = from_prev[:, :1]
    shard_grad, tail_shard = (
        lax.psum_scatter(local_grad, "mp", scatter_dimension=2, tiled=True),
        lax.psum_scatter(tail_rows, "mp", scatter_dimension=2, tiled=True),
    )
    tail_next = passed_along(tail_shard, "tm", -1)
    layer_grad = shard_grad + jnp.concatenate(
        [jnp.zeros_like(shard_grad[:, : length - 1]), tail_next], axis=1
    )
    weight_full = jnp.einsum(
        "jsck,scn->jkn",
        lax.all_gather(stacked, "mp", axis=3, tiled=True),
        flat_grad,
        preferred_element_type=jnp.float32,
    )
    weight_full = weight_full.reshape(2 * weight_full.shape[1], 3, channels)
    weight_shard = lax.psum_scatter(weight_full, "tm", scatter_dimension=0, tiled=True)
    bias_grad = lax.psum(bias_part, "tm")
    return (layer_grad, weight_shard, bias_grad)


def per_device(inputs, first_weight, first_bias, second_weight, second_bias, cotangent):
    full_first, full_second = (
        lax.all_gather(first_weight, "tm", axis=0, tiled=True),
        lax.all_gather(second_weight, "tm", axis=0, tiled=True),
    )
    view_first = weight_view(full_first)
    view_second = weight_view(full_second)
    hidden_out, saved_first = forward_layer(inputs, view_first, first_bias)
    hidden = hidden_out.astype(jnp.bfloat16)
    top_out, saved_second = forward_layer(hidden, view_second, second_bias)
    again_first, again_second = (
        lax.all_gather(first_weight, "tm", axis=0, tiled=True),
        lax.all_gather(second_weight, "tm", axis=0, tiled=True),
    )
    back_first = weight_view(again_first)
    back_second = weight_view(again_second)
    hidden_grad, second_weightgrad, second_biasgrad = backward_layer(
        cotangent.astype(jnp.float32), saved_second, back_second
    )
    input_grad, first_weightgrad, first_biasgrad = backward_layer(
        hidden_grad, saved_first, back_first
    )
    return (
        top_out.astype(jnp.bfloat16),
        input_grad,
        first_weightgrad,
        first_biasgrad,
        second_weightgrad,
        second_biasgrad,
    )


def choose(owned):
    def run(inputs, first_weight, *rest):
        sizes = inputs.shape[0] == 1 and inputs.shape[1] == 256 and first_weight.shape == (576, 3, 576)
        plan = owned_channels if owned and sizes else per_device
        return plan(inputs, first_weight, *rest)

    return run


def solution(mesh):
    placed = (
        P(None, "tm", "mp"),
        P("tm", None, "mp"),
        P(None, "mp"),
        P("tm", None, "mp"),
        P(None, "mp"),
        P(None, "tm", "mp"),
    )
    owned = mesh.shape["tm"] == 2 * NZ and mesh.shape["mp"] == 4
    return jax.shard_map(
        choose(owned),
        mesh=mesh,
        in_specs=placed,
        out_specs=(
            P(None, "tm", "mp"),
            P(None, "tm", "mp"),
            P("tm", None, "mp"),
            P(None, "mp"),
            P("tm", None, "mp"),
            P(None, "mp"),
        ),
        check_vma=False,
    )
```

```python
import jax
import jax.numpy as jnp
from jax import lax
from jax.experimental import pallas as pl
from jax.experimental.pallas import tpu as pltpu
from jax.sharding import PartitionSpec as P

BF = jnp.bfloat16
F32 = jnp.float32
LANES = 128
MIB = 2**20

NZ = 4


def mod(value):
    return lax.rem(value + 2 * NZ, NZ)


def flip(bit, by):
    return bit if by == 0 else 1 - bit


def moved(array, target):
    pairs = []
    for z in range(NZ):
        for x in range(2):
            for y in range(2):
                for c in range(2):
                    tz, tx, ty, tc = target(z, x, y, c)
                    pairs.append(((z * 2 + x) * 4 + y * 2 + c, (tz * 2 + tx) * 4 + ty * 2 + tc))
    return lax.ppermute(array, ("tm", "mp"), pairs)


def over_x(array):
    return moved(array, lambda z, x, y, c: (z, 1 - x, y, c))


def over_y(array):
    return moved(array, lambda z, x, y, c: (z, x, 1 - y, c))


def over_core(array):
    return moved(array, lambda z, x, y, c: (z, x, y, 1 - c))


def over_z(array, by):
    return moved(array, lambda z, x, y, c: ((z + by) % NZ, x, y, c))


def call(body, outs, args, scratch=(), vmem=28, flops=0, after=()):
    whole = pl.BlockSpec(memory_space=pltpu.VMEM)
    moved_bytes = sum(a.size * a.dtype.itemsize for a in args)
    for shape, kind in outs:
        size = jnp.dtype(kind).itemsize
        for extent in shape:
            size *= extent
        moved_bytes += size
    specs = [pl.BlockSpec(memory_space=pltpu.SMEM)] + [whole] * (len(args) - 1)
    specs += [pl.BlockSpec(memory_space=pl.ANY)] * len(after)
    count = len(args)

    def run(*refs):
        body(*refs[:count], *refs[count + len(after) :])

    return pl.pallas_call(
        run,
        out_shape=[jax.ShapeDtypeStruct(shape, kind) for shape, kind in outs],
        in_specs=specs,
        out_specs=[whole] * len(outs),
        scratch_shapes=list(scratch),
        compiler_params=pltpu.CompilerParams(vmem_limit_bytes=vmem * MIB),
        cost_estimate=pl.CostEstimate(flops=flops, bytes_accessed=moved_bytes, transcendentals=0),
    )(*args, *after)


EARLY = 10**11


def relay(array, after, flops=EARLY):
    anywhere = pl.BlockSpec(memory_space=pl.ANY)

    def body(*refs):
        pass

    return pl.pallas_call(
        body,
        out_shape=jax.ShapeDtypeStruct(array.shape, array.dtype),
        in_specs=[anywhere] * (1 + len(after)),
        out_specs=anywhere,
        input_output_aliases={0: 0},
        cost_estimate=pl.CostEstimate(flops=flops, bytes_accessed=0, transcendentals=0),
    )(array, *after)


def pack_weight(ids, weight, along=None, after=()):
    rows, gates, columns = weight.shape
    own = columns // 8
    extra = [] if along is None else [along]

    def body(ids, w, *rest):
        outs, turned = rest[len(extra) : len(extra) + 2], rest[-1]
        if extra:
            rest[-2][...] = rest[0][...]
        z, c = ids[0], ids[3]
        for g in range(gates):
            turned[g] = w[g].astype(F32).T
        for r in range(2):
            for pair in range(NZ // 2):
                both = []
                for dz in (2 * pair, 2 * pair + 1):
                    at = pl.ds(pl.multiple_of((mod(z + dz) * 2 + flip(c, r)) * own, 8), own)
                    both.append(jnp.concatenate([turned[g, at, :] for g in range(gates)], axis=0))
                outs[r][pair] = jnp.concatenate(both, axis=1).astype(BF)

    return call(
        body,
        [((NZ // 2, gates * own, 2 * rows), BF)] * 2 + [(a.shape, a.dtype) for a in extra],
        [ids, jnp.transpose(weight, (1, 0, 2)), *extra],
        [pltpu.VMEM((gates, columns, rows), F32)],
        after=after,
    )


def blocks_over_x(groups, back=False):
    def to(r):
        if back:
            return lambda z, x, y, c: (z, c, y, x ^ r)
        return lambda z, x, y, c: (z, c ^ r, y, x)

    return [moved(groups[r], to(r)) for r in range(2)]


def blocks_over_z(both, sign):
    return [both[0]] + [over_z(both[dz], sign * dz) for dz in range(1, NZ)]


def regroup(ids, pieces, groups, small=(), after=()):
    count = len(pieces)
    _, part, width = groups[0].shape
    rows = width // 2
    near_shape = (count,) + pieces[0].shape
    small_shape = (2,) + small[0].shape[1:] if small else None

    def body(ids, *rest):
        ins, (r0, r1) = rest[:count], rest[count : count + 2]
        tiny = rest[count + 2 : count + 2 + len(small)]
        outs = rest[count + 2 + len(small) :]
        for at in range(count):
            outs[0][at] = ins[at][...]
        for dz in range(NZ):
            lanes = slice((dz % 2) * rows, (dz % 2 + 1) * rows)
            parts = [group[dz // 2].astype(F32)[:, lanes] for group in (r0, r1)]
            outs[1 + dz][...] = jnp.concatenate(parts, axis=1).astype(BF)
        for at in range(NZ if small else 0):
            for k in range(2):
                outs[1 + NZ + at][k] = tiny[k][at]

    made = call(
        body,
        [(near_shape, BF)] + [((part, width), BF)] * NZ + ([(small_shape, BF)] * NZ if small else []),
        [ids, *pieces, *groups, *small],
        after=after,
    )
    return made[0], made[1 : 1 + NZ], made[1 + NZ :]


def regroup_back(ids, both, after=()):
    part, width = both[0].shape
    rows = width // 2

    def body(ids, *rest):
        ins, outs = rest[:NZ], rest[NZ:]
        for r in range(2):
            lanes = slice(r * rows, (r + 1) * rows)
            for pair in range(NZ // 2):
                parts = [ins[2 * pair + k][...].astype(F32)[:, lanes] for k in range(2)]
                outs[r][pair] = jnp.concatenate(parts, axis=1).astype(BF)

    return call(body, [((NZ // 2, part, width), BF)] * 2, [ids, *both], after=after, flops=EARLY)


def join_weight(ids, blocks):
    part, width = blocks[0].shape
    rows = width // 2

    def body(ids, *rest):
        ins, (wide, tall), joined = rest[:NZ], rest[NZ : NZ + 2], rest[NZ + 2]
        z, x = ids[0], ids[1]
        for dz in range(NZ):
            source = mod(z - dz)
            both = ins[dz][...].astype(F32)
            for r in range(2):
                base = (flip(x, r) * 2 + source // 2) * part
                at = pl.ds(pl.multiple_of(base, 8), part)
                joined[lax.rem(source, 2), at, :] = both[:, r * rows : (r + 1) * rows]
        for half in range(2):
            at = pl.ds(half * 2 * part, 2 * part)
            both = jnp.concatenate([joined[0, at, :], joined[1, at, :]], axis=1)
            wide[at, :] = both.astype(BF)
        for y in range(2):
            tall[pl.ds(y * rows, rows), :] = joined[y].T.astype(BF)

    return call(
        body,
        [((4 * part, 2 * rows), BF), ((2 * rows, 4 * part), BF)],
        [ids, *blocks],
        [pltpu.VMEM((2, 4 * part, rows), F32)],
        flops=EARLY,
    )


def halves(array, axis):
    half = array.shape[axis] // 2
    return lax.slice_in_dim(array, 0, half, axis=axis), lax.slice_in_dim(array, half, 2 * half, axis=axis)


def along_z(piece):
    return [piece] + [over_z(piece, dz) for dz in range(1, NZ)]


def gather_plane(near, axis):
    from_x, from_y = over_x(near), over_y(near)
    return [near, from_x, from_y, over_y(halves(from_x, axis + 1)[0]), over_x(halves(from_y, axis + 1)[1])]


def add_diagonal(ids, parts, axis, after=()):
    _, to_x, to_y, diag_a, diag_b = parts
    half = diag_a.shape[axis + 1]
    first = (slice(None),) * (axis + 1) + (pl.ds(0, half),)
    second = (slice(None),) * (axis + 1) + (pl.ds(half, half),)

    def body(ids, to_x, to_y, at_x, at_y, out_x, out_y):
        out_x[first] = (to_x[first] + at_x[...].astype(F32)).astype(BF)
        out_x[second] = to_x[second].astype(BF)
        out_y[first] = to_y[first].astype(BF)
        out_y[second] = (to_y[second] + at_y[...].astype(F32)).astype(BF)

    args = [ids, to_x, to_y, over_y(diag_a), over_x(diag_b)]
    return call(body, [(to_x.shape, BF)] * 2, args, after=after)


def add_plane(ids, own, from_x, from_y, after=()):
    def body(ids, own, from_x, from_y, *outs):
        for step in range(NZ):
            plane = own[step] + from_x[step].astype(F32) + from_y[step].astype(F32)
            outs[step][...] = plane.astype(outs[step].dtype)

    outs = [(own.shape[1:], BF)] * (NZ - 1) + [(own.shape[1:], F32)]
    return call(body, outs, [ids, own, from_x, from_y], after=after)


def sum_planes(planes):
    total = planes[NZ - 1]
    for step in range(NZ - 1):
        total = total + over_z(planes[step], step + 1).astype(F32)
    return total


def partial_gates(ids, wide, found, channel_pieces, after=()):
    total, depth = wide.shape
    part = total // 4
    rows = depth // 2
    if channel_pieces:
        own, length = found[0].shape[1:]
    else:
        length = found[0].shape[2] * 8
    span = 512

    def body(ids, w, *rest):
        ins, (u, mine, theirs), (prev, cur) = rest[:5], rest[5:8], rest[8:]
        z, x, y, c = ids[0], ids[1], ids[2], ids[3]
        for dz in range(NZ):
            near, at_x, at_y, diag_a, diag_b = [part.at[dz] for part in ins]
            source = mod(z - dz)
            if channel_pieces:
                half = length // 2
                for other in range(2):
                    row = pl.multiple_of(flip(y, other) * rows + source * 2 * own, 16)
                    for k in range(2):
                        cols = pl.ds(k * half, half)
                        if other:
                            a, b = at_y[:, cols], (diag_a, diag_b)[k][...]
                        else:
                            a, b = near[:, cols], at_x[:, cols]
                        a, b = a.astype(F32), b.astype(F32)
                        pair = jnp.concatenate([jnp.where(x == 0, a, b), jnp.where(x == 0, b, a)], axis=0)
                        u[pl.ds(row, 2 * own), cols] = pair.astype(BF)
            else:
                block = length // 8
                here = pl.ds(pl.multiple_of((source * 2 + x) * block, block), block)
                there = pl.ds(pl.multiple_of((source * 2 + 1 - x) * block, block), block)
                top = pl.multiple_of(y * rows, 16)
                low = pl.multiple_of((1 - y) * rows, 16)
                u[pl.ds(top, rows), here] = near[...]
                u[pl.ds(top, rows), there] = at_x[...]
                u[pl.ds(low, rows), here] = at_y[...]
                u[pl.ds(low, rows // 2), there] = diag_a[...]
                u[pl.ds(pl.multiple_of(low + rows // 2, 16), rows // 2), there] = diag_b[...]
        for start in range(0, length, span):
            cols = pl.ds(start, span)
            made = jnp.dot(w[...], u[:, cols], preferred_element_type=F32)
            for core in range(2):
                prev[core, :, cols] = made[2 * core * part : (2 * core + 1) * part]
                cur[core, :, cols] = made[(2 * core + 1) * part : (2 * core + 2) * part]
        first = lax.broadcasted_iota(jnp.int32, (part, length), 1) == 0
        for out, core in ((mine, c), (theirs, 1 - c)):
            out[...] = cur[core] + jnp.where(first, 0.0, pltpu.roll(prev[core], 1, 1))

    return call(
        body,
        [((depth, length), BF), ((part, length), F32), ((part, length), F32)],
        [ids, wide, *found],
        [pltpu.VMEM((2, part, length), F32), pltpu.VMEM((2, part, length), F32)],
        after=after,
        flops=2 * total * depth * length,
    )


def scan_lanes(forget, driven, backward):
    own, length = driven.shape
    lane = lax.broadcasted_iota(jnp.int32, (own, LANES), 1)
    count = length // LANES
    order = list(range(count))[:: -1 if backward else 1]
    blocks = [None] * count
    carry = jnp.zeros((own, 1), F32)
    together = 4
    for start in range(0, count, together):
        group = order[start : start + together]
        reach = [forget[:, block * LANES : (block + 1) * LANES] for block in group]
        state = [driven[:, block * LANES : (block + 1) * LANES] for block in group]
        by = 1
        while by < LANES:
            shift = LANES - by if backward else by
            inside = lane < LANES - by if backward else lane >= by
            for at in range(len(group)):
                r, s = reach[at], state[at]
                state[at] = s + jnp.where(inside, r * pltpu.roll(s, shift, 1), 0.0)
                reach[at] = jnp.where(inside, r * pltpu.roll(r, shift, 1), r)
            by *= 2
        for at, block in enumerate(group):
            blocks[block] = state[at] + reach[at] * carry
            carry = blocks[block][:, :1] if backward else blocks[block][:, LANES - 1 :]
    return blocks


def squash(value):
    return 1.0 / (1.0 + jnp.exp(-value))


def activate(mine, theirs, bias, own):
    gates = [
        mine[pl.ds(g * own, own), :] + theirs[pl.ds(g * own, own), :] + bias[pl.ds(g * own, own), :]
        for g in range(3)
    ]
    return jnp.tanh(gates[0]), squash(gates[1]), squash(gates[2])


def put_blocks(ref, blocks):
    for at, block in enumerate(blocks):
        ref[:, pl.ds(at * LANES, LANES)] = block


def gate_gradients(grad, candidate, forget, outgate, cells, adjoint, wide, gate_grad):
    own, length = grad.shape
    driven = grad[...] * outgate[...]
    last = lax.broadcasted_iota(jnp.int32, (own, length), 1) == length - 1
    later = jnp.where(last, 0.0, pltpu.roll(forget[...], length - 1, 1))
    put_blocks(adjoint, scan_lanes(later, driven, True))
    f, a = forget[...], candidate[...]
    away = 1.0 - f
    before = jnp.where(
        lax.broadcasted_iota(jnp.int32, (own, length), 1) == 0, 0.0, pltpu.roll(cells[...], 1, 1)
    )
    wide[pl.ds(0, own), :] = adjoint[...] * away * (1.0 - a * a)
    wide[pl.ds(own, own), :] = adjoint[...] * (before - a) * f * away
    o = outgate[...]
    wide[pl.ds(2 * own, own), :] = grad[...] * cells[...] * o * (1.0 - o)
    gate_grad[...] = wide[...].astype(BF)


def first_cells(ids, mine, theirs, bias, after=()):
    part, length = mine.shape
    own = part // 3

    def body(ids, mine, theirs, bias, hidden, cand, forg, outg, cells):
        candidate, forget, outgate = activate(mine, theirs, bias, own)
        cand[...], forg[...], outg[...] = candidate, forget, outgate
        put_blocks(cells, scan_lanes(forget, (1.0 - forget) * candidate, False))
        hidden[...] = (outgate * cells[...]).astype(BF)

    return call(
        body,
        [((own, length), BF)] + [((own, length), F32)] * 4,
        [ids, mine, theirs, bias],
        after=after,
    )


def first_gate_grad(ids, grad, saved, after=()):
    own, length = grad.shape

    def body(ids, grad, cand, forg, outg, cells, gate_grad, adjoint, wide):
        gate_gradients(grad, cand, forg, outg, cells, adjoint, wide, gate_grad)

    return call(
        body,
        [((3 * own, length), BF)],
        [ids, grad, *saved],
        [pltpu.VMEM((own, length), F32), pltpu.VMEM((3 * own, length), F32)],
        after=after,
    )[0]


def second_cells(ids, mine, theirs, bias, cot_pieces):
    part, length = mine.shape
    own = part // 3
    block = length // 8

    def body(ids, mine, theirs, bias, *rest):
        cots, outs, gate_grad = rest[:NZ], rest[NZ : NZ + 2], rest[NZ + 2]
        grad, cand, forg, outg, cells, adjoint, wide = rest[NZ + 3 :]
        z, x = ids[0], ids[1]
        for dz in range(NZ):
            for dx in range(2):
                i = mod(z - dz) * 2 + flip(x, dx)
                grad[:, pl.ds(pl.multiple_of(i * block, block), block)] = cots[dz][dx].astype(F32)
        candidate, forget, outgate = activate(mine, theirs, bias, own)
        cand[...], forg[...], outg[...] = candidate, forget, outgate
        put_blocks(cells, scan_lanes(forget, (1.0 - forget) * candidate, False))
        adjoint[...] = outgate * cells[...]
        for dz in range(NZ):
            for dx in range(2):
                i = mod(z + dz) * 2 + flip(x, dx)
                piece = adjoint[:, pl.ds(pl.multiple_of(i * block, block), block)]
                outs[dx][dz] = piece.astype(BF)
        gate_gradients(grad, cand, forg, outg, cells, adjoint, wide, gate_grad)

    made = call(
        body,
        [((NZ, own, block), BF)] * 2 + [((part, length), BF)],
        [ids, mine, theirs, bias, *cot_pieces],
        [pltpu.VMEM((own, length), F32)] * 6 + [pltpu.VMEM((part, length), F32)],
    )
    return made[:2], made[2]


def split_cotangent(ids, cotangent):
    channels, block = cotangent.shape
    own = channels // 8

    def body(ids, cot, *rest):
        outs, wide = rest[:2], rest[2]
        wide[...] = cot[...].astype(F32)
        for dz in range(NZ):
            for dx in range(2):
                i = mod(ids[0] + dz) * 2 + flip(ids[1], dx)
                outs[dx][dz] = wide[pl.ds(pl.multiple_of(i * own, 8), own), :].astype(BF)

    return call(body, [((NZ, own, block), BF)] * 2, [ids, cotangent], [pltpu.VMEM((channels, block), F32)])


def pair_up(ids, first, second, after=()):
    shape = (2,) + first.shape[1:]

    def body(ids, first, second, *outs):
        for at in range(NZ):
            outs[at][0] = first[at]
            outs[at][1] = second[at]

    return call(body, [(shape, BF)] * NZ, [ids, first, second], after=after)


def join_outputs(ids, pieces):
    _, own, block = pieces[0].shape

    def body(ids, *rest):
        ins, out, wide = rest[:NZ], rest[NZ], rest[NZ + 1]
        for dz in range(NZ):
            for dx in range(2):
                i = mod(ids[0] - dz) * 2 + flip(ids[1], dx)
                wide[pl.ds(pl.multiple_of(i * own, 8), own), :] = ins[dz][dx].astype(F32)
        out[...] = wide[...].astype(BF)

    return call(body, [((8 * own, block), BF)], [ids, *pieces], [pltpu.VMEM((8 * own, block), F32)])[0]


def input_parts(ids, tall, grads, channel_pieces, after=()):
    depth, total = tall.shape
    length = grads.shape[1]
    rows = depth // 2
    own = rows // 8
    block = length // 8
    span = 512
    shape = (NZ, own, length) if channel_pieces else (NZ, rows, block)
    half = (NZ, own, length // 2) if channel_pieces else (NZ, rows // 2, block)

    def body(ids, w, grads, *rest):
        outs, v = rest[:5], rest[5]
        z, x, y = ids[0], ids[1], ids[2]
        for start in range(0, length, span):
            cols = pl.ds(start, span)
            v[:, cols] = jnp.dot(w[...], grads[:, cols], preferred_element_type=F32)
        for step in range(NZ):
            target = mod(z + 1 + step)

            def piece(dx, dy, k=None):
                i = target * 2 + flip(x, dx)
                if channel_pieces:
                    row = pl.multiple_of(flip(y, dy) * rows + i * own, 8)
                    cols = slice(None) if k is None else pl.ds(k * length // 2, length // 2)
                    return v[pl.ds(row, own), cols]
                cols = pl.ds(pl.multiple_of(i * block, block), block)
                row = flip(y, dy) * rows
                if k is None:
                    return v[pl.ds(pl.multiple_of(row, 8), rows), cols]
                return v[pl.ds(pl.multiple_of(row + k * rows // 2, 8), rows // 2), cols]

            outs[0][step] = piece(0, 0)
            outs[1][step] = piece(1, 0)
            outs[2][step] = piece(0, 1)
            outs[3][step] = piece(1, 1, 0).astype(BF)
            outs[4][step] = piece(1, 1, 1).astype(BF)

    return call(
        body,
        [(shape, F32), (shape, F32), (shape, F32), (half, BF), (half, BF)],
        [ids, tall, grads],
        [pltpu.VMEM((depth, length), F32)],
        after=after,
        flops=2 * depth * total * length,
    )


def weight_blocks(ids, mine, theirs, u, after=()):
    part, length = mine.shape
    depth = u.shape[0]
    total, rows = 4 * part, depth // 2

    def body(ids, mine, theirs, u, grads, *rest):
        outs, made = rest[:NZ], rest[NZ]
        z, x, c = ids[0], ids[1], ids[3]
        last = lax.broadcasted_iota(jnp.int32, (part, length), 1) == length - 1
        for core in range(2):
            now = jnp.where(c == core, mine[...].astype(F32), theirs[...].astype(F32))
            after = jnp.where(last, 0.0, pltpu.roll(now, length - 1, 1))
            grads[pl.ds(core * 2 * part, 2 * part), :] = jnp.concatenate([after, now], axis=0).astype(BF)
        contract = (((1,), (1,)), ((), ()))
        for y in range(2):
            made[y] = lax.dot_general(
                grads[...], u[pl.ds(y * rows, rows), :], contract, preferred_element_type=F32
            )
        sums = lax.dot_general(jnp.ones((8, length), BF), grads[...], contract, preferred_element_type=F32)
        line = lax.broadcasted_iota(jnp.int32, (8, part), 0)
        tails = []
        for r in range(2):
            bias = jnp.where(flip(x, r) == 0, sums[:, part : 2 * part], sums[:, 3 * part : 4 * part])
            high = bias.astype(BF).astype(F32)
            tail = jnp.where(line == 0, high, jnp.where(line == 1, bias - high, 0.0))
            tails.append(jnp.concatenate([tail, jnp.zeros((8, rows - part), F32)], axis=1))
        for dz in range(NZ):
            source = mod(z - dz)
            both = []
            for r in range(2):
                at = pl.ds(pl.multiple_of((flip(x, r) * 2 + source // 2) * part, 8), part)
                both.append(jnp.concatenate([made[lax.rem(source, 2), at, :], tails[r]], axis=0))
            outs[dz][...] = jnp.concatenate(both, axis=1).astype(BF)

    made = call(
        body,
        [((total, length), BF)] + [((part + 8, 2 * rows), BF)] * NZ,
        [ids, mine, theirs, u],
        [pltpu.VMEM((2, total, rows), F32)],
        after=after,
        flops=2 * depth * total * length,
    )
    return made[0], made[1:]


def unpack_weight(ids, groups):
    _, height, width = groups[0].shape
    part, rows = height - 8, width // 2
    own = part // 3
    columns = own * 8

    def body(ids, r0, r1, out, bias, joined):
        z, c = ids[0], ids[3]
        for r, group in enumerate((r0, r1)):
            for pair in range(NZ // 2):
                both = group[pair].astype(F32)
                for k in range(2):
                    i = mod(z + 2 * pair + k) * 2 + flip(c, r)
                    block = both[:, k * rows : (k + 1) * rows]
                    for g in range(3):
                        at = pl.ds(pl.multiple_of(i * own, 8), own)
                        joined[g, at, :] = block[g * own : (g + 1) * own]
                    bias[pl.ds(i, 1), :] = (block[part : part + 1] + block[part + 1 : part + 2])[:, :part]
        for g in range(3):
            out[g] = joined[g].T

    grad, bias = call(
        body,
        [((3, rows, columns), F32), ((8, part), F32)],
        [ids, *groups],
        [pltpu.VMEM((3, columns, rows), F32)],
    )
    bias = jnp.transpose(bias.reshape(8, 3, own), (1, 0, 2)).reshape(3, columns)
    return grad, bias


def owned_bias(bias, own):
    i = lax.axis_index("tm")
    return lax.dynamic_slice_in_dim(bias, i * own, own, axis=1).reshape(3 * own, 1)


def owned_channels(inputs, first_weight, first_bias, second_weight, second_bias, cotangent):
    tm, mp = lax.axis_index("tm"), lax.axis_index("mp")
    ids = jnp.stack([tm // 2, tm % 2, mp // 2, mp % 2]).astype(jnp.int32)
    own = first_weight.shape[2] // 8

    *w1, u_piece = pack_weight(ids, first_weight, inputs[0].T)
    near, w1, _ = regroup(ids, along_z(u_piece), blocks_over_x(w1))
    u_found = gather_plane(near, 0)
    wide_1, tall_1 = join_weight(ids, blocks_over_z(w1, 1))
    w2 = pack_weight(ids, second_weight, after=u_found[3:])

    u, mine, theirs = partial_gates(ids, wide_1, u_found, False, after=w2)
    w2 = blocks_over_x(w2)
    hidden, *saved = first_cells(relay(ids, w2), mine, over_core(theirs), owned_bias(first_bias, own))
    cot_here, cot_there = split_cotangent(ids, cotangent[0].T)
    cots = pair_up(ids, cot_here, over_x(cot_there))
    near, w2, _ = regroup(ids, along_z(hidden), w2, after=cots)
    h_found = gather_plane(near, 1)
    wide_2, tall_2 = join_weight(ids, blocks_over_z(w2, 1))
    cots = [cots[0]] + [over_z(cots[dz], dz) for dz in range(1, NZ)]
    h, mine, theirs = partial_gates(ids, wide_2, h_found, True, after=cots)
    outs, gate_grad = second_cells(ids, mine, over_core(theirs), owned_bias(second_bias, own), cots)

    grads, dw2 = weight_blocks(ids, gate_grad, over_core(gate_grad), h)
    outs = pair_up(ids, outs[0], over_x(outs[1]))
    parts = input_parts(ids, tall_2, grads, True, after=outs)
    dw2 = blocks_over_z(dw2, -1)
    sent_x, sent_y = add_diagonal(ids, parts, 1)
    dw2 = regroup_back(ids, dw2)
    planes = add_plane(ids, parts[0], over_x(sent_x), over_y(sent_y), after=dw2)
    hidden_grad = sum_planes(planes)
    dw2 = blocks_over_x(dw2, True)
    gate_grad = first_gate_grad(ids, hidden_grad, saved, after=dw2)

    grads, dw1 = weight_blocks(ids, gate_grad, over_core(gate_grad), u)
    outs = [outs[0]] + [over_z(outs[dz], dz) for dz in range(1, NZ)]
    parts = input_parts(ids, tall_1, grads, False, after=outs)
    dw1 = blocks_over_z(dw1, -1)
    second_grad, second_bias_grad = unpack_weight(ids, dw2)
    outputs = join_outputs(ids, outs)
    sent_x, sent_y = add_diagonal(ids, parts, 0, after=[second_grad, outputs])
    dw1 = regroup_back(ids, dw1)
    planes = add_plane(ids, parts[0], over_x(sent_x), over_y(sent_y), after=dw1)
    input_grad = sum_planes(planes)
    first_grad, first_bias_grad = unpack_weight(ids, blocks_over_x(dw1, True))
    first_grad, second_grad = (jnp.transpose(grad, (1, 0, 2)) for grad in (first_grad, second_grad))
    return (
        outputs.T[None],
        input_grad.T[None],
        first_grad,
        first_bias_grad,
        second_grad,
        second_bias_grad,
    )


def prefix(value, axis, join, neutral, backward):
    count, mine = (lax.axis_size(axis), lax.axis_index(axis))
    pieces = jax.tree.map(lambda part: lax.all_gather(part, axis), value)
    if backward:
        pieces = jax.tree.map(lambda part: part[::-1], pieces)
        mine = count - 1 - mine
    total = jax.tree.map(
        lambda part, zero: jnp.full_like(part, 0) + jnp.asarray(zero, part.dtype), value, neutral
    )

    def hop(position, total):
        longer = join(total, jax.tree.map(lambda part: part[position], pieces))
        return jax.tree.map(lambda new, old: jnp.where(position < mine, new, old), longer, total)

    return lax.fori_loop(0, count - 1, hop, total)


def passed_along(array, axis, by):
    size = lax.axis_size(axis)
    pairs = [(i, i + by) for i in range(size) if 0 <= i + by < size]
    return lax.ppermute(array, axis, pairs)


def affine_join(earlier, later):
    return (earlier[0] * later[0], later[0] * earlier[1] + later[1])


def weight_view(gathered):
    return gathered.reshape(2, gathered.shape[0] // 2, gathered.shape[1] * gathered.shape[2])


def span_prefix(product, offset):
    identity = (jnp.ones_like(product), jnp.zeros_like(offset))
    result = prefix((product, offset), "tm", affine_join, identity, False)
    return result[1]


def span_suffix(product, offset):
    identity = (jnp.ones_like(product), jnp.zeros_like(offset))
    result = prefix((product, offset), "tm", affine_join, identity, True)
    return result[1]


def forward_layer(layer_in, view, bias):
    seq_count, length, channels = layer_in.shape
    prev_row = passed_along(layer_in[:, length - 1 :], "tm", 1)
    previous = jnp.concatenate([prev_row, layer_in[:, : length - 1]], axis=1)
    stacked = jnp.stack([previous, layer_in])
    summed = jnp.einsum(
        "jsck,jkn->scn",
        lax.all_gather(stacked, "mp", axis=3, tiled=True),
        view,
        preferred_element_type=jnp.float32,
    )
    gates = summed.reshape(seq_count, length, 3, channels) + bias
    candidate = jnp.tanh(gates[:, :, 0])
    forget = jax.nn.sigmoid(gates[:, :, 1])
    outgate = jax.nn.sigmoid(gates[:, :, 2])
    product, offset = lax.associative_scan(
        affine_join, (forget, (1.0 - forget) * candidate), axis=1
    )
    carry_in = span_prefix(product[:, length - 1], offset[:, length - 1])
    cells = offset + product * carry_in[:, None]
    cells_prev = jnp.concatenate([carry_in[:, None], cells[:, : length - 1]], axis=1)
    return (outgate * cells, (stacked, candidate, forget, outgate, cells, cells_prev))


def backward_layer(grad_in, saved, view):
    stacked, candidate, forget, outgate, cells, cells_prev = saved
    seq_count, length, channels = grad_in.shape
    driven = grad_in * outgate
    next_forget = jnp.concatenate([forget[:, 1:], jnp.ones_like(forget[:, :1])], axis=1)
    reach, local_adj = lax.associative_scan(
        affine_join, (next_forget[:, ::-1], driven[:, ::-1]), axis=1
    )
    reach = reach[:, ::-1]
    local_adj = local_adj[:, ::-1]
    first_forget = forget[:, 0]
    incoming = span_suffix(first_forget * reach[:, 0], first_forget * local_adj[:, 0])
    adjoint = local_adj + reach * incoming[:, None]
    grad_cand = adjoint * (1.0 - forget) * (1.0 - candidate * candidate)
    grad_forget = adjoint * (cells_prev - candidate) * forget * (1.0 - forget)
    grad_outgate = grad_in * cells * outgate * (1.0 - outgate)
    gate_grad = jnp.stack([grad_cand, grad_forget, grad_outgate], axis=2).astype(jnp.bfloat16)
    flat_grad = gate_grad.reshape(seq_count, length, 3 * channels)
    bias_part = jnp.sum(gate_grad, axis=(0, 1), dtype=jnp.float32)
    back_both = jnp.einsum("scn,jkn->jsck", flat_grad, view, preferred_element_type=jnp.float32)
    from_prev = back_both[0]
    from_current = back_both[1]
    local_grad = from_current + jnp.concatenate(
        [from_prev[:, 1:], jnp.zeros_like(from_prev[:, :1])], axis=1
    )
    tail_rows = from_prev[:, :1]
    shard_grad, tail_shard = (
        lax.psum_scatter(local_grad, "mp", scatter_dimension=2, tiled=True),
        lax.psum_scatter(tail_rows, "mp", scatter_dimension=2, tiled=True),
    )
    tail_next = passed_along(tail_shard, "tm", -1)
    layer_grad = shard_grad + jnp.concatenate(
        [jnp.zeros_like(shard_grad[:, : length - 1]), tail_next], axis=1
    )
    weight_full = jnp.einsum(
        "jsck,scn->jkn",
        lax.all_gather(stacked, "mp", axis=3, tiled=True),
        flat_grad,
        preferred_element_type=jnp.float32,
    )
    weight_full = weight_full.reshape(2 * weight_full.shape[1], 3, channels)
    weight_shard = lax.psum_scatter(weight_full, "tm", scatter_dimension=0, tiled=True)
    bias_grad = lax.psum(bias_part, "tm")
    return (layer_grad, weight_shard, bias_grad)


def per_device(inputs, first_weight, first_bias, second_weight, second_bias, cotangent):
    full_first, full_second = (
        lax.all_gather(first_weight, "tm", axis=0, tiled=True),
        lax.all_gather(second_weight, "tm", axis=0, tiled=True),
    )
    view_first = weight_view(full_first)
    view_second = weight_view(full_second)
    hidden_out, saved_first = forward_layer(inputs, view_first, first_bias)
    hidden = hidden_out.astype(jnp.bfloat16)
    top_out, saved_second = forward_layer(hidden, view_second, second_bias)
    again_first, again_second = (
        lax.all_gather(first_weight, "tm", axis=0, tiled=True),
        lax.all_gather(second_weight, "tm", axis=0, tiled=True),
    )
    back_first = weight_view(again_first)
    back_second = weight_view(again_second)
    hidden_grad, second_weightgrad, second_biasgrad = backward_layer(
        cotangent.astype(jnp.float32), saved_second, back_second
    )
    input_grad, first_weightgrad, first_biasgrad = backward_layer(
        hidden_grad, saved_first, back_first
    )
    return (
        top_out.astype(jnp.bfloat16),
        input_grad,
        first_weightgrad,
        first_biasgrad,
        second_weightgrad,
        second_biasgrad,
    )


def choose(owned):
    def run(inputs, first_weight, *rest):
        sizes = inputs.shape[0] == 1 and inputs.shape[1] == 256 and first_weight.shape == (576, 3, 576)
        plan = owned_channels if owned and sizes else per_device
        return plan(inputs, first_weight, *rest)

    return run


def solution(mesh):
    placed = (
        P(None, "tm", "mp"),
        P("tm", None, "mp"),
        P(None, "mp"),
        P("tm", None, "mp"),
        P(None, "mp"),
        P(None, "tm", "mp"),
    )
    owned = mesh.shape["tm"] == 2 * NZ and mesh.shape["mp"] == 4
    return jax.shard_map(
        choose(owned),
        mesh=mesh,
        in_specs=placed,
        out_specs=(
            P(None, "tm", "mp"),
            P(None, "tm", "mp"),
            P("tm", None, "mp"),
            P(None, "mp"),
            P("tm", None, "mp"),
            P(None, "mp"),
        ),
        check_vma=False,
    )
```

```python
import jax
import jax.numpy as jnp
from jax import lax
from jax.experimental import pallas as pl
from jax.experimental.pallas import tpu as pltpu
from jax.sharding import PartitionSpec as P

BF = jnp.bfloat16
F32 = jnp.float32
LANES = 128
SPAN = 512
MIB = 2**20

NZ = 4


def mod(value):
    return lax.rem(value + 2 * NZ, NZ)


def flip(bit, by):
    return bit if by == 0 else 1 - bit


def moved(array, target):
    pairs = []
    for z in range(NZ):
        for x in range(2):
            for y in range(2):
                for c in range(2):
                    tz, tx, ty, tc = target(z, x, y, c)
                    pairs.append(((z * 2 + x) * 4 + y * 2 + c, (tz * 2 + tx) * 4 + ty * 2 + tc))
    return lax.ppermute(array, ("tm", "mp"), pairs)


def over_x(array):
    return moved(array, lambda z, x, y, c: (z, 1 - x, y, c))


def over_y(array):
    return moved(array, lambda z, x, y, c: (z, x, 1 - y, c))


def over_core(array):
    return moved(array, lambda z, x, y, c: (z, x, y, 1 - c))


def over_z(array, by):
    return moved(array, lambda z, x, y, c: ((z + by) % NZ, x, y, c))


def call(body, outs, args, scratch=(), vmem=28, flops=0, after=()):
    whole = pl.BlockSpec(memory_space=pltpu.VMEM)
    moved_bytes = sum(a.size * a.dtype.itemsize for a in args)
    for shape, kind in outs:
        size = jnp.dtype(kind).itemsize
        for extent in shape:
            size *= extent
        moved_bytes += size
    specs = [pl.BlockSpec(memory_space=pltpu.SMEM)] + [whole] * (len(args) - 1)
    specs += [pl.BlockSpec(memory_space=pl.ANY)] * len(after)
    count = len(args)

    def run(*refs):
        body(*refs[:count], *refs[count + len(after) :])

    return pl.pallas_call(
        run,
        out_shape=[jax.ShapeDtypeStruct(shape, kind) for shape, kind in outs],
        in_specs=specs,
        out_specs=[whole] * len(outs),
        scratch_shapes=list(scratch),
        compiler_params=pltpu.CompilerParams(vmem_limit_bytes=vmem * MIB),
        cost_estimate=pl.CostEstimate(flops=flops, bytes_accessed=moved_bytes, transcendentals=0),
    )(*args, *after)


EARLY = 10**11
SOON = 10**10


def relay(arrays, after, flops=0):
    anywhere = pl.BlockSpec(memory_space=pl.ANY)
    count = len(arrays)

    def body(*refs):
        pass

    return pl.pallas_call(
        body,
        out_shape=[jax.ShapeDtypeStruct(array.shape, array.dtype) for array in arrays],
        in_specs=[anywhere] * (count + len(after)),
        out_specs=[anywhere] * count,
        input_output_aliases={at: at for at in range(count)},
        cost_estimate=pl.CostEstimate(flops=flops, bytes_accessed=0, transcendentals=0),
    )(*arrays, *after)


def pack_weight(ids, weight, along=None, after=()):
    rows, gates, columns = weight.shape
    own = columns // 8
    extra = [] if along is None else [along]

    def body(ids, w, *rest):
        outs, turned = rest[len(extra) : len(extra) + 2], rest[-1]
        if extra:
            rest[-2][...] = rest[0][...]
        z, c = ids[0], ids[3]
        for g in range(gates):
            turned[g] = w[g].astype(F32).T
        for r in range(2):
            for pair in range(NZ // 2):
                both = []
                for dz in (2 * pair, 2 * pair + 1):
                    at = pl.ds(pl.multiple_of((mod(z + dz) * 2 + flip(c, r)) * own, 8), own)
                    both.append(jnp.concatenate([turned[g, at, :] for g in range(gates)], axis=0))
                outs[r][pair] = jnp.concatenate(both, axis=1).astype(BF)

    return call(
        body,
        [((NZ // 2, gates * own, 2 * rows), BF)] * 2 + [(a.shape, a.dtype) for a in extra],
        [ids, jnp.transpose(weight, (1, 0, 2)), *extra],
        [pltpu.VMEM((gates, columns, rows), F32)],
        after=after,
    )


def blocks_over_x(groups, back=False):
    def to(r):
        if back:
            return lambda z, x, y, c: (z, c, y, x ^ r)
        return lambda z, x, y, c: (z, c ^ r, y, x)

    return [moved(groups[r], to(r)) for r in range(2)]


def blocks_over_z(both, sign):
    return [both[0]] + [over_z(both[dz], sign * dz) for dz in range(1, NZ)]


def regroup(ids, pieces, groups, after=()):
    count, wide = len(pieces), len(groups) > 0
    outs = [((count,) + pieces[0].shape, BF)] if count else []
    if wide:
        _, part, width = groups[0].shape
        rows = width // 2
        outs += [((part, width), BF)] * NZ

    def body(ids, *rest):
        ins, given = rest[:count], rest[count : count + len(groups)]
        made = rest[count + len(groups) :]
        for at in range(count):
            made[0][at] = ins[at][...]
        for dz in range(NZ if wide else 0):
            lanes = slice((dz % 2) * rows, (dz % 2 + 1) * rows)
            parts = [group[dz // 2].astype(F32)[:, lanes] for group in given]
            made[-NZ + dz][...] = jnp.concatenate(parts, axis=1).astype(BF)

    made = list(call(body, outs, [ids, *pieces, *groups], after=after))
    return (made[:1] if count else []) + [made[-NZ:]] * wide


def regroup_back(ids, both, after=()):
    part, width = both[0].shape
    rows = width // 2

    def body(ids, *rest):
        ins, outs = rest[:NZ], rest[NZ:]
        for r in range(2):
            lanes = slice(r * rows, (r + 1) * rows)
            for pair in range(NZ // 2):
                parts = [ins[2 * pair + k][...].astype(F32)[:, lanes] for k in range(2)]
                outs[r][pair] = jnp.concatenate(parts, axis=1).astype(BF)

    return call(body, [((NZ // 2, part, width), BF)] * 2, [ids, *both], after=after, flops=EARLY)


def join_weight(ids, blocks):
    part, width = blocks[0].shape
    rows = width // 2

    def body(ids, *rest):
        ins, (wide, tall), joined = rest[:NZ], rest[NZ : NZ + 2], rest[NZ + 2]
        z, x = ids[0], ids[1]
        for dz in range(NZ):
            source = mod(z - dz)
            both = ins[dz][...].astype(F32)
            for r in range(2):
                base = (flip(x, r) * 2 + source // 2) * part
                at = pl.ds(pl.multiple_of(base, 8), part)
                joined[lax.rem(source, 2), at, :] = both[:, r * rows : (r + 1) * rows]
        for half in range(2):
            at = pl.ds(half * 2 * part, 2 * part)
            both = jnp.concatenate([joined[0, at, :], joined[1, at, :]], axis=1)
            wide[at, :] = both.astype(BF)
        for y in range(2):
            tall[pl.ds(y * rows, rows), :] = joined[y].T.astype(BF)

    return call(
        body,
        [((4 * part, 2 * rows), BF), ((2 * rows, 4 * part), BF)],
        [ids, *blocks],
        [pltpu.VMEM((2, 4 * part, rows), F32)],
        flops=EARLY,
    )


def halves(array, axis):
    half = array.shape[axis] // 2
    return lax.slice_in_dim(array, 0, half, axis=axis), lax.slice_in_dim(array, half, 2 * half, axis=axis)


def along_z(piece):
    return [piece] + [over_z(piece, dz) for dz in range(1, NZ)]


def stacked(arrays, rank):
    found = []
    for at, array in enumerate(arrays):
        found += [(at, None)] if len(array.shape) == rank else [(at, k) for k in range(array.shape[0])]
    return found


def corner(ids, from_x, from_y, axis, after=()):
    lists = [stacked(part, 2) for part in (from_x, from_y)]
    piece = from_x[0].shape[-2:]
    half = tuple(extent // 2 if at == axis else extent for at, extent in enumerate(piece))

    def body(ids, *rest):
        ins = rest[: len(from_x)], rest[len(from_x) : -2]
        for k in range(2):
            cut = (slice(None),) * axis + (pl.ds(k * half[axis], half[axis]),)
            for dz, (at, index) in enumerate(lists[k]):
                ref = ins[k][at] if index is None else ins[k][at].at[index]
                rest[-2 + k][dz] = ref[cut]

    return call(body, [((NZ,) + half, BF)] * 2, [ids, *from_x, *from_y], after=after)


def add_diagonal(ids, parts, axis, after=()):
    _, to_x, to_y, at_x, at_y = parts
    half = at_x.shape[axis + 1]

    def body(ids, to_x, to_y, at_x, at_y, out_x, out_y):
        cuts = [(slice(None),) * (axis + 1) + (pl.ds(k * half, half),) for k in range(2)]
        for k, (to, came, out) in enumerate(((to_x, at_x, out_x), (to_y, at_y, out_y))):
            out[cuts[k]] = (to[cuts[k]] + came[...].astype(F32)).astype(BF)
            out[cuts[1 - k]] = to[cuts[1 - k]].astype(BF)

    return call(body, [(to_x.shape, BF)] * 2, [ids, to_x, to_y, at_x, at_y], after=after)


def add_plane(ids, own, from_x, from_y, after=()):
    def body(ids, own, from_x, from_y, *outs):
        for step in range(NZ):
            plane = own[step] + from_x[step].astype(F32) + from_y[step].astype(F32)
            outs[step][...] = plane.astype(outs[step].dtype)

    outs = [(own.shape[1:], BF)] * (NZ - 1) + [(own.shape[1:], F32)]
    return call(body, outs, [ids, own, from_x, from_y], after=after)


def total_of(own, others):
    total = own[...]
    for other in others:
        total = total + other[...].astype(F32)
    return total


def add_all(ids, own, others):
    def body(ids, own, *rest):
        rest[-1][...] = total_of(own, rest[:-1])

    return call(body, [(own.shape, F32)], [ids, own, *others])[0]


def partial_gates(ids, wide, near, from_x, from_y, diagonal, channel_pieces, after=()):
    total, depth = wide.shape
    part = total // 4
    rows = depth // 2
    if channel_pieces:
        own, length = near[0].shape[-2:]
    else:
        length = near[0].shape[-1] * 8
    groups = [list(near), list(from_x), list(from_y), *[[part] for part in diagonal]]
    found = [array for group in groups for array in group]
    places = [stacked(group, 2) for group in groups]
    first = [sum(len(group) for group in groups[:at]) for at in range(len(groups))]

    def body(ids, w, *rest):
        ins, (u, mine, theirs) = rest[:-3], rest[-3:]
        z, x, y, c = ids[0], ids[1], ids[2], ids[3]
        for dz in range(NZ):
            refs = []
            for base, place in zip(first, places):
                at, index = place[dz]
                refs.append(ins[base + at] if index is None else ins[base + at].at[index])
            near, at_x, at_y, diag_a, diag_b = refs
            source = mod(z - dz)
            if channel_pieces:
                half = length // 2
                for other in range(2):
                    row = pl.multiple_of(flip(y, other) * rows + source * 2 * own, 16)
                    for k in range(2):
                        cols = pl.ds(k * half, half)
                        if other:
                            a, b = at_y[:, cols], (diag_a, diag_b)[k][...]
                        else:
                            a, b = near[:, cols], at_x[:, cols]
                        a, b = a.astype(F32), b.astype(F32)
                        pair = jnp.concatenate([jnp.where(x == 0, a, b), jnp.where(x == 0, b, a)], axis=0)
                        u[pl.ds(row, 2 * own), cols] = pair.astype(BF)
            else:
                block = length // 8
                here = pl.ds(pl.multiple_of((source * 2 + x) * block, block), block)
                there = pl.ds(pl.multiple_of((source * 2 + 1 - x) * block, block), block)
                top = pl.multiple_of(y * rows, 16)
                low = pl.multiple_of((1 - y) * rows, 16)
                u[pl.ds(top, rows), here] = near[...]
                u[pl.ds(top, rows), there] = at_x[...]
                u[pl.ds(low, rows), here] = at_y[...]
                u[pl.ds(low, rows // 2), there] = diag_a[...]
                u[pl.ds(pl.multiple_of(low + rows // 2, 16), rows // 2), there] = diag_b[...]
        lane = lax.broadcasted_iota(jnp.int32, (part, SPAN), 1)

        def step(cols, k, carry):
            lasts = []
            for out, core, before in ((mine, c, carry[0]), (theirs, 1 - c, carry[1])):
                rows = pl.ds(pl.multiple_of(core * 2 * part, 16), 2 * part)
                made = jnp.dot(w[rows, :], u[:, cols], preferred_element_type=F32)
                prev = made[:part]
                out[:, cols] = made[part:] + jnp.where(lane == 0, before, pltpu.roll(prev, 1, 1))
                lasts.append(prev[:, SPAN - 1 :])
            return tuple(lasts)

        zero = jnp.zeros((part, 1), F32)
        spans(length, step, (zero, zero))

    return call(
        body,
        [((depth, length), BF), ((part, length), F32), ((part, length), F32)],
        [ids, wide, *found],
        after=after,
        flops=2 * total * depth * length,
    )


def spans(length, step, carry, backward=False):
    count = length // SPAN

    def run(n, carry):
        k = count - 1 - n if backward else n
        return step(pl.ds(pl.multiple_of(k * SPAN, SPAN), SPAN), k, carry)

    return lax.fori_loop(0, count, run, carry)


def scan_span(forget, driven, carry, backward):
    own, length = driven.shape
    lane = lax.broadcasted_iota(jnp.int32, (own, LANES), 1)
    blocks = [slice(at, at + LANES) for at in range(0, length, LANES)]
    reach, state = [forget[:, cols] for cols in blocks], [driven[:, cols] for cols in blocks]
    by = 1
    while by < LANES:
        shift = LANES - by if backward else by
        inside = lane < LANES - by if backward else lane >= by
        for at in range(len(blocks)):
            r, s = reach[at], state[at]
            state[at] = s + jnp.where(inside, r * pltpu.roll(s, shift, 1), 0.0)
            reach[at] = jnp.where(inside, r * pltpu.roll(r, shift, 1), r)
        by *= 2
    for at in range(len(blocks))[:: -1 if backward else 1]:
        state[at] = state[at] + reach[at] * carry
        carry = state[at][:, :1] if backward else state[at][:, LANES - 1 :]
    return jnp.concatenate(state, axis=1), carry


def squash(value):
    return 1.0 / (1.0 + jnp.exp(-value))


def forward_scan(mine, theirs, bias, cand, forg, outg, cells, result):
    own, length = cells.shape

    def step(cols, k, carry):
        gates = []
        for g in range(3):
            rows = pl.ds(g * own, own)
            gates.append(mine[rows, cols] + theirs[rows, cols] + bias[rows, :])
        candidate, forget, outgate = jnp.tanh(gates[0]), squash(gates[1]), squash(gates[2])
        state, carry = scan_span(forget, (1.0 - forget) * candidate, carry, False)
        cand[:, cols], forg[:, cols], outg[:, cols], cells[:, cols] = candidate, forget, outgate, state
        result(cols, outgate * state)
        return carry

    spans(length, step, jnp.zeros((own, 1), F32))


def backward_scan(grad_of, cand, forg, outg, cells, gate_grad):
    own, length = cells.shape
    lane = lax.broadcasted_iota(jnp.int32, (own, SPAN), 1)

    def step(cols, k, carry):
        adjoint_after, forget_after = carry
        grad, a, f, o, now = grad_of(cols), cand[:, cols], forg[:, cols], outg[:, cols], cells[:, cols]
        later = jnp.where(lane == SPAN - 1, forget_after, pltpu.roll(f, SPAN - 1, 1))
        adjoint, adjoint_first = scan_span(later, grad * o, adjoint_after, True)
        last = cells[:, pl.ds(pl.multiple_of(jnp.maximum(k * SPAN - LANES, 0), LANES), LANES)][:, LANES - 1 :]
        before = jnp.where(lane == 0, jnp.where(k == 0, 0.0, last), pltpu.roll(now, 1, 1))
        away = 1.0 - f
        gate_grad[:, cols] = jnp.concatenate(
            [
                adjoint * away * (1.0 - a * a),
                adjoint * (before - a) * f * away,
                grad * now * o * (1.0 - o),
            ],
            axis=0,
        ).astype(BF)
        return adjoint_first, f[:, :1]

    zero = jnp.zeros((own, 1), F32)
    spans(length, step, (zero, zero), True)


def first_cells(ids, mine, theirs, bias, after=()):
    part, length = mine.shape
    own = part // 3

    def body(ids, mine, theirs, bias, hidden, cand, forg, outg, cells):
        def result(cols, value):
            hidden[:, cols] = value.astype(BF)

        forward_scan(mine, theirs, bias, cand, forg, outg, cells, result)

    return call(
        body,
        [((own, length), BF)] + [((own, length), F32)] * 4,
        [ids, mine, theirs, bias],
        after=after,
    )


def first_gate_grad(ids, own, others, saved, after=()):
    channels, length = own.shape

    def body(ids, own, *rest):
        ins, (cand, forg, outg, cells), gate_grad = rest[: len(others)], rest[-5:-1], rest[-1]

        def grad_of(cols):
            total = own[:, cols]
            for other in ins:
                total = total + other[:, cols].astype(F32)
            return total

        backward_scan(grad_of, cand, forg, outg, cells, gate_grad)

    return call(body, [((3 * channels, length), BF)], [ids, own, *others, *saved], after=after)[0]


def second_cells(ids, mine, theirs, bias, cot_pieces):
    part, length = mine.shape
    own = part // 3
    block = length // 8

    def body(ids, mine, theirs, bias, *rest):
        cots, outs, gate_grad = rest[:NZ], rest[NZ : NZ + 2], rest[NZ + 2]
        grad, cand, forg, outg, cells, made = rest[NZ + 3 :]
        z, x = ids[0], ids[1]
        for dz in range(NZ):
            for dx in range(2):
                i = mod(z - dz) * 2 + flip(x, dx)
                grad[:, pl.ds(pl.multiple_of(i * block, block), block)] = cots[dz][dx]

        def result(cols, value):
            made[:, cols] = value.astype(BF)

        forward_scan(mine, theirs, bias, cand, forg, outg, cells, result)
        for dz in range(NZ):
            for dx in range(2):
                i = mod(z + dz) * 2 + flip(x, dx)
                outs[dx][dz] = made[:, pl.ds(pl.multiple_of(i * block, block), block)]
        backward_scan(lambda cols: grad[:, cols].astype(F32), cand, forg, outg, cells, gate_grad)

    made = call(
        body,
        [((NZ, own, block), BF)] * 2 + [((part, length), BF)],
        [ids, mine, theirs, bias, *cot_pieces],
        [pltpu.VMEM((own, length), BF)] + [pltpu.VMEM((own, length), F32)] * 4 + [pltpu.VMEM((own, length), BF)],
    )
    return made[:2], made[2]


def split_cotangent(ids, cotangent):
    channels, block = cotangent.shape
    own = channels // 8

    def body(ids, cot, *rest):
        outs, wide = rest[:2], rest[2]
        wide[...] = cot[...].astype(F32)
        for dz in range(NZ):
            for dx in range(2):
                i = mod(ids[0] + dz) * 2 + flip(ids[1], dx)
                outs[dx][dz] = wide[pl.ds(pl.multiple_of(i * own, 8), own), :].astype(BF)

    return call(body, [((NZ, own, block), BF)] * 2, [ids, cotangent], [pltpu.VMEM((channels, block), F32)])


def pair_up(ids, first, second, after=()):
    shape = (2,) + first.shape[1:]

    def body(ids, first, second, *outs):
        for at in range(NZ):
            outs[at][0] = first[at]
            outs[at][1] = second[at]

    return call(body, [(shape, BF)] * NZ, [ids, first, second], after=after)


def join_outputs(ids, pieces):
    _, own, block = pieces[0].shape

    def body(ids, *rest):
        ins, out, wide = rest[:NZ], rest[NZ], rest[NZ + 1]
        for dz in range(NZ):
            for dx in range(2):
                i = mod(ids[0] - dz) * 2 + flip(ids[1], dx)
                wide[pl.ds(pl.multiple_of(i * own, 8), own), :] = ins[dz][dx].astype(F32)
        out[...] = wide[...].astype(BF)

    return call(body, [((8 * own, block), BF)], [ids, *pieces], [pltpu.VMEM((8 * own, block), F32)])[0]


def input_parts(ids, tall, mine, theirs, channel_pieces, after=()):
    depth, total = tall.shape
    part, length = mine.shape
    rows = depth // 2
    own = rows // 8
    block = length // 8
    shape = (NZ, own, length) if channel_pieces else (NZ, rows, block)
    half = (NZ, own, length // 2) if channel_pieces else (NZ, rows // 2, block)

    def body(ids, w, mine, theirs, grads, *rest):
        outs, v = rest[:5], rest[5]
        z, x, y, c = ids[0], ids[1], ids[2], ids[3]
        lane = lax.broadcasted_iota(jnp.int32, (part, SPAN), 1)

        def product(cols, k, carry):
            firsts = []
            for given, core, first in ((mine, c, carry[0]), (theirs, 1 - c, carry[1])):
                now = given[:, cols].astype(F32)
                later = jnp.where(lane == SPAN - 1, first, pltpu.roll(now, SPAN - 1, 1))
                at = pl.ds(pl.multiple_of(core * 2 * part, 16), 2 * part)
                grads[at, cols] = jnp.concatenate([later, now], axis=0).astype(BF)
                firsts.append(now[:, :1])
            v[:, cols] = jnp.dot(w[...], grads[:, cols], preferred_element_type=F32)
            return tuple(firsts)

        zero = jnp.zeros((part, 1), F32)
        spans(length, product, (zero, zero), True)
        for step in range(NZ):
            target = mod(z + 1 + step)

            def piece(dx, dy, k=None):
                i = target * 2 + flip(x, dx)
                if channel_pieces:
                    row = pl.multiple_of(flip(y, dy) * rows + i * own, 8)
                    cols = slice(None) if k is None else pl.ds(k * length // 2, length // 2)
                    return v[pl.ds(row, own), cols]
                cols = pl.ds(pl.multiple_of(i * block, block), block)
                row = flip(y, dy) * rows
                if k is None:
                    return v[pl.ds(pl.multiple_of(row, 8), rows), cols]
                return v[pl.ds(pl.multiple_of(row + k * rows // 2, 8), rows // 2), cols]

            outs[0][step] = piece(0, 0)
            outs[1][step] = piece(1, 0)
            outs[2][step] = piece(0, 1)
            outs[3][step] = piece(1, 1, 0).astype(BF)
            outs[4][step] = piece(1, 1, 1).astype(BF)

    made = call(
        body,
        [((total, length), BF), (shape, F32), (shape, F32), (shape, F32), (half, BF), (half, BF)],
        [ids, tall, mine, theirs],
        [pltpu.VMEM((depth, length), F32)],
        after=after,
        flops=2 * depth * total * length,
    )
    return made[0], made[1:]


def weight_blocks(ids, grads, u, after=()):
    total, length = grads.shape
    depth = u.shape[0]
    part, rows = total // 4, depth // 2

    def body(ids, grads, u, *rest):
        outs, made = rest[:NZ], rest[NZ]
        z, x = ids[0], ids[1]
        contract = (((1,), (1,)), ((), ()))
        for y in range(2):
            made[y] = lax.dot_general(
                grads[...], u[pl.ds(y * rows, rows), :], contract, preferred_element_type=F32
            )
        sums = lax.dot_general(jnp.ones((8, length), BF), grads[...], contract, preferred_element_type=F32)
        line = lax.broadcasted_iota(jnp.int32, (8, part), 0)
        tails = []
        for r in range(2):
            bias = jnp.where(flip(x, r) == 0, sums[:, part : 2 * part], sums[:, 3 * part : 4 * part])
            high = bias.astype(BF).astype(F32)
            tail = jnp.where(line == 0, high, jnp.where(line == 1, bias - high, 0.0))
            tails.append(jnp.concatenate([tail, jnp.zeros((8, rows - part), F32)], axis=1))
        for dz in range(NZ):
            source = mod(z - dz)
            both = []
            for r in range(2):
                at = pl.ds(pl.multiple_of((flip(x, r) * 2 + source // 2) * part, 8), part)
                both.append(jnp.concatenate([made[lax.rem(source, 2), at, :], tails[r]], axis=0))
            outs[dz][...] = jnp.concatenate(both, axis=1).astype(BF)

    return call(
        body,
        [((part + 8, 2 * rows), BF)] * NZ,
        [ids, grads, u],
        [pltpu.VMEM((2, total, rows), F32)],
        after=after,
        flops=2 * depth * total * length,
    )


def unpack_weight(ids, groups):
    _, height, width = groups[0].shape
    part, rows = height - 8, width // 2
    own = part // 3
    columns = own * 8

    def body(ids, r0, r1, out, bias, joined):
        z, c = ids[0], ids[3]
        for r, group in enumerate((r0, r1)):
            for pair in range(NZ // 2):
                both = group[pair].astype(F32)
                for k in range(2):
                    i = mod(z + 2 * pair + k) * 2 + flip(c, r)
                    block = both[:, k * rows : (k + 1) * rows]
                    for g in range(3):
                        at = pl.ds(pl.multiple_of(i * own, 8), own)
                        joined[g, at, :] = block[g * own : (g + 1) * own]
                    bias[pl.ds(i, 1), :] = (block[part : part + 1] + block[part + 1 : part + 2])[:, :part]
        for g in range(3):
            out[g] = joined[g].T

    grad, bias = call(
        body,
        [((3, rows, columns), F32), ((8, part), F32)],
        [ids, *groups],
        [pltpu.VMEM((3, columns, rows), F32)],
    )
    bias = jnp.transpose(bias.reshape(8, 3, own), (1, 0, 2)).reshape(3, columns)
    return grad, bias


def owned_bias(bias, own):
    i = lax.axis_index("tm")
    return lax.dynamic_slice_in_dim(bias, i * own, own, axis=1).reshape(3 * own, 1)


def back_rounds(ids, parts, blocks, axis, after=()):
    blocks = blocks_over_z(blocks, -1)
    parts = [*parts[:3], over_y(parts[3]), over_x(parts[4])]
    sent_x, sent_y = add_diagonal(ids, parts, axis, after=after)
    groups = regroup_back(ids, blocks)
    *planes, own = add_plane(ids, parts[0], over_x(sent_x), over_y(sent_y), after=groups)
    others = [over_z(plane, step + 1) for step, plane in enumerate(planes)]
    return own, others, blocks_over_x(groups, True)


def owned_channels(inputs, first_weight, first_bias, second_weight, second_bias, cotangent):
    tm, mp = lax.axis_index("tm"), lax.axis_index("mp")
    ids = jnp.stack([tm // 2, tm % 2, mp // 2, mp % 2]).astype(jnp.int32)
    own = first_weight.shape[2] // 8

    *w1, u_piece = pack_weight(ids, first_weight, inputs[0].T)
    near, w1 = regroup(ids, along_z(u_piece), blocks_over_x(w1))
    from_x, from_y = over_x(near), over_y(near)
    wide_1, tall_1 = join_weight(ids, blocks_over_z(w1, 1))
    diag = corner(ids, [from_x], [from_y], 0)
    diag = [over_y(diag[0]), over_x(diag[1])]
    w2 = pack_weight(ids, second_weight)
    cot_here, cot_there = split_cotangent(ids, cotangent[0].T)
    cots = pair_up(ids, cot_here, over_x(cot_there))

    u, mine, theirs = partial_gates(ids, wide_1, [near], [from_x], [from_y], diag, False, after=[*w2, *cots])
    cots = [cots[0]] + [over_z(cots[dz], dz) for dz in range(1, NZ)]
    w2 = blocks_over_x(relay(w2, diag))
    (ids_2,) = relay([ids], [*w2, *cots[1:]], SOON)
    hidden, *saved = first_cells(ids_2, mine, over_core(theirs), owned_bias(first_bias, own))

    from_x, from_y = [over_x(hidden)], [over_y(hidden)]
    far, w2 = regroup(ids, along_z(hidden)[1:], w2, after=[*from_x, *from_y])
    from_x, from_y = [*from_x, over_x(far)], [*from_y, over_y(far)]
    wide_2, tall_2 = join_weight(ids, blocks_over_z(w2, 1))
    diag = corner(ids, from_x, from_y, 1)
    diag = [over_y(diag[0]), over_x(diag[1])]
    h, mine, theirs = partial_gates(ids, wide_2, [hidden, far], from_x, from_y, diag, True)
    outs, gate_grad = second_cells(ids, mine, over_core(theirs), owned_bias(second_bias, own), cots)

    outs = pair_up(ids, outs[0], over_x(outs[1]))
    grads, parts = input_parts(ids, tall_2, gate_grad, over_core(gate_grad), True)
    dw2 = weight_blocks(ids, grads, h, after=outs)
    plane, others, dw2 = back_rounds(ids, parts, dw2, 1)
    gate_grad = first_gate_grad(ids, plane, others, saved, after=dw2)

    grads, parts = input_parts(ids, tall_1, gate_grad, over_core(gate_grad), False)
    outs = [outs[0]] + [over_z(outs[dz], dz) for dz in range(1, NZ)]
    dw1 = weight_blocks(ids, grads, u, after=outs)
    second_grad, second_bias_grad = unpack_weight(ids, dw2)
    outputs = join_outputs(ids, outs)
    plane, others, dw1 = back_rounds(ids, parts, dw1, 0, [second_grad, outputs])
    input_grad = add_all(ids, plane, others)
    first_grad, first_bias_grad = unpack_weight(ids, dw1)
    first_grad, second_grad = (jnp.transpose(grad, (1, 0, 2)) for grad in (first_grad, second_grad))
    return (
        outputs.T[None],
        input_grad.T[None],
        first_grad,
        first_bias_grad,
        second_grad,
        second_bias_grad,
    )


def prefix(value, axis, join, neutral, backward):
    count, mine = (lax.axis_size(axis), lax.axis_index(axis))
    pieces = jax.tree.map(lambda part: lax.all_gather(part, axis), value)
    if backward:
        pieces = jax.tree.map(lambda part: part[::-1], pieces)
        mine = count - 1 - mine
    total = jax.tree.map(
        lambda part, zero: jnp.full_like(part, 0) + jnp.asarray(zero, part.dtype), value, neutral
    )

    def hop(position, total):
        longer = join(total, jax.tree.map(lambda part: part[position], pieces))
        return jax.tree.map(lambda new, old: jnp.where(position < mine, new, old), longer, total)

    return lax.fori_loop(0, count - 1, hop, total)


def passed_along(array, axis, by):
    size = lax.axis_size(axis)
    pairs = [(i, i + by) for i in range(size) if 0 <= i + by < size]
    return lax.ppermute(array, axis, pairs)


def affine_join(earlier, later):
    return (earlier[0] * later[0], later[0] * earlier[1] + later[1])


def weight_view(gathered):
    return gathered.reshape(2, gathered.shape[0] // 2, gathered.shape[1] * gathered.shape[2])


def span_prefix(product, offset):
    identity = (jnp.ones_like(product), jnp.zeros_like(offset))
    result = prefix((product, offset), "tm", affine_join, identity, False)
    return result[1]


def span_suffix(product, offset):
    identity = (jnp.ones_like(product), jnp.zeros_like(offset))
    result = prefix((product, offset), "tm", affine_join, identity, True)
    return result[1]


def forward_layer(layer_in, view, bias):
    seq_count, length, channels = layer_in.shape
    prev_row = passed_along(layer_in[:, length - 1 :], "tm", 1)
    previous = jnp.concatenate([prev_row, layer_in[:, : length - 1]], axis=1)
    stacked = jnp.stack([previous, layer_in])
    summed = jnp.einsum(
        "jsck,jkn->scn",
        lax.all_gather(stacked, "mp", axis=3, tiled=True),
        view,
        preferred_element_type=jnp.float32,
    )
    gates = summed.reshape(seq_count, length, 3, channels) + bias
    candidate = jnp.tanh(gates[:, :, 0])
    forget = jax.nn.sigmoid(gates[:, :, 1])
    outgate = jax.nn.sigmoid(gates[:, :, 2])
    product, offset = lax.associative_scan(
        affine_join, (forget, (1.0 - forget) * candidate), axis=1
    )
    carry_in = span_prefix(product[:, length - 1], offset[:, length - 1])
    cells = offset + product * carry_in[:, None]
    cells_prev = jnp.concatenate([carry_in[:, None], cells[:, : length - 1]], axis=1)
    return (outgate * cells, (stacked, candidate, forget, outgate, cells, cells_prev))


def backward_layer(grad_in, saved, view):
    stacked, candidate, forget, outgate, cells, cells_prev = saved
    seq_count, length, channels = grad_in.shape
    driven = grad_in * outgate
    next_forget = jnp.concatenate([forget[:, 1:], jnp.ones_like(forget[:, :1])], axis=1)
    reach, local_adj = lax.associative_scan(
        affine_join, (next_forget[:, ::-1], driven[:, ::-1]), axis=1
    )
    reach = reach[:, ::-1]
    local_adj = local_adj[:, ::-1]
    first_forget = forget[:, 0]
    incoming = span_suffix(first_forget * reach[:, 0], first_forget * local_adj[:, 0])
    adjoint = local_adj + reach * incoming[:, None]
    grad_cand = adjoint * (1.0 - forget) * (1.0 - candidate * candidate)
    grad_forget = adjoint * (cells_prev - candidate) * forget * (1.0 - forget)
    grad_outgate = grad_in * cells * outgate * (1.0 - outgate)
    gate_grad = jnp.stack([grad_cand, grad_forget, grad_outgate], axis=2).astype(jnp.bfloat16)
    flat_grad = gate_grad.reshape(seq_count, length, 3 * channels)
    bias_part = jnp.sum(gate_grad, axis=(0, 1), dtype=jnp.float32)
    back_both = jnp.einsum("scn,jkn->jsck", flat_grad, view, preferred_element_type=jnp.float32)
    from_prev = back_both[0]
    from_current = back_both[1]
    local_grad = from_current + jnp.concatenate(
        [from_prev[:, 1:], jnp.zeros_like(from_prev[:, :1])], axis=1
    )
    tail_rows = from_prev[:, :1]
    shard_grad, tail_shard = (
        lax.psum_scatter(local_grad, "mp", scatter_dimension=2, tiled=True),
        lax.psum_scatter(tail_rows, "mp", scatter_dimension=2, tiled=True),
    )
    tail_next = passed_along(tail_shard, "tm", -1)
    layer_grad = shard_grad + jnp.concatenate(
        [jnp.zeros_like(shard_grad[:, : length - 1]), tail_next], axis=1
    )
    weight_full = jnp.einsum(
        "jsck,scn->jkn",
        lax.all_gather(stacked, "mp", axis=3, tiled=True),
        flat_grad,
        preferred_element_type=jnp.float32,
    )
    weight_full = weight_full.reshape(2 * weight_full.shape[1], 3, channels)
    weight_shard = lax.psum_scatter(weight_full, "tm", scatter_dimension=0, tiled=True)
    bias_grad = lax.psum(bias_part, "tm")
    return (layer_grad, weight_shard, bias_grad)


def per_device(inputs, first_weight, first_bias, second_weight, second_bias, cotangent):
    full_first, full_second = (
        lax.all_gather(first_weight, "tm", axis=0, tiled=True),
        lax.all_gather(second_weight, "tm", axis=0, tiled=True),
    )
    view_first = weight_view(full_first)
    view_second = weight_view(full_second)
    hidden_out, saved_first = forward_layer(inputs, view_first, first_bias)
    hidden = hidden_out.astype(jnp.bfloat16)
    top_out, saved_second = forward_layer(hidden, view_second, second_bias)
    again_first, again_second = (
        lax.all_gather(first_weight, "tm", axis=0, tiled=True),
        lax.all_gather(second_weight, "tm", axis=0, tiled=True),
    )
    back_first = weight_view(again_first)
    back_second = weight_view(again_second)
    hidden_grad, second_weightgrad, second_biasgrad = backward_layer(
        cotangent.astype(jnp.float32), saved_second, back_second
    )
    input_grad, first_weightgrad, first_biasgrad = backward_layer(
        hidden_grad, saved_first, back_first
    )
    return (
        top_out.astype(jnp.bfloat16),
        input_grad,
        first_weightgrad,
        first_biasgrad,
        second_weightgrad,
        second_biasgrad,
    )


def choose(owned):
    def run(inputs, first_weight, *rest):
        sizes = inputs.shape[0] == 1 and inputs.shape[1] == 256 and first_weight.shape == (576, 3, 576)
        plan = owned_channels if owned and sizes else per_device
        return plan(inputs, first_weight, *rest)

    return run


def solution(mesh):
    placed = (
        P(None, "tm", "mp"),
        P("tm", None, "mp"),
        P(None, "mp"),
        P("tm", None, "mp"),
        P(None, "mp"),
        P(None, "tm", "mp"),
    )
    owned = mesh.shape["tm"] == 2 * NZ and mesh.shape["mp"] == 4
    return jax.shard_map(
        choose(owned),
        mesh=mesh,
        in_specs=placed,
        out_specs=(
            P(None, "tm", "mp"),
            P(None, "tm", "mp"),
            P("tm", None, "mp"),
            P(None, "mp"),
            P("tm", None, "mp"),
            P(None, "mp"),
        ),
        check_vma=False,
    )
```

```python
import jax
import jax.numpy as jnp
from jax import lax
from jax.experimental import pallas as pl
from jax.experimental.pallas import tpu as pltpu
from jax.sharding import PartitionSpec as P

BF = jnp.bfloat16
F32 = jnp.float32
LANES = 128
SPAN = 512
MIB = 2**20

NZ = 4


def mod(value):
    return lax.rem(value + 2 * NZ, NZ)


def flip(bit, by):
    return bit if by == 0 else 1 - bit


def moved(array, target):
    pairs = []
    for z in range(NZ):
        for x in range(2):
            for y in range(2):
                for c in range(2):
                    tz, tx, ty, tc = target(z, x, y, c)
                    pairs.append(((z * 2 + x) * 4 + y * 2 + c, (tz * 2 + tx) * 4 + ty * 2 + tc))
    return lax.ppermute(array, ("tm", "mp"), pairs)


def over_x(array):
    return moved(array, lambda z, x, y, c: (z, 1 - x, y, c))


def over_y(array):
    return moved(array, lambda z, x, y, c: (z, x, 1 - y, c))


def over_core(array):
    return moved(array, lambda z, x, y, c: (z, x, y, 1 - c))


def over_z(array, by):
    return moved(array, lambda z, x, y, c: ((z + by) % NZ, x, y, c))


def call(body, outs, args, scratch=(), vmem=28, flops=0, after=(), far_in=(), far_out=()):
    whole = pl.BlockSpec(memory_space=pltpu.VMEM)
    anywhere = pl.BlockSpec(memory_space=pl.ANY)
    moved_bytes = sum(a.size * a.dtype.itemsize for at, a in enumerate(args) if at not in far_in)
    for at, (shape, kind) in enumerate(outs):
        size = 0 if at in far_out else jnp.dtype(kind).itemsize
        for extent in shape:
            size *= extent
        moved_bytes += size
    specs = [pl.BlockSpec(memory_space=pltpu.SMEM)]
    specs += [anywhere if at in far_in else whole for at in range(1, len(args))]
    specs += [anywhere] * len(after)
    count = len(args)

    def run(*refs):
        body(*refs[:count], *refs[count + len(after) :])

    return pl.pallas_call(
        run,
        out_shape=[jax.ShapeDtypeStruct(shape, kind) for shape, kind in outs],
        in_specs=specs,
        out_specs=[anywhere if at in far_out else whole for at in range(len(outs))],
        scratch_shapes=list(scratch),
        compiler_params=pltpu.CompilerParams(vmem_limit_bytes=vmem * MIB),
        cost_estimate=pl.CostEstimate(flops=flops, bytes_accessed=moved_bytes, transcendentals=0),
    )(*args, *after)


ROOMY = 42 * 10**6


def roomy(shape, kind):
    size = jnp.dtype(kind).itemsize
    for extent in shape:
        size *= extent
    return ((-(-ROOMY // size),) + shape, kind)


EARLY = 10**11
SOON = 10**10


def relay(arrays, after, flops=0):
    anywhere = pl.BlockSpec(memory_space=pl.ANY)
    count = len(arrays)

    def body(*refs):
        pass

    return pl.pallas_call(
        body,
        out_shape=[jax.ShapeDtypeStruct(array.shape, array.dtype) for array in arrays],
        in_specs=[anywhere] * (count + len(after)),
        out_specs=[anywhere] * count,
        input_output_aliases={at: at for at in range(count)},
        cost_estimate=pl.CostEstimate(flops=flops, bytes_accessed=0, transcendentals=0),
    )(*arrays, *after)


def pack_weight(ids, weight, bias, along=None, after=()):
    rows, gates, columns = weight.shape
    own = columns // 8
    extra = [] if along is None else [along]

    def body(ids, w, bias, *rest):
        outs, column = rest[len(extra) : len(extra) + 2], rest[len(extra) + 2]
        turned, upright = rest[-2:]
        if extra:
            rest[-3][...] = rest[0][...]
        z, x, c = ids[0], ids[1], ids[3]
        mine = pl.ds(pl.multiple_of((z * 2 + x) * own, 8), own)
        for g in range(gates):
            upright[...] = jnp.broadcast_to(bias[g : g + 1, :], (8, columns)).T
            column[pl.ds(g * own, own), :] = upright[mine, :1]
        for g in range(gates):
            turned[g] = w[g].astype(F32).T
        for r in range(2):
            for pair in range(NZ // 2):
                both = []
                for dz in (2 * pair, 2 * pair + 1):
                    at = pl.ds(pl.multiple_of((mod(z + dz) * 2 + flip(c, r)) * own, 8), own)
                    both.append(jnp.concatenate([turned[g, at, :] for g in range(gates)], axis=0))
                outs[r][pair] = jnp.concatenate(both, axis=1).astype(BF)

    return call(
        body,
        [((NZ // 2, gates * own, 2 * rows), BF)] * 2
        + [((gates * own, 1), F32)]
        + [(a.shape, a.dtype) for a in extra],
        [ids, jnp.transpose(weight, (1, 0, 2)), bias, *extra],
        [pltpu.VMEM((gates, columns, rows), F32), pltpu.VMEM((columns, 8), F32)],
        after=after,
    )


def blocks_over_x(groups, back=False):
    def to(r):
        if back:
            return lambda z, x, y, c: (z, c, y, x ^ r)
        return lambda z, x, y, c: (z, c ^ r, y, x)

    return [moved(groups[r], to(r)) for r in range(2)]


def blocks_over_z(both, sign):
    return [both[0]] + [over_z(both[dz], sign * dz) for dz in range(1, NZ)]


def regroup(ids, pieces, groups, after=()):
    count, wide = len(pieces), len(groups) > 0
    outs = [((count,) + pieces[0].shape, BF)] if count else []
    if wide:
        _, part, width = groups[0].shape
        rows = width // 2
        outs += [((part, width), BF)] * NZ

    def body(ids, *rest):
        ins, given = rest[:count], rest[count : count + len(groups)]
        made = rest[count + len(groups) :]
        for at in range(count):
            made[0][at] = ins[at][...]
        for dz in range(NZ if wide else 0):
            lanes = slice((dz % 2) * rows, (dz % 2 + 1) * rows)
            parts = [group[dz // 2].astype(F32)[:, lanes] for group in given]
            made[-NZ + dz][...] = jnp.concatenate(parts, axis=1).astype(BF)

    made = list(call(body, outs, [ids, *pieces, *groups], after=after))
    return (made[:1] if count else []) + [made[-NZ:]] * wide


def regroup_back(ids, both, after=()):
    part, width = both[0].shape
    rows = width // 2

    def body(ids, *rest):
        ins, outs = rest[:NZ], rest[NZ:]
        for r in range(2):
            lanes = slice(r * rows, (r + 1) * rows)
            for pair in range(NZ // 2):
                parts = [ins[2 * pair + k][...].astype(F32)[:, lanes] for k in range(2)]
                outs[r][pair] = jnp.concatenate(parts, axis=1).astype(BF)

    return call(body, [((NZ // 2, part, width), BF)] * 2, [ids, *both], after=after, flops=EARLY)


def join_weight(ids, blocks):
    part, width = blocks[0].shape
    rows = width // 2

    def body(ids, *rest):
        ins, (wide, tall), joined = rest[:NZ], rest[NZ : NZ + 2], rest[NZ + 2]
        z, x = ids[0], ids[1]
        for dz in range(NZ):
            source = mod(z - dz)
            both = ins[dz][...].astype(F32)
            for r in range(2):
                base = (flip(x, r) * 2 + source // 2) * part
                at = pl.ds(pl.multiple_of(base, 8), part)
                joined[lax.rem(source, 2), at, :] = both[:, r * rows : (r + 1) * rows]
        for half in range(2):
            at = pl.ds(half * 2 * part, 2 * part)
            both = jnp.concatenate([joined[0, at, :], joined[1, at, :]], axis=1)
            wide[at, :] = both.astype(BF)
        for y in range(2):
            tall[pl.ds(y * rows, rows), :] = joined[y].T.astype(BF)

    return call(
        body,
        [((4 * part, 2 * rows), BF), ((2 * rows, 4 * part), BF)],
        [ids, *blocks],
        [pltpu.VMEM((2, 4 * part, rows), F32)],
        flops=EARLY,
    )


def halves(array, axis):
    half = array.shape[axis] // 2
    return lax.slice_in_dim(array, 0, half, axis=axis), lax.slice_in_dim(array, half, 2 * half, axis=axis)


def along_z(piece):
    return [piece] + [over_z(piece, dz) for dz in range(1, NZ)]


def stacked(arrays, rank):
    found = []
    for at, array in enumerate(arrays):
        found += [(at, None)] if len(array.shape) == rank else [(at, k) for k in range(array.shape[0])]
    return found


def corner(ids, from_x, from_y, axis, after=()):
    lists = [stacked(part, 2) for part in (from_x, from_y)]
    piece = from_x[0].shape[-2:]
    half = tuple(extent // 2 if at == axis else extent for at, extent in enumerate(piece))

    def body(ids, *rest):
        ins = rest[: len(from_x)], rest[len(from_x) : -2]
        for k in range(2):
            cut = (slice(None),) * axis + (pl.ds(k * half[axis], half[axis]),)
            for dz, (at, index) in enumerate(lists[k]):
                ref = ins[k][at] if index is None else ins[k][at].at[index]
                rest[-2 + k][dz] = ref[cut]

    return call(body, [((NZ,) + half, BF)] * 2, [ids, *from_x, *from_y], after=after)


def add_diagonal(ids, parts, axis, after=()):
    _, to_x, to_y, at_x, at_y = parts
    half = at_x.shape[axis + 1]

    def body(ids, to_x, to_y, at_x, at_y, out_x, out_y):
        cuts = [(slice(None),) * (axis + 1) + (pl.ds(k * half, half),) for k in range(2)]
        for k, (to, came, out) in enumerate(((to_x, at_x, out_x), (to_y, at_y, out_y))):
            out[cuts[k]] = (to[cuts[k]] + came[...].astype(F32)).astype(BF)
            out[cuts[1 - k]] = to[cuts[1 - k]].astype(BF)

    return call(body, [(to_x.shape, BF)] * 2, [ids, to_x, to_y, at_x, at_y], after=after)


def add_plane(ids, own, from_x, from_y, after=()):
    def body(ids, own, from_x, from_y, *outs):
        for step in range(NZ):
            plane = own[step] + from_x[step].astype(F32) + from_y[step].astype(F32)
            outs[step][...] = plane.astype(outs[step].dtype)

    outs = [(own.shape[1:], BF)] * (NZ - 1) + [(own.shape[1:], F32)]
    return call(body, outs, [ids, own, from_x, from_y], after=after)


def total_of(own, others):
    total = own[...]
    for other in others:
        total = total + other[...].astype(F32)
    return total


def add_all(ids, own, others):
    def body(ids, own, *rest):
        rest[-1][...] = total_of(own, rest[:-1])

    return call(body, [(own.shape, F32)], [ids, own, *others])[0]


def partial_gates(ids, wide, near, from_x, from_y, diagonal, channel_pieces, after=()):
    total, depth = wide.shape
    part = total // 4
    rows = depth // 2
    if channel_pieces:
        own, length = near[0].shape[-2:]
    else:
        length = near[0].shape[-1] * 8
    groups = [list(near), list(from_x), list(from_y), *[[part] for part in diagonal]]
    found = [array for group in groups for array in group]
    places = [stacked(group, 2) for group in groups]
    first = [sum(len(group) for group in groups[:at]) for at in range(len(groups))]

    def body(ids, w, *rest):
        ins, (kept, mine, theirs, u, done) = rest[:-5], rest[-5:]
        z, x, y, c = ids[0], ids[1], ids[2], ids[3]
        for dz in range(NZ):
            refs = []
            for base, place in zip(first, places):
                at, index = place[dz]
                refs.append(ins[base + at] if index is None else ins[base + at].at[index])
            near, at_x, at_y, diag_a, diag_b = refs
            source = mod(z - dz)
            if channel_pieces:
                half = length // 2
                for other in range(2):
                    row = pl.multiple_of(flip(y, other) * rows + source * 2 * own, 16)
                    for k in range(2):
                        cols = pl.ds(k * half, half)
                        if other:
                            a, b = at_y[:, cols], (diag_a, diag_b)[k][...]
                        else:
                            a, b = near[:, cols], at_x[:, cols]
                        a, b = a.astype(F32), b.astype(F32)
                        pair = jnp.concatenate([jnp.where(x == 0, a, b), jnp.where(x == 0, b, a)], axis=0)
                        u[pl.ds(row, 2 * own), cols] = pair.astype(BF)
            else:
                block = length // 8
                here = pl.ds(pl.multiple_of((source * 2 + x) * block, block), block)
                there = pl.ds(pl.multiple_of((source * 2 + 1 - x) * block, block), block)
                top = pl.multiple_of(y * rows, 16)
                low = pl.multiple_of((1 - y) * rows, 16)
                u[pl.ds(top, rows), here] = near[...]
                u[pl.ds(top, rows), there] = at_x[...]
                u[pl.ds(low, rows), here] = at_y[...]
                u[pl.ds(low, rows // 2), there] = diag_a[...]
                u[pl.ds(pl.multiple_of(low + rows // 2, 16), rows // 2), there] = diag_b[...]
        keep = pltpu.make_async_copy(u, kept.at[0], done)
        keep.start()
        lane = lax.broadcasted_iota(jnp.int32, (part, SPAN), 1)

        def step(cols, k, carry):
            lasts = []
            for out, core, before in ((mine, c, carry[0]), (theirs, 1 - c, carry[1])):
                rows = pl.ds(pl.multiple_of(core * 2 * part, 16), 2 * part)
                made = jnp.dot(w[rows, :], u[:, cols], preferred_element_type=F32)
                prev = made[:part]
                out[:, cols] = made[part:] + jnp.where(lane == 0, before, pltpu.roll(prev, 1, 1))
                lasts.append(prev[:, SPAN - 1 :])
            return tuple(lasts)

        zero = jnp.zeros((part, 1), F32)
        spans(length, step, (zero, zero))
        keep.wait()

    return call(
        body,
        [roomy((depth, length), BF), ((part, length), F32), ((part, length), F32)],
        [ids, wide, *found],
        [pltpu.VMEM((depth, length), BF), pltpu.SemaphoreType.DMA],
        after=after,
        flops=2 * total * depth * length,
        far_out=(0,),
    )


def spans(length, step, carry, backward=False):
    count = length // SPAN

    def run(n, carry):
        k = count - 1 - n if backward else n
        return step(pl.ds(pl.multiple_of(k * SPAN, SPAN), SPAN), k, carry)

    return lax.fori_loop(0, count, run, carry)


def scan_span(forget, driven, carry, backward):
    own, length = driven.shape
    lane = lax.broadcasted_iota(jnp.int32, (own, LANES), 1)
    blocks = [slice(at, at + LANES) for at in range(0, length, LANES)]
    reach, state = [forget[:, cols] for cols in blocks], [driven[:, cols] for cols in blocks]
    by = 1
    while by < LANES:
        shift = LANES - by if backward else by
        inside = lane < LANES - by if backward else lane >= by
        for at in range(len(blocks)):
            r, s = reach[at], state[at]
            state[at] = s + jnp.where(inside, r * pltpu.roll(s, shift, 1), 0.0)
            reach[at] = jnp.where(inside, r * pltpu.roll(r, shift, 1), r)
        by *= 2
    for at in range(len(blocks))[:: -1 if backward else 1]:
        state[at] = state[at] + reach[at] * carry
        carry = state[at][:, :1] if backward else state[at][:, LANES - 1 :]
    return jnp.concatenate(state, axis=1), carry


def squash(value):
    return 1.0 / (1.0 + jnp.exp(-value))


def forward_scan(mine, theirs, bias, cand, forg, outg, cells, result):
    own, length = cells.shape

    def step(cols, k, carry):
        gates = []
        for g in range(3):
            rows = pl.ds(g * own, own)
            gates.append(mine[rows, cols] + theirs[rows, cols] + bias[rows, :])
        candidate, forget, outgate = jnp.tanh(gates[0]), squash(gates[1]), squash(gates[2])
        state, carry = scan_span(forget, (1.0 - forget) * candidate, carry, False)
        cand[:, cols], forg[:, cols], outg[:, cols], cells[:, cols] = candidate, forget, outgate, state
        result(cols, outgate * state)
        return carry

    spans(length, step, jnp.zeros((own, 1), F32))


def backward_scan(grad_of, cand, forg, outg, cells, gate_grad):
    own, length = cells.shape
    lane = lax.broadcasted_iota(jnp.int32, (own, SPAN), 1)

    def step(cols, k, carry):
        adjoint_after, forget_after = carry
        grad, a, f, o, now = grad_of(cols), cand[:, cols], forg[:, cols], outg[:, cols], cells[:, cols]
        later = jnp.where(lane == SPAN - 1, forget_after, pltpu.roll(f, SPAN - 1, 1))
        adjoint, adjoint_first = scan_span(later, grad * o, adjoint_after, True)
        last = cells[:, pl.ds(pl.multiple_of(jnp.maximum(k * SPAN - LANES, 0), LANES), LANES)][:, LANES - 1 :]
        before = jnp.where(lane == 0, jnp.where(k == 0, 0.0, last), pltpu.roll(now, 1, 1))
        away = 1.0 - f
        gate_grad[:, cols] = jnp.concatenate(
            [
                adjoint * away * (1.0 - a * a),
                adjoint * (before - a) * f * away,
                grad * now * o * (1.0 - o),
            ],
            axis=0,
        ).astype(BF)
        return adjoint_first, f[:, :1]

    zero = jnp.zeros((own, 1), F32)
    spans(length, step, (zero, zero), True)


def first_cells(ids, mine, theirs, bias, after=()):
    part, length = mine.shape
    own = part // 3

    def body(ids, mine, theirs, bias, hidden, kept, *rest):
        made, done = rest[:4], rest[4]

        def result(cols, value):
            hidden[:, cols] = value.astype(BF)

        forward_scan(mine, theirs, bias, *made, result)
        copies = [pltpu.make_async_copy(made[at], kept.at[at], done.at[at]) for at in range(4)]
        for copy in copies:
            copy.start()
        for copy in copies:
            copy.wait()

    return call(
        body,
        [((own, length), BF), roomy((own, length), F32)],
        [ids, mine, theirs, bias],
        [pltpu.VMEM((own, length), F32)] * 4 + [pltpu.SemaphoreType.DMA((4,))],
        after=after,
        far_out=(1,),
    )


def first_gate_grad(ids, own, others, saved, after=()):
    channels, length = own.shape

    def body(ids, own, *rest):
        ins, held, gate_grad = rest[: len(others)], rest[-5:-1], rest[-1]

        def grad_of(cols):
            total = own[:, cols]
            for other in ins:
                total = total + other[:, cols].astype(F32)
            return total

        backward_scan(grad_of, *held, gate_grad)

    args = [ids, own, *others, *[saved[at] for at in range(4)]]
    return call(body, [((3 * channels, length), BF)], args, after=after)[0]


def second_cells(ids, mine, theirs, bias, cot_pieces):
    part, length = mine.shape
    own = part // 3
    block = length // 8

    def body(ids, mine, theirs, bias, *rest):
        cots, outs, gate_grad = rest[:NZ], rest[NZ : NZ + 2], rest[NZ + 2]
        grad, cand, forg, outg, cells, made = rest[NZ + 3 :]
        z, x = ids[0], ids[1]
        for dz in range(NZ):
            for dx in range(2):
                i = mod(z - dz) * 2 + flip(x, dx)
                grad[:, pl.ds(pl.multiple_of(i * block, block), block)] = cots[dz][dx]

        def result(cols, value):
            made[:, cols] = value.astype(BF)

        forward_scan(mine, theirs, bias, cand, forg, outg, cells, result)
        for dz in range(NZ):
            for dx in range(2):
                i = mod(z + dz) * 2 + flip(x, dx)
                outs[dx][dz] = made[:, pl.ds(pl.multiple_of(i * block, block), block)]
        backward_scan(lambda cols: grad[:, cols].astype(F32), cand, forg, outg, cells, gate_grad)

    made = call(
        body,
        [((NZ, own, block), BF)] * 2 + [((part, length), BF)],
        [ids, mine, theirs, bias, *cot_pieces],
        [pltpu.VMEM((own, length), BF)] + [pltpu.VMEM((own, length), F32)] * 4 + [pltpu.VMEM((own, length), BF)],
    )
    return made[:2], made[2]


def split_cotangent(ids, cotangent):
    channels, block = cotangent.shape
    own = channels // 8

    def body(ids, cot, *rest):
        outs, wide = rest[:2], rest[2]
        wide[...] = cot[...].astype(F32)
        for dz in range(NZ):
            for dx in range(2):
                i = mod(ids[0] + dz) * 2 + flip(ids[1], dx)
                outs[dx][dz] = wide[pl.ds(pl.multiple_of(i * own, 8), own), :].astype(BF)

    return call(body, [((NZ, own, block), BF)] * 2, [ids, cotangent], [pltpu.VMEM((channels, block), F32)])


def pair_up(ids, first, second, after=()):
    shape = (2,) + first.shape[1:]

    def body(ids, first, second, *outs):
        for at in range(NZ):
            outs[at][0] = first[at]
            outs[at][1] = second[at]

    return call(body, [(shape, BF)] * NZ, [ids, first, second], after=after)


def join_outputs(ids, pieces):
    _, own, block = pieces[0].shape

    def body(ids, *rest):
        ins, out, wide = rest[:NZ], rest[NZ], rest[NZ + 1]
        for dz in range(NZ):
            for dx in range(2):
                i = mod(ids[0] - dz) * 2 + flip(ids[1], dx)
                wide[pl.ds(pl.multiple_of(i * own, 8), own), :] = ins[dz][dx].astype(F32)
        out[...] = wide[...].astype(BF)

    return call(body, [((8 * own, block), BF)], [ids, *pieces], [pltpu.VMEM((8 * own, block), F32)])[0]


def input_parts(ids, tall, mine, theirs, channel_pieces, after=()):
    depth, total = tall.shape
    part, length = mine.shape
    rows = depth // 2
    own = rows // 8
    block = length // 8
    shape = (NZ, own, length) if channel_pieces else (NZ, rows, block)
    half = (NZ, own, length // 2) if channel_pieces else (NZ, rows // 2, block)

    def body(ids, w, mine, theirs, grads, *rest):
        outs, v = rest[:5], rest[5]
        z, x, y, c = ids[0], ids[1], ids[2], ids[3]
        lane = lax.broadcasted_iota(jnp.int32, (part, SPAN), 1)

        def product(cols, k, carry):
            firsts = []
            for given, core, first in ((mine, c, carry[0]), (theirs, 1 - c, carry[1])):
                now = given[:, cols].astype(F32)
                later = jnp.where(lane == SPAN - 1, first, pltpu.roll(now, SPAN - 1, 1))
                at = pl.ds(pl.multiple_of(core * 2 * part, 16), 2 * part)
                grads[at, cols] = jnp.concatenate([later, now], axis=0).astype(BF)
                firsts.append(now[:, :1])
            v[:, cols] = jnp.dot(w[...], grads[:, cols], preferred_element_type=F32)
            return tuple(firsts)

        zero = jnp.zeros((part, 1), F32)
        spans(length, product, (zero, zero), True)
        for step in range(NZ):
            target = mod(z + 1 + step)

            def piece(dx, dy, k=None):
                i = target * 2 + flip(x, dx)
                if channel_pieces:
                    row = pl.multiple_of(flip(y, dy) * rows + i * own, 8)
                    cols = slice(None) if k is None else pl.ds(k * length // 2, length // 2)
                    return v[pl.ds(row, own), cols]
                cols = pl.ds(pl.multiple_of(i * block, block), block)
                row = flip(y, dy) * rows
                if k is None:
                    return v[pl.ds(pl.multiple_of(row, 8), rows), cols]
                return v[pl.ds(pl.multiple_of(row + k * rows // 2, 8), rows // 2), cols]

            outs[0][step] = piece(0, 0)
            outs[1][step] = piece(1, 0)
            outs[2][step] = piece(0, 1)
            outs[3][step] = piece(1, 1, 0).astype(BF)
            outs[4][step] = piece(1, 1, 1).astype(BF)

    made = call(
        body,
        [((total, length), BF), (shape, F32), (shape, F32), (shape, F32), (half, BF), (half, BF)],
        [ids, tall, mine, theirs],
        [pltpu.VMEM((depth, length), F32)],
        after=after,
        flops=2 * depth * total * length,
    )
    return made[0], made[1:]


def weight_blocks(ids, grads, u, after=()):
    total, length = grads.shape
    depth = u.shape[0]
    part, rows = total // 4, depth // 2

    def body(ids, grads, u, *rest):
        outs, made = rest[:NZ], rest[NZ]
        z, x = ids[0], ids[1]
        contract = (((1,), (1,)), ((), ()))
        for y in range(2):
            made[y] = lax.dot_general(
                grads[...], u[pl.ds(y * rows, rows), :], contract, preferred_element_type=F32
            )
        sums = lax.dot_general(jnp.ones((8, length), BF), grads[...], contract, preferred_element_type=F32)
        line = lax.broadcasted_iota(jnp.int32, (8, part), 0)
        tails = []
        for r in range(2):
            bias = jnp.where(flip(x, r) == 0, sums[:, part : 2 * part], sums[:, 3 * part : 4 * part])
            high = bias.astype(BF).astype(F32)
            tail = jnp.where(line == 0, high, jnp.where(line == 1, bias - high, 0.0))
            tails.append(jnp.concatenate([tail, jnp.zeros((8, rows - part), F32)], axis=1))
        for dz in range(NZ):
            source = mod(z - dz)
            both = []
            for r in range(2):
                at = pl.ds(pl.multiple_of((flip(x, r) * 2 + source // 2) * part, 8), part)
                both.append(jnp.concatenate([made[lax.rem(source, 2), at, :], tails[r]], axis=0))
            outs[dz][...] = jnp.concatenate(both, axis=1).astype(BF)

    return call(
        body,
        [((part + 8, 2 * rows), BF)] * NZ,
        [ids, grads, u],
        [pltpu.VMEM((2, total, rows), F32)],
        after=after,
        flops=2 * depth * total * length,
    )


def unpack_weight(ids, groups):
    _, height, width = groups[0].shape
    part, rows = height - 8, width // 2
    own = part // 3
    columns = own * 8

    def body(ids, r0, r1, out, bias, joined):
        z, c = ids[0], ids[3]
        for r, group in enumerate((r0, r1)):
            for pair in range(NZ // 2):
                both = group[pair].astype(F32)
                for k in range(2):
                    i = mod(z + 2 * pair + k) * 2 + flip(c, r)
                    block = both[:, k * rows : (k + 1) * rows]
                    for g in range(3):
                        at = pl.ds(pl.multiple_of(i * own, 8), own)
                        joined[g, at, :] = block[g * own : (g + 1) * own]
                    bias[pl.ds(i, 1), :] = (block[part : part + 1] + block[part + 1 : part + 2])[:, :part]
        for g in range(3):
            out[g] = joined[g].T

    grad, bias = call(
        body,
        [((3, rows, columns), F32), ((8, part), F32)],
        [ids, *groups],
        [pltpu.VMEM((3, columns, rows), F32)],
    )
    bias = jnp.transpose(bias.reshape(8, 3, own), (1, 0, 2)).reshape(3, columns)
    return grad, bias


def back_rounds(ids, parts, blocks, axis, after=()):
    blocks = blocks_over_z(blocks, -1)
    parts = [*parts[:3], over_y(parts[3]), over_x(parts[4])]
    sent_x, sent_y = add_diagonal(ids, parts, axis, after=after)
    groups = regroup_back(ids, blocks)
    *planes, own = add_plane(ids, parts[0], over_x(sent_x), over_y(sent_y), after=groups)
    others = [over_z(plane, step + 1) for step, plane in enumerate(planes)]
    return own, others, blocks_over_x(groups, True)


def owned_channels(inputs, first_weight, first_bias, second_weight, second_bias, cotangent):
    tm, mp = lax.axis_index("tm"), lax.axis_index("mp")
    ids = jnp.stack([tm // 2, tm % 2, mp // 2, mp % 2]).astype(jnp.int32)

    *w1, column_1, u_piece = pack_weight(ids, first_weight, first_bias, inputs[0].T)
    near, w1 = regroup(ids, along_z(u_piece), blocks_over_x(w1))
    from_x, from_y = over_x(near), over_y(near)
    wide_1, tall_1 = join_weight(ids, blocks_over_z(w1, 1))
    cot_here, cot_there = split_cotangent(ids, cotangent[0].T)
    diag = corner(ids, [from_x], [from_y], 0)
    (cot_there,) = relay([cot_there], [diag[0]])
    diag = [over_y(diag[0]), over_x(diag[1])]
    cots = pair_up(ids, cot_here, over_x(cot_there))
    *w2, column_2 = pack_weight(ids, second_weight, second_bias)

    cots = [cots[0]] + [over_z(cots[dz], dz) for dz in range(1, NZ)]
    u, mine, theirs = partial_gates(ids, wide_1, [near], [from_x], [from_y], diag, False, after=[*w2, *cots])
    theirs = over_core(theirs)
    hidden, saved = first_cells(ids, mine, theirs, column_1)

    w2 = blocks_over_x(relay(w2, [hidden]))
    near, w2 = regroup(ids, along_z(hidden), w2)
    from_x, from_y = [over_x(near)], [over_y(near)]
    wide_2, tall_2 = join_weight(ids, blocks_over_z(w2, 1))
    diag = corner(ids, from_x, from_y, 1)
    diag = [over_y(diag[0]), over_x(diag[1])]
    h, mine, theirs = partial_gates(ids, wide_2, [near], from_x, from_y, diag, True)
    outs, gate_grad = second_cells(ids, mine, over_core(theirs), column_2, cots)

    outs = pair_up(ids, outs[0], over_x(outs[1]))
    grads, parts = input_parts(ids, tall_2, gate_grad, over_core(gate_grad), True)
    dw2 = weight_blocks(ids, grads, h[0], after=outs)
    plane, others, dw2 = back_rounds(ids, parts, dw2, 1)
    gate_grad = first_gate_grad(ids, plane, others, saved, after=dw2)

    grads, parts = input_parts(ids, tall_1, gate_grad, over_core(gate_grad), False)
    outs = [outs[0]] + [over_z(outs[dz], dz) for dz in range(1, NZ)]
    dw1 = weight_blocks(ids, grads, u[0], after=outs)
    second_grad, second_bias_grad = unpack_weight(ids, dw2)
    outputs = join_outputs(ids, outs)
    plane, others, dw1 = back_rounds(ids, parts, dw1, 0, [second_grad, outputs])
    input_grad = add_all(ids, plane, others)
    first_grad, first_bias_grad = unpack_weight(ids, dw1)
    first_grad, second_grad = (jnp.transpose(grad, (1, 0, 2)) for grad in (first_grad, second_grad))
    return (
        outputs.T[None],
        input_grad.T[None],
        first_grad,
        first_bias_grad,
        second_grad,
        second_bias_grad,
    )


def prefix(value, axis, join, neutral, backward):
    count, mine = (lax.axis_size(axis), lax.axis_index(axis))
    pieces = jax.tree.map(lambda part: lax.all_gather(part, axis), value)
    if backward:
        pieces = jax.tree.map(lambda part: part[::-1], pieces)
        mine = count - 1 - mine
    total = jax.tree.map(
        lambda part, zero: jnp.full_like(part, 0) + jnp.asarray(zero, part.dtype), value, neutral
    )

    def hop(position, total):
        longer = join(total, jax.tree.map(lambda part: part[position], pieces))
        return jax.tree.map(lambda new, old: jnp.where(position < mine, new, old), longer, total)

    return lax.fori_loop(0, count - 1, hop, total)


def passed_along(array, axis, by):
    size = lax.axis_size(axis)
    pairs = [(i, i + by) for i in range(size) if 0 <= i + by < size]
    return lax.ppermute(array, axis, pairs)


def affine_join(earlier, later):
    return (earlier[0] * later[0], later[0] * earlier[1] + later[1])


def weight_view(gathered):
    return gathered.reshape(2, gathered.shape[0] // 2, gathered.shape[1] * gathered.shape[2])


def span_prefix(product, offset):
    identity = (jnp.ones_like(product), jnp.zeros_like(offset))
    result = prefix((product, offset), "tm", affine_join, identity, False)
    return result[1]


def span_suffix(product, offset):
    identity = (jnp.ones_like(product), jnp.zeros_like(offset))
    result = prefix((product, offset), "tm", affine_join, identity, True)
    return result[1]


def forward_layer(layer_in, view, bias):
    seq_count, length, channels = layer_in.shape
    prev_row = passed_along(layer_in[:, length - 1 :], "tm", 1)
    previous = jnp.concatenate([prev_row, layer_in[:, : length - 1]], axis=1)
    stacked = jnp.stack([previous, layer_in])
    summed = jnp.einsum(
        "jsck,jkn->scn",
        lax.all_gather(stacked, "mp", axis=3, tiled=True),
        view,
        preferred_element_type=jnp.float32,
    )
    gates = summed.reshape(seq_count, length, 3, channels) + bias
    candidate = jnp.tanh(gates[:, :, 0])
    forget = jax.nn.sigmoid(gates[:, :, 1])
    outgate = jax.nn.sigmoid(gates[:, :, 2])
    product, offset = lax.associative_scan(
        affine_join, (forget, (1.0 - forget) * candidate), axis=1
    )
    carry_in = span_prefix(product[:, length - 1], offset[:, length - 1])
    cells = offset + product * carry_in[:, None]
    cells_prev = jnp.concatenate([carry_in[:, None], cells[:, : length - 1]], axis=1)
    return (outgate * cells, (stacked, candidate, forget, outgate, cells, cells_prev))


def backward_layer(grad_in, saved, view):
    stacked, candidate, forget, outgate, cells, cells_prev = saved
    seq_count, length, channels = grad_in.shape
    driven = grad_in * outgate
    next_forget = jnp.concatenate([forget[:, 1:], jnp.ones_like(forget[:, :1])], axis=1)
    reach, local_adj = lax.associative_scan(
        affine_join, (next_forget[:, ::-1], driven[:, ::-1]), axis=1
    )
    reach = reach[:, ::-1]
    local_adj = local_adj[:, ::-1]
    first_forget = forget[:, 0]
    incoming = span_suffix(first_forget * reach[:, 0], first_forget * local_adj[:, 0])
    adjoint = local_adj + reach * incoming[:, None]
    grad_cand = adjoint * (1.0 - forget) * (1.0 - candidate * candidate)
    grad_forget = adjoint * (cells_prev - candidate) * forget * (1.0 - forget)
    grad_outgate = grad_in * cells * outgate * (1.0 - outgate)
    gate_grad = jnp.stack([grad_cand, grad_forget, grad_outgate], axis=2).astype(jnp.bfloat16)
    flat_grad = gate_grad.reshape(seq_count, length, 3 * channels)
    bias_part = jnp.sum(gate_grad, axis=(0, 1), dtype=jnp.float32)
    back_both = jnp.einsum("scn,jkn->jsck", flat_grad, view, preferred_element_type=jnp.float32)
    from_prev = back_both[0]
    from_current = back_both[1]
    local_grad = from_current + jnp.concatenate(
        [from_prev[:, 1:], jnp.zeros_like(from_prev[:, :1])], axis=1
    )
    tail_rows = from_prev[:, :1]
    shard_grad, tail_shard = (
        lax.psum_scatter(local_grad, "mp", scatter_dimension=2, tiled=True),
        lax.psum_scatter(tail_rows, "mp", scatter_dimension=2, tiled=True),
    )
    tail_next = passed_along(tail_shard, "tm", -1)
    layer_grad = shard_grad + jnp.concatenate(
        [jnp.zeros_like(shard_grad[:, : length - 1]), tail_next], axis=1
    )
    weight_full = jnp.einsum(
        "jsck,scn->jkn",
        lax.all_gather(stacked, "mp", axis=3, tiled=True),
        flat_grad,
        preferred_element_type=jnp.float32,
    )
    weight_full = weight_full.reshape(2 * weight_full.shape[1], 3, channels)
    weight_shard = lax.psum_scatter(weight_full, "tm", scatter_dimension=0, tiled=True)
    bias_grad = lax.psum(bias_part, "tm")
    return (layer_grad, weight_shard, bias_grad)


def per_device(inputs, first_weight, first_bias, second_weight, second_bias, cotangent):
    full_first, full_second = (
        lax.all_gather(first_weight, "tm", axis=0, tiled=True),
        lax.all_gather(second_weight, "tm", axis=0, tiled=True),
    )
    view_first = weight_view(full_first)
    view_second = weight_view(full_second)
    hidden_out, saved_first = forward_layer(inputs, view_first, first_bias)
    hidden = hidden_out.astype(jnp.bfloat16)
    top_out, saved_second = forward_layer(hidden, view_second, second_bias)
    again_first, again_second = (
        lax.all_gather(first_weight, "tm", axis=0, tiled=True),
        lax.all_gather(second_weight, "tm", axis=0, tiled=True),
    )
    back_first = weight_view(again_first)
    back_second = weight_view(again_second)
    hidden_grad, second_weightgrad, second_biasgrad = backward_layer(
        cotangent.astype(jnp.float32), saved_second, back_second
    )
    input_grad, first_weightgrad, first_biasgrad = backward_layer(
        hidden_grad, saved_first, back_first
    )
    return (
        top_out.astype(jnp.bfloat16),
        input_grad,
        first_weightgrad,
        first_biasgrad,
        second_weightgrad,
        second_biasgrad,
    )


def choose(owned):
    def run(inputs, first_weight, *rest):
        sizes = inputs.shape[0] == 1 and inputs.shape[1] == 256 and first_weight.shape == (576, 3, 576)
        plan = owned_channels if owned and sizes else per_device
        return plan(inputs, first_weight, *rest)

    return run


def solution(mesh):
    placed = (
        P(None, "tm", "mp"),
        P("tm", None, "mp"),
        P(None, "mp"),
        P("tm", None, "mp"),
        P(None, "mp"),
        P(None, "tm", "mp"),
    )
    owned = mesh.shape["tm"] == 2 * NZ and mesh.shape["mp"] == 4
    return jax.shard_map(
        choose(owned),
        mesh=mesh,
        in_specs=placed,
        out_specs=(
            P(None, "tm", "mp"),
            P(None, "tm", "mp"),
            P("tm", None, "mp"),
            P(None, "mp"),
            P("tm", None, "mp"),
            P(None, "mp"),
        ),
        check_vma=False,
    )
```

```python
import jax
import jax.numpy as jnp
from jax import lax
from jax.experimental import pallas as pl
from jax.experimental.pallas import tpu as pltpu
from jax.sharding import PartitionSpec as P

BF = jnp.bfloat16
F32 = jnp.float32
LANES = 128
SPAN = 512
MIB = 2**20

NZ = 4


def mod(value):
    return lax.rem(value + 2 * NZ, NZ)


def flip(bit, by):
    return bit if by == 0 else 1 - bit


def moved(array, target):
    pairs = []
    for z in range(NZ):
        for x in range(2):
            for y in range(2):
                for c in range(2):
                    tz, tx, ty, tc = target(z, x, y, c)
                    pairs.append(((z * 2 + x) * 4 + y * 2 + c, (tz * 2 + tx) * 4 + ty * 2 + tc))
    return lax.ppermute(array, ("tm", "mp"), pairs)


def over_x(array):
    return moved(array, lambda z, x, y, c: (z, 1 - x, y, c))


def over_y(array):
    return moved(array, lambda z, x, y, c: (z, x, 1 - y, c))


def over_core(array):
    return moved(array, lambda z, x, y, c: (z, x, y, 1 - c))


def over_z(array, by):
    return moved(array, lambda z, x, y, c: ((z + by) % NZ, x, y, c))


def call(body, outs, args, scratch=(), vmem=28, flops=0, after=(), far_in=(), far_out=()):
    whole = pl.BlockSpec(memory_space=pltpu.VMEM)
    anywhere = pl.BlockSpec(memory_space=pl.ANY)
    moved_bytes = sum(a.size * a.dtype.itemsize for at, a in enumerate(args) if at not in far_in)
    for at, (shape, kind) in enumerate(outs):
        size = 0 if at in far_out else jnp.dtype(kind).itemsize
        for extent in shape:
            size *= extent
        moved_bytes += size
    specs = [pl.BlockSpec(memory_space=pltpu.SMEM)]
    specs += [anywhere if at in far_in else whole for at in range(1, len(args))]
    specs += [anywhere] * len(after)
    count = len(args)

    def run(*refs):
        body(*refs[:count], *refs[count + len(after) :])

    return pl.pallas_call(
        run,
        out_shape=[jax.ShapeDtypeStruct(shape, kind) for shape, kind in outs],
        in_specs=specs,
        out_specs=[anywhere if at in far_out else whole for at in range(len(outs))],
        scratch_shapes=list(scratch),
        compiler_params=pltpu.CompilerParams(vmem_limit_bytes=vmem * MIB),
        cost_estimate=pl.CostEstimate(flops=flops, bytes_accessed=moved_bytes, transcendentals=0),
    )(*args, *after)


ROOMY = 42 * 10**6


def roomy(shape, kind):
    size = jnp.dtype(kind).itemsize
    for extent in shape:
        size *= extent
    return ((-(-ROOMY // size),) + shape, kind)


EARLY = 10**11
SOON = 10**10


def relay(arrays, after, flops=0):
    anywhere = pl.BlockSpec(memory_space=pl.ANY)
    count = len(arrays)

    def body(*refs):
        pass

    return pl.pallas_call(
        body,
        out_shape=[jax.ShapeDtypeStruct(array.shape, array.dtype) for array in arrays],
        in_specs=[anywhere] * (count + len(after)),
        out_specs=[anywhere] * count,
        input_output_aliases={at: at for at in range(count)},
        cost_estimate=pl.CostEstimate(flops=flops, bytes_accessed=0, transcendentals=0),
    )(*arrays, *after)


def pack_weight(ids, weight, bias, along=None, after=()):
    rows, gates, columns = weight.shape
    own = columns // 8
    extra = [] if along is None else [along]

    def body(ids, w, bias, *rest):
        outs, column = rest[len(extra) : len(extra) + 2], rest[len(extra) + 2]
        turned, upright = rest[-2:]
        if extra:
            rest[-3][...] = rest[0][...]
        z, x, c = ids[0], ids[1], ids[3]
        mine = pl.ds(pl.multiple_of((z * 2 + x) * own, 8), own)
        for g in range(gates):
            upright[...] = jnp.broadcast_to(bias[g : g + 1, :], (8, columns)).T
            column[pl.ds(g * own, own), :] = upright[mine, :1]

        def turn(g, carry):
            turned[g] = w[g].astype(F32).T
            return carry

        lax.fori_loop(0, gates, turn, 0)
        for r in range(2):
            for pair in range(NZ // 2):
                both = []
                for dz in (2 * pair, 2 * pair + 1):
                    at = pl.ds(pl.multiple_of((mod(z + dz) * 2 + flip(c, r)) * own, 8), own)
                    both.append(jnp.concatenate([turned[g, at, :] for g in range(gates)], axis=0))
                outs[r][pair] = jnp.concatenate(both, axis=1).astype(BF)

    return call(
        body,
        [((NZ // 2, gates * own, 2 * rows), BF)] * 2
        + [((gates * own, 1), F32)]
        + [(a.shape, a.dtype) for a in extra],
        [ids, jnp.transpose(weight, (1, 0, 2)), bias, *extra],
        [pltpu.VMEM((gates, columns, rows), F32), pltpu.VMEM((columns, 8), F32)],
        after=after,
    )


def blocks_over_x(groups, back=False):
    def to(r):
        if back:
            return lambda z, x, y, c: (z, c, y, x ^ r)
        return lambda z, x, y, c: (z, c ^ r, y, x)

    return [moved(groups[r], to(r)) for r in range(2)]


def blocks_over_z(both, sign):
    return [both[0]] + [over_z(both[dz], sign * dz) for dz in range(1, NZ)]


def regroup(ids, pieces, groups, after=()):
    count, wide = len(pieces), len(groups) > 0
    outs = [((count,) + pieces[0].shape, BF)] if count else []
    if wide:
        _, part, width = groups[0].shape
        rows = width // 2
        outs += [((part, width), BF)] * NZ

    def body(ids, *rest):
        ins, given = rest[:count], rest[count : count + len(groups)]
        made = rest[count + len(groups) :]
        for at in range(count):
            made[0][at] = ins[at][...]
        for dz in range(NZ if wide else 0):
            lanes = slice((dz % 2) * rows, (dz % 2 + 1) * rows)
            parts = [group[dz // 2].astype(F32)[:, lanes] for group in given]
            made[-NZ + dz][...] = jnp.concatenate(parts, axis=1).astype(BF)

    made = list(call(body, outs, [ids, *pieces, *groups], after=after))
    return (made[:1] if count else []) + [made[-NZ:]] * wide


def regroup_back(ids, both, after=()):
    part, width = both[0].shape
    rows = width // 2

    def body(ids, *rest):
        ins, outs = rest[:NZ], rest[NZ:]
        for r in range(2):
            lanes = slice(r * rows, (r + 1) * rows)
            for pair in range(NZ // 2):
                parts = [ins[2 * pair + k][...].astype(F32)[:, lanes] for k in range(2)]
                outs[r][pair] = jnp.concatenate(parts, axis=1).astype(BF)

    return call(body, [((NZ // 2, part, width), BF)] * 2, [ids, *both], after=after, flops=EARLY)


def join_weight(ids, blocks):
    part, width = blocks[0].shape
    rows = width // 2

    def body(ids, *rest):
        ins, (wide, tall), joined = rest[:NZ], rest[NZ : NZ + 2], rest[NZ + 2]
        z, x = ids[0], ids[1]
        for dz in range(NZ):
            source = mod(z - dz)
            both = ins[dz][...].astype(F32)
            for r in range(2):
                base = (flip(x, r) * 2 + source // 2) * part
                at = pl.ds(pl.multiple_of(base, 8), part)
                joined[lax.rem(source, 2), at, :] = both[:, r * rows : (r + 1) * rows]
        for half in range(2):
            at = pl.ds(half * 2 * part, 2 * part)
            both = jnp.concatenate([joined[0, at, :], joined[1, at, :]], axis=1)
            wide[at, :] = both.astype(BF)
        for y in range(2):
            tall[pl.ds(y * rows, rows), :] = joined[y].T.astype(BF)

    return call(
        body,
        [((4 * part, 2 * rows), BF), ((2 * rows, 4 * part), BF)],
        [ids, *blocks],
        [pltpu.VMEM((2, 4 * part, rows), F32)],
        flops=EARLY,
    )


def halves(array, axis):
    half = array.shape[axis] // 2
    return lax.slice_in_dim(array, 0, half, axis=axis), lax.slice_in_dim(array, half, 2 * half, axis=axis)


def along_z(piece):
    return [piece] + [over_z(piece, dz) for dz in range(1, NZ)]


def stacked(arrays, rank):
    found = []
    for at, array in enumerate(arrays):
        found += [(at, None)] if len(array.shape) == rank else [(at, k) for k in range(array.shape[0])]
    return found


def corner(ids, from_x, from_y, axis, after=()):
    lists = [stacked(part, 2) for part in (from_x, from_y)]
    piece = from_x[0].shape[-2:]
    half = tuple(extent // 2 if at == axis else extent for at, extent in enumerate(piece))

    def body(ids, *rest):
        ins = rest[: len(from_x)], rest[len(from_x) : -2]
        for k in range(2):
            cut = (slice(None),) * axis + (pl.ds(k * half[axis], half[axis]),)
            for dz, (at, index) in enumerate(lists[k]):
                ref = ins[k][at] if index is None else ins[k][at].at[index]
                rest[-2 + k][dz] = ref[cut]

    return call(body, [((NZ,) + half, BF)] * 2, [ids, *from_x, *from_y], after=after)


def add_diagonal(ids, parts, axis, after=()):
    _, to_x, to_y, at_x, at_y = parts
    half = at_x.shape[axis + 1]

    def body(ids, to_x, to_y, at_x, at_y, out_x, out_y):
        cuts = [(slice(None),) * (axis + 1) + (pl.ds(k * half, half),) for k in range(2)]
        for k, (to, came, out) in enumerate(((to_x, at_x, out_x), (to_y, at_y, out_y))):
            out[cuts[k]] = (to[cuts[k]] + came[...].astype(F32)).astype(BF)
            out[cuts[1 - k]] = to[cuts[1 - k]].astype(BF)

    return call(body, [(to_x.shape, BF)] * 2, [ids, to_x, to_y, at_x, at_y], after=after)


def add_plane(ids, own, from_x, from_y, after=()):
    def body(ids, own, from_x, from_y, *outs):
        for step in range(NZ):
            plane = own[step] + from_x[step].astype(F32) + from_y[step].astype(F32)
            outs[step][...] = plane.astype(outs[step].dtype)

    outs = [(own.shape[1:], BF)] * (NZ - 1) + [(own.shape[1:], F32)]
    return call(body, outs, [ids, own, from_x, from_y], after=after)


def total_of(own, others):
    total = own[...]
    for other in others:
        total = total + other[...].astype(F32)
    return total


def add_all(ids, own, others):
    def body(ids, own, *rest):
        rest[-1][...] = total_of(own, rest[:-1])

    return call(body, [(own.shape, F32)], [ids, own, *others])[0]


def partial_gates(ids, wide, near, from_x, from_y, diagonal, channel_pieces, after=()):
    total, depth = wide.shape
    part = total // 4
    rows = depth // 2
    if channel_pieces:
        own, length = near.shape[-2:]
    else:
        length = near.shape[-1] * 8
    found = [near, from_x, from_y, *diagonal]

    def body(ids, w, *rest):
        ins, (kept, mine, theirs, u, done) = rest[:-5], rest[-5:]
        z, x, y, c = ids[0], ids[1], ids[2], ids[3]

        def lay(dz, carry):
            near, at_x, at_y, diag_a, diag_b = [part.at[dz] for part in ins]
            source = mod(z - dz)
            if channel_pieces:
                half = length // 2
                for other in range(2):
                    row = pl.multiple_of(flip(y, other) * rows + source * 2 * own, 16)
                    for k in range(2):
                        cols = pl.ds(k * half, half)
                        if other:
                            a, b = at_y[:, cols], (diag_a, diag_b)[k][...]
                        else:
                            a, b = near[:, cols], at_x[:, cols]
                        a, b = a.astype(F32), b.astype(F32)
                        pair = jnp.concatenate([jnp.where(x == 0, a, b), jnp.where(x == 0, b, a)], axis=0)
                        u[pl.ds(row, 2 * own), cols] = pair.astype(BF)
            else:
                block = length // 8
                here = pl.ds(pl.multiple_of((source * 2 + x) * block, block), block)
                there = pl.ds(pl.multiple_of((source * 2 + 1 - x) * block, block), block)
                top = pl.multiple_of(y * rows, 16)
                low = pl.multiple_of((1 - y) * rows, 16)
                u[pl.ds(top, rows), here] = near[...]
                u[pl.ds(top, rows), there] = at_x[...]
                u[pl.ds(low, rows), here] = at_y[...]
                u[pl.ds(low, rows // 2), there] = diag_a[...]
                u[pl.ds(pl.multiple_of(low + rows // 2, 16), rows // 2), there] = diag_b[...]
            return carry

        lax.fori_loop(0, NZ, lay, 0)
        keep = pltpu.make_async_copy(u, kept.at[0], done)
        keep.start()
        lane = lax.broadcasted_iota(jnp.int32, (part, SPAN), 1)

        def step(cols, k, carry):
            lasts = []
            for out, core, before in ((mine, c, carry[0]), (theirs, 1 - c, carry[1])):
                rows = pl.ds(pl.multiple_of(core * 2 * part, 16), 2 * part)
                made = jnp.dot(w[rows, :], u[:, cols], preferred_element_type=F32)
                prev = made[:part]
                out[:, cols] = made[part:] + jnp.where(lane == 0, before, pltpu.roll(prev, 1, 1))
                lasts.append(prev[:, SPAN - 1 :])
            return tuple(lasts)

        zero = jnp.zeros((part, 1), F32)
        spans(length, step, (zero, zero))
        keep.wait()

    return call(
        body,
        [roomy((depth, length), BF), ((part, length), F32), ((part, length), F32)],
        [ids, wide, *found],
        [pltpu.VMEM((depth, length), BF), pltpu.SemaphoreType.DMA],
        after=after,
        flops=2 * total * depth * length,
        far_out=(0,),
    )


def spans(length, step, carry, backward=False):
    count = length // SPAN

    def run(n, carry):
        k = count - 1 - n if backward else n
        return step(pl.ds(pl.multiple_of(k * SPAN, SPAN), SPAN), k, carry)

    return lax.fori_loop(0, count, run, carry)


def scan_span(forget, driven, carry, backward):
    own, length = driven.shape
    lane = lax.broadcasted_iota(jnp.int32, (own, LANES), 1)
    blocks = [slice(at, at + LANES) for at in range(0, length, LANES)]
    reach, state = [forget[:, cols] for cols in blocks], [driven[:, cols] for cols in blocks]
    by = 1
    while by < LANES:
        shift = LANES - by if backward else by
        inside = lane < LANES - by if backward else lane >= by
        for at in range(len(blocks)):
            r, s = reach[at], state[at]
            state[at] = s + jnp.where(inside, r * pltpu.roll(s, shift, 1), 0.0)
            reach[at] = jnp.where(inside, r * pltpu.roll(r, shift, 1), r)
        by *= 2
    for at in range(len(blocks))[:: -1 if backward else 1]:
        state[at] = state[at] + reach[at] * carry
        carry = state[at][:, :1] if backward else state[at][:, LANES - 1 :]
    return jnp.concatenate(state, axis=1), carry


def squash(value):
    return 1.0 / (1.0 + jnp.exp(-value))


def forward_scan(mine, theirs, bias, cand, forg, outg, cells, result):
    own, length = cells.shape

    def step(cols, k, carry):
        gates = []
        for g in range(3):
            rows = pl.ds(g * own, own)
            gates.append(mine[rows, cols] + theirs[rows, cols] + bias[rows, :])
        candidate, forget, outgate = jnp.tanh(gates[0]), squash(gates[1]), squash(gates[2])
        state, carry = scan_span(forget, (1.0 - forget) * candidate, carry, False)
        cand[:, cols], forg[:, cols], outg[:, cols], cells[:, cols] = candidate, forget, outgate, state
        result(cols, outgate * state)
        return carry

    spans(length, step, jnp.zeros((own, 1), F32))


def backward_scan(grad_of, cand, forg, outg, cells, gate_grad):
    own, length = cells.shape
    lane = lax.broadcasted_iota(jnp.int32, (own, SPAN), 1)

    def step(cols, k, carry):
        adjoint_after, forget_after = carry
        grad, a, f, o, now = grad_of(cols), cand[:, cols], forg[:, cols], outg[:, cols], cells[:, cols]
        later = jnp.where(lane == SPAN - 1, forget_after, pltpu.roll(f, SPAN - 1, 1))
        adjoint, adjoint_first = scan_span(later, grad * o, adjoint_after, True)
        last = cells[:, pl.ds(pl.multiple_of(jnp.maximum(k * SPAN - LANES, 0), LANES), LANES)][:, LANES - 1 :]
        before = jnp.where(lane == 0, jnp.where(k == 0, 0.0, last), pltpu.roll(now, 1, 1))
        away = 1.0 - f
        gate_grad[:, cols] = jnp.concatenate(
            [
                adjoint * away * (1.0 - a * a),
                adjoint * (before - a) * f * away,
                grad * now * o * (1.0 - o),
            ],
            axis=0,
        ).astype(BF)
        return adjoint_first, f[:, :1]

    zero = jnp.zeros((own, 1), F32)
    spans(length, step, (zero, zero), True)


def first_cells(ids, mine, theirs, bias, after=()):
    part, length = mine.shape
    own = part // 3

    def body(ids, mine, theirs, bias, hidden, kept, *rest):
        made, done = rest[:4], rest[4]

        def result(cols, value):
            hidden[:, cols] = value.astype(BF)

        forward_scan(mine, theirs, bias, *made, result)
        copies = [pltpu.make_async_copy(made[at], kept.at[at], done.at[at]) for at in range(4)]
        for copy in copies:
            copy.start()
        for copy in copies:
            copy.wait()

    return call(
        body,
        [((own, length), BF), roomy((own, length), F32)],
        [ids, mine, theirs, bias],
        [pltpu.VMEM((own, length), F32)] * 4 + [pltpu.SemaphoreType.DMA((4,))],
        after=after,
        far_out=(1,),
    )


def first_gate_grad(ids, own, others, saved, after=()):
    channels, length = own.shape

    def body(ids, own, *rest):
        ins, held, gate_grad = rest[: len(others)], rest[-5:-1], rest[-1]

        def grad_of(cols):
            total = own[:, cols]
            for other in ins:
                total = total + other[:, cols].astype(F32)
            return total

        backward_scan(grad_of, *held, gate_grad)

    args = [ids, own, *others, *[saved[at] for at in range(4)]]
    return call(body, [((3 * channels, length), BF)], args, after=after)[0]


def second_cells(ids, mine, theirs, bias, cot_pieces):
    part, length = mine.shape
    own = part // 3
    block = length // 8

    def body(ids, mine, theirs, bias, *rest):
        cots, outs, gate_grad = rest[:NZ], rest[NZ : NZ + 2], rest[NZ + 2]
        grad, cand, forg, outg, cells, made = rest[NZ + 3 :]
        z, x = ids[0], ids[1]
        for dz in range(NZ):
            for dx in range(2):
                i = mod(z - dz) * 2 + flip(x, dx)
                grad[:, pl.ds(pl.multiple_of(i * block, block), block)] = cots[dz][dx]

        def result(cols, value):
            made[:, cols] = value.astype(BF)

        forward_scan(mine, theirs, bias, cand, forg, outg, cells, result)
        for dz in range(NZ):
            for dx in range(2):
                i = mod(z + dz) * 2 + flip(x, dx)
                outs[dx][dz] = made[:, pl.ds(pl.multiple_of(i * block, block), block)]
        backward_scan(lambda cols: grad[:, cols].astype(F32), cand, forg, outg, cells, gate_grad)

    made = call(
        body,
        [((NZ, own, block), BF)] * 2 + [((part, length), BF)],
        [ids, mine, theirs, bias, *cot_pieces],
        [pltpu.VMEM((own, length), BF)] + [pltpu.VMEM((own, length), F32)] * 4 + [pltpu.VMEM((own, length), BF)],
    )
    return made[:2], made[2]


def split_cotangent(ids, cotangent):
    channels, block = cotangent.shape
    own = channels // 8

    def body(ids, cot, *rest):
        outs, wide = rest[:2], rest[2]
        wide[...] = cot[...].astype(F32)
        for dz in range(NZ):
            for dx in range(2):
                i = mod(ids[0] + dz) * 2 + flip(ids[1], dx)
                outs[dx][dz] = wide[pl.ds(pl.multiple_of(i * own, 8), own), :].astype(BF)

    return call(body, [((NZ, own, block), BF)] * 2, [ids, cotangent], [pltpu.VMEM((channels, block), F32)])


def pair_up(ids, first, second, after=()):
    shape = (2,) + first.shape[1:]

    def body(ids, first, second, *outs):
        for at in range(NZ):
            outs[at][0] = first[at]
            outs[at][1] = second[at]

    return call(body, [(shape, BF)] * NZ, [ids, first, second], after=after)


def join_outputs(ids, pieces):
    _, own, block = pieces[0].shape

    def body(ids, *rest):
        ins, out, wide = rest[:NZ], rest[NZ], rest[NZ + 1]
        for dz in range(NZ):
            for dx in range(2):
                i = mod(ids[0] - dz) * 2 + flip(ids[1], dx)
                wide[pl.ds(pl.multiple_of(i * own, 8), own), :] = ins[dz][dx].astype(F32)
        out[...] = wide[...].astype(BF)

    return call(body, [((8 * own, block), BF)], [ids, *pieces], [pltpu.VMEM((8 * own, block), F32)])[0]


def input_parts(ids, tall, mine, theirs, channel_pieces, after=()):
    depth, total = tall.shape
    part, length = mine.shape
    rows = depth // 2
    own = rows // 8
    block = length // 8
    shape = (NZ, own, length) if channel_pieces else (NZ, rows, block)
    half = (NZ, own, length // 2) if channel_pieces else (NZ, rows // 2, block)

    def body(ids, w, mine, theirs, grads, *rest):
        outs, v = rest[:5], rest[5]
        z, x, y, c = ids[0], ids[1], ids[2], ids[3]
        lane = lax.broadcasted_iota(jnp.int32, (part, SPAN), 1)

        def product(cols, k, carry):
            firsts = []
            for given, core, first in ((mine, c, carry[0]), (theirs, 1 - c, carry[1])):
                now = given[:, cols].astype(F32)
                later = jnp.where(lane == SPAN - 1, first, pltpu.roll(now, SPAN - 1, 1))
                at = pl.ds(pl.multiple_of(core * 2 * part, 16), 2 * part)
                grads[at, cols] = jnp.concatenate([later, now], axis=0).astype(BF)
                firsts.append(now[:, :1])
            v[:, cols] = jnp.dot(w[...], grads[:, cols], preferred_element_type=F32)
            return tuple(firsts)

        zero = jnp.zeros((part, 1), F32)
        spans(length, product, (zero, zero), True)

        def hand_out(step, carry):
            target = mod(z + 1 + step)

            def piece(dx, dy, k=None):
                i = target * 2 + flip(x, dx)
                if channel_pieces:
                    row = pl.multiple_of(flip(y, dy) * rows + i * own, 8)
                    cols = slice(None) if k is None else pl.ds(k * length // 2, length // 2)
                    return v[pl.ds(row, own), cols]
                cols = pl.ds(pl.multiple_of(i * block, block), block)
                row = flip(y, dy) * rows
                if k is None:
                    return v[pl.ds(pl.multiple_of(row, 8), rows), cols]
                return v[pl.ds(pl.multiple_of(row + k * rows // 2, 8), rows // 2), cols]

            outs[0][step] = piece(0, 0)
            outs[1][step] = piece(1, 0)
            outs[2][step] = piece(0, 1)
            outs[3][step] = piece(1, 1, 0).astype(BF)
            outs[4][step] = piece(1, 1, 1).astype(BF)
            return carry

        lax.fori_loop(0, NZ, hand_out, 0)

    made = call(
        body,
        [((total, length), BF), (shape, F32), (shape, F32), (shape, F32), (half, BF), (half, BF)],
        [ids, tall, mine, theirs],
        [pltpu.VMEM((depth, length), F32)],
        after=after,
        flops=2 * depth * total * length,
    )
    return made[0], made[1:]


def weight_blocks(ids, grads, u, after=()):
    total, length = grads.shape
    depth = u.shape[0]
    part, rows = total // 4, depth // 2

    def body(ids, grads, u, *rest):
        outs, made = rest[:NZ], rest[NZ]
        z, x = ids[0], ids[1]
        contract = (((1,), (1,)), ((), ()))

        def product(y, carry):
            at = pl.ds(pl.multiple_of(y * rows, 16), rows)
            made[y] = lax.dot_general(grads[...], u[at, :], contract, preferred_element_type=F32)
            return carry

        lax.fori_loop(0, 2, product, 0)
        sums = lax.dot_general(jnp.ones((8, length), BF), grads[...], contract, preferred_element_type=F32)
        line = lax.broadcasted_iota(jnp.int32, (8, part), 0)
        tails = []
        for r in range(2):
            bias = jnp.where(flip(x, r) == 0, sums[:, part : 2 * part], sums[:, 3 * part : 4 * part])
            high = bias.astype(BF).astype(F32)
            tail = jnp.where(line == 0, high, jnp.where(line == 1, bias - high, 0.0))
            tails.append(jnp.concatenate([tail, jnp.zeros((8, rows - part), F32)], axis=1))
        for dz in range(NZ):
            source = mod(z - dz)
            both = []
            for r in range(2):
                at = pl.ds(pl.multiple_of((flip(x, r) * 2 + source // 2) * part, 8), part)
                both.append(jnp.concatenate([made[lax.rem(source, 2), at, :], tails[r]], axis=0))
            outs[dz][...] = jnp.concatenate(both, axis=1).astype(BF)

    return call(
        body,
        [((part + 8, 2 * rows), BF)] * NZ,
        [ids, grads, u],
        [pltpu.VMEM((2, total, rows), F32)],
        after=after,
        flops=2 * depth * total * length,
    )


def unpack_weight(ids, groups):
    _, height, width = groups[0].shape
    part, rows = height - 8, width // 2
    own = part // 3
    columns = own * 8

    def body(ids, r0, r1, out, bias, joined):
        z, c = ids[0], ids[3]
        for r, group in enumerate((r0, r1)):
            for pair in range(NZ // 2):
                both = group[pair].astype(F32)
                for k in range(2):
                    i = mod(z + 2 * pair + k) * 2 + flip(c, r)
                    block = both[:, k * rows : (k + 1) * rows]
                    for g in range(3):
                        at = pl.ds(pl.multiple_of(i * own, 8), own)
                        joined[g, at, :] = block[g * own : (g + 1) * own]
                    bias[pl.ds(i, 1), :] = (block[part : part + 1] + block[part + 1 : part + 2])[:, :part]

        def turn(g, carry):
            out[g] = joined[g].T
            return carry

        lax.fori_loop(0, 3, turn, 0)

    grad, bias = call(
        body,
        [((3, rows, columns), F32), ((8, part), F32)],
        [ids, *groups],
        [pltpu.VMEM((3, columns, rows), F32)],
    )
    bias = jnp.transpose(bias.reshape(8, 3, own), (1, 0, 2)).reshape(3, columns)
    return grad, bias


def back_rounds(ids, parts, blocks, axis, after=()):
    blocks = blocks_over_z(blocks, -1)
    parts = [*parts[:3], over_y(parts[3]), over_x(parts[4])]
    sent_x, sent_y = add_diagonal(ids, parts, axis, after=after)
    groups = regroup_back(ids, blocks)
    *planes, own = add_plane(ids, parts[0], over_x(sent_x), over_y(sent_y), after=groups)
    others = [over_z(plane, step + 1) for step, plane in enumerate(planes)]
    return own, others, blocks_over_x(groups, True)


def owned_channels(inputs, first_weight, first_bias, second_weight, second_bias, cotangent):
    tm, mp = lax.axis_index("tm"), lax.axis_index("mp")
    ids = jnp.stack([tm // 2, tm % 2, mp // 2, mp % 2]).astype(jnp.int32)

    *w1, column_1 = pack_weight(ids, first_weight, first_bias)
    near, w1 = regroup(ids, along_z(inputs[0].T), blocks_over_x(w1))
    from_x, from_y = over_x(near), over_y(near)
    wide_1, tall_1 = join_weight(ids, blocks_over_z(w1, 1))
    cot_here, cot_there = split_cotangent(ids, cotangent[0].T)
    diag = corner(ids, [from_x], [from_y], 0)
    (cot_there,) = relay([cot_there], [diag[0]])
    diag = [over_y(diag[0]), over_x(diag[1])]
    cots = pair_up(ids, cot_here, over_x(cot_there))
    *w2, column_2 = pack_weight(ids, second_weight, second_bias)

    cots = [cots[0]] + [over_z(cots[dz], dz) for dz in range(1, NZ)]
    u, mine, theirs = partial_gates(ids, wide_1, near, from_x, from_y, diag, False, after=[*w2, *cots])
    theirs = over_core(theirs)
    hidden, saved = first_cells(ids, mine, theirs, column_1)

    w2 = blocks_over_x(relay(w2, [hidden]))
    near, w2 = regroup(ids, along_z(hidden), w2)
    from_x, from_y = [over_x(near)], [over_y(near)]
    wide_2, tall_2 = join_weight(ids, blocks_over_z(w2, 1))
    diag = corner(ids, from_x, from_y, 1)
    diag = [over_y(diag[0]), over_x(diag[1])]
    h, mine, theirs = partial_gates(ids, wide_2, near, *from_x, *from_y, diag, True)
    outs, gate_grad = second_cells(ids, mine, over_core(theirs), column_2, cots)

    grads, parts = input_parts(ids, tall_2, gate_grad, over_core(gate_grad), True)
    outs = pair_up(ids, outs[0], over_x(outs[1]), after=[grads])
    dw2 = weight_blocks(ids, grads, h[0], after=outs)
    plane, others, dw2 = back_rounds(ids, parts, dw2, 1)
    gate_grad = first_gate_grad(ids, plane, others, saved, after=dw2)

    grads, parts = input_parts(ids, tall_1, gate_grad, over_core(gate_grad), False)
    outs = [outs[0]] + [over_z(outs[dz], dz) for dz in range(1, NZ)]
    dw1 = weight_blocks(ids, grads, u[0])
    second_grad, second_bias_grad = unpack_weight(ids, dw2)
    outputs = join_outputs(ids, outs)
    plane, others, dw1 = back_rounds(ids, parts, dw1, 0, [second_grad, outputs])
    input_grad = add_all(ids, plane, others)
    first_grad, first_bias_grad = unpack_weight(ids, dw1)
    first_grad, second_grad = (jnp.transpose(grad, (1, 0, 2)) for grad in (first_grad, second_grad))
    return (
        outputs.T[None],
        input_grad.T[None],
        first_grad,
        first_bias_grad,
        second_grad,
        second_bias_grad,
    )


def prefix(value, axis, join, neutral, backward):
    count, mine = (lax.axis_size(axis), lax.axis_index(axis))
    pieces = jax.tree.map(lambda part: lax.all_gather(part, axis), value)
    if backward:
        pieces = jax.tree.map(lambda part: part[::-1], pieces)
        mine = count - 1 - mine
    total = jax.tree.map(
        lambda part, zero: jnp.full_like(part, 0) + jnp.asarray(zero, part.dtype), value, neutral
    )

    def hop(position, total):
        longer = join(total, jax.tree.map(lambda part: part[position], pieces))
        return jax.tree.map(lambda new, old: jnp.where(position < mine, new, old), longer, total)

    return lax.fori_loop(0, count - 1, hop, total)


def passed_along(array, axis, by):
    size = lax.axis_size(axis)
    pairs = [(i, i + by) for i in range(size) if 0 <= i + by < size]
    return lax.ppermute(array, axis, pairs)


def affine_join(earlier, later):
    return (earlier[0] * later[0], later[0] * earlier[1] + later[1])


def weight_view(gathered):
    return gathered.reshape(2, gathered.shape[0] // 2, gathered.shape[1] * gathered.shape[2])


def span_prefix(product, offset):
    identity = (jnp.ones_like(product), jnp.zeros_like(offset))
    result = prefix((product, offset), "tm", affine_join, identity, False)
    return result[1]


def span_suffix(product, offset):
    identity = (jnp.ones_like(product), jnp.zeros_like(offset))
    result = prefix((product, offset), "tm", affine_join, identity, True)
    return result[1]


def forward_layer(layer_in, view, bias):
    seq_count, length, channels = layer_in.shape
    prev_row = passed_along(layer_in[:, length - 1 :], "tm", 1)
    previous = jnp.concatenate([prev_row, layer_in[:, : length - 1]], axis=1)
    stacked = jnp.stack([previous, layer_in])
    summed = jnp.einsum(
        "jsck,jkn->scn",
        lax.all_gather(stacked, "mp", axis=3, tiled=True),
        view,
        preferred_element_type=jnp.float32,
    )
    gates = summed.reshape(seq_count, length, 3, channels) + bias
    candidate = jnp.tanh(gates[:, :, 0])
    forget = jax.nn.sigmoid(gates[:, :, 1])
    outgate = jax.nn.sigmoid(gates[:, :, 2])
    product, offset = lax.associative_scan(
        affine_join, (forget, (1.0 - forget) * candidate), axis=1
    )
    carry_in = span_prefix(product[:, length - 1], offset[:, length - 1])
    cells = offset + product * carry_in[:, None]
    cells_prev = jnp.concatenate([carry_in[:, None], cells[:, : length - 1]], axis=1)
    return (outgate * cells, (stacked, candidate, forget, outgate, cells, cells_prev))


def backward_layer(grad_in, saved, view):
    stacked, candidate, forget, outgate, cells, cells_prev = saved
    seq_count, length, channels = grad_in.shape
    driven = grad_in * outgate
    next_forget = jnp.concatenate([forget[:, 1:], jnp.ones_like(forget[:, :1])], axis=1)
    reach, local_adj = lax.associative_scan(
        affine_join, (next_forget[:, ::-1], driven[:, ::-1]), axis=1
    )
    reach = reach[:, ::-1]
    local_adj = local_adj[:, ::-1]
    first_forget = forget[:, 0]
    incoming = span_suffix(first_forget * reach[:, 0], first_forget * local_adj[:, 0])
    adjoint = local_adj + reach * incoming[:, None]
    grad_cand = adjoint * (1.0 - forget) * (1.0 - candidate * candidate)
    grad_forget = adjoint * (cells_prev - candidate) * forget * (1.0 - forget)
    grad_outgate = grad_in * cells * outgate * (1.0 - outgate)
    gate_grad = jnp.stack([grad_cand, grad_forget, grad_outgate], axis=2).astype(jnp.bfloat16)
    flat_grad = gate_grad.reshape(seq_count, length, 3 * channels)
    bias_part = jnp.sum(gate_grad, axis=(0, 1), dtype=jnp.float32)
    back_both = jnp.einsum("scn,jkn->jsck", flat_grad, view, preferred_element_type=jnp.float32)
    from_prev = back_both[0]
    from_current = back_both[1]
    local_grad = from_current + jnp.concatenate(
        [from_prev[:, 1:], jnp.zeros_like(from_prev[:, :1])], axis=1
    )
    tail_rows = from_prev[:, :1]
    shard_grad, tail_shard = (
        lax.psum_scatter(local_grad, "mp", scatter_dimension=2, tiled=True),
        lax.psum_scatter(tail_rows, "mp", scatter_dimension=2, tiled=True),
    )
    tail_next = passed_along(tail_shard, "tm", -1)
    layer_grad = shard_grad + jnp.concatenate(
        [jnp.zeros_like(shard_grad[:, : length - 1]), tail_next], axis=1
    )
    weight_full = jnp.einsum(
        "jsck,scn->jkn",
        lax.all_gather(stacked, "mp", axis=3, tiled=True),
        flat_grad,
        preferred_element_type=jnp.float32,
    )
    weight_full = weight_full.reshape(2 * weight_full.shape[1], 3, channels)
    weight_shard = lax.psum_scatter(weight_full, "tm", scatter_dimension=0, tiled=True)
    bias_grad = lax.psum(bias_part, "tm")
    return (layer_grad, weight_shard, bias_grad)


def per_device(inputs, first_weight, first_bias, second_weight, second_bias, cotangent):
    full_first, full_second = (
        lax.all_gather(first_weight, "tm", axis=0, tiled=True),
        lax.all_gather(second_weight, "tm", axis=0, tiled=True),
    )
    view_first = weight_view(full_first)
    view_second = weight_view(full_second)
    hidden_out, saved_first = forward_layer(inputs, view_first, first_bias)
    hidden = hidden_out.astype(jnp.bfloat16)
    top_out, saved_second = forward_layer(hidden, view_second, second_bias)
    again_first, again_second = (
        lax.all_gather(first_weight, "tm", axis=0, tiled=True),
        lax.all_gather(second_weight, "tm", axis=0, tiled=True),
    )
    back_first = weight_view(again_first)
    back_second = weight_view(again_second)
    hidden_grad, second_weightgrad, second_biasgrad = backward_layer(
        cotangent.astype(jnp.float32), saved_second, back_second
    )
    input_grad, first_weightgrad, first_biasgrad = backward_layer(
        hidden_grad, saved_first, back_first
    )
    return (
        top_out.astype(jnp.bfloat16),
        input_grad,
        first_weightgrad,
        first_biasgrad,
        second_weightgrad,
        second_biasgrad,
    )


def choose(owned):
    def run(inputs, first_weight, *rest):
        sizes = inputs.shape[0] == 1 and inputs.shape[1] == 256 and first_weight.shape == (576, 3, 576)
        plan = owned_channels if owned and sizes else per_device
        return plan(inputs, first_weight, *rest)

    return run


def solution(mesh):
    placed = (
        P(None, "tm", "mp"),
        P("tm", None, "mp"),
        P(None, "mp"),
        P("tm", None, "mp"),
        P(None, "mp"),
        P(None, "tm", "mp"),
    )
    owned = mesh.shape["tm"] == 2 * NZ and mesh.shape["mp"] == 4
    return jax.shard_map(
        choose(owned),
        mesh=mesh,
        in_specs=placed,
        out_specs=(
            P(None, "tm", "mp"),
            P(None, "tm", "mp"),
            P("tm", None, "mp"),
            P(None, "mp"),
            P("tm", None, "mp"),
            P(None, "mp"),
        ),
        check_vma=False,
    )
```

```python
import jax
import jax.numpy as jnp
from jax import lax
from jax.experimental import pallas as pl
from jax.experimental.pallas import tpu as pltpu
from jax.sharding import PartitionSpec as P

BF = jnp.bfloat16
F32 = jnp.float32
LANES = 128
SPAN = 512
WIDE = 1024
MIB = 2**20

NZ = 4


def mod(value):
    return lax.rem(value + 2 * NZ, NZ)


def flip(bit, by):
    return bit if by == 0 else 1 - bit


def moved(array, target):
    pairs = []
    for z in range(NZ):
        for x in range(2):
            for y in range(2):
                for c in range(2):
                    tz, tx, ty, tc = target(z, x, y, c)
                    pairs.append(((z * 2 + x) * 4 + y * 2 + c, (tz * 2 + tx) * 4 + ty * 2 + tc))
    return lax.ppermute(array, ("tm", "mp"), pairs)


def over_x(array):
    return moved(array, lambda z, x, y, c: (z, 1 - x, y, c))


def over_y(array):
    return moved(array, lambda z, x, y, c: (z, x, 1 - y, c))


def over_core(array):
    return moved(array, lambda z, x, y, c: (z, x, y, 1 - c))


def over_z(array, by):
    return moved(array, lambda z, x, y, c: ((z + by) % NZ, x, y, c))


def call(body, outs, args, scratch=(), vmem=28, flops=0, after=(), far_in=(), far_out=()):
    whole = pl.BlockSpec(memory_space=pltpu.VMEM)
    anywhere = pl.BlockSpec(memory_space=pl.ANY)
    moved_bytes = sum(a.size * a.dtype.itemsize for at, a in enumerate(args) if at not in far_in)
    for at, (shape, kind) in enumerate(outs):
        size = 0 if at in far_out else jnp.dtype(kind).itemsize
        for extent in shape:
            size *= extent
        moved_bytes += size
    specs = [pl.BlockSpec(memory_space=pltpu.SMEM)]
    specs += [anywhere if at in far_in else whole for at in range(1, len(args))]
    specs += [anywhere] * len(after)
    count = len(args)

    def run(*refs):
        body(*refs[:count], *refs[count + len(after) :])

    return pl.pallas_call(
        run,
        out_shape=[jax.ShapeDtypeStruct(shape, kind) for shape, kind in outs],
        in_specs=specs,
        out_specs=[anywhere if at in far_out else whole for at in range(len(outs))],
        scratch_shapes=list(scratch),
        compiler_params=pltpu.CompilerParams(vmem_limit_bytes=vmem * MIB),
        cost_estimate=pl.CostEstimate(flops=flops, bytes_accessed=moved_bytes, transcendentals=0),
    )(*args, *after)


ROOMY = 42 * 10**6


def roomy(shape, kind):
    size = jnp.dtype(kind).itemsize
    for extent in shape:
        size *= extent
    return ((-(-ROOMY // size),) + shape, kind)


EARLY = 10**11
SOON = 10**10


def relay(arrays, after, flops=0):
    anywhere = pl.BlockSpec(memory_space=pl.ANY)
    count = len(arrays)

    def body(*refs):
        pass

    return pl.pallas_call(
        body,
        out_shape=[jax.ShapeDtypeStruct(array.shape, array.dtype) for array in arrays],
        in_specs=[anywhere] * (count + len(after)),
        out_specs=[anywhere] * count,
        input_output_aliases={at: at for at in range(count)},
        cost_estimate=pl.CostEstimate(flops=flops, bytes_accessed=0, transcendentals=0),
    )(*arrays, *after)


def pack_weight(ids, weight, bias, along=None, after=()):
    rows, gates, columns = weight.shape
    own = columns // 8
    extra = [] if along is None else [along]

    def body(ids, w, bias, *rest):
        outs, column = rest[len(extra) : len(extra) + 2], rest[len(extra) + 2]
        turned, upright = rest[-2:]
        if extra:
            rest[-3][...] = rest[0][...]
        z, x, c = ids[0], ids[1], ids[3]
        mine = pl.ds(pl.multiple_of((z * 2 + x) * own, 8), own)
        for g in range(gates):
            upright[...] = jnp.broadcast_to(bias[g : g + 1, :], (8, columns)).T
            column[pl.ds(g * own, own), :] = upright[mine, :1]

        def turn(g, carry):
            turned[g] = w[g].astype(F32).T
            return carry

        lax.fori_loop(0, gates, turn, 0)
        for r in range(2):
            for pair in range(NZ // 2):
                both = []
                for dz in (2 * pair, 2 * pair + 1):
                    at = pl.ds(pl.multiple_of((mod(z + dz) * 2 + flip(c, r)) * own, 8), own)
                    both.append(jnp.concatenate([turned[g, at, :] for g in range(gates)], axis=0))
                outs[r][pair] = jnp.concatenate(both, axis=1).astype(BF)

    return call(
        body,
        [((NZ // 2, gates * own, 2 * rows), BF)] * 2
        + [((gates * own, 1), F32)]
        + [(a.shape, a.dtype) for a in extra],
        [ids, jnp.transpose(weight, (1, 0, 2)), bias, *extra],
        [pltpu.VMEM((gates, columns, rows), F32), pltpu.VMEM((columns, 8), F32)],
        after=after,
    )


def blocks_over_x(groups, back=False):
    def to(r):
        if back:
            return lambda z, x, y, c: (z, c, y, x ^ r)
        return lambda z, x, y, c: (z, c ^ r, y, x)

    return [moved(groups[r], to(r)) for r in range(2)]


def blocks_over_z(both, sign):
    return [both[0]] + [over_z(both[dz], sign * dz) for dz in range(1, NZ)]


def regroup(ids, pieces, groups, after=()):
    count, wide = len(pieces), len(groups) > 0
    outs = [((count,) + pieces[0].shape, BF)] if count else []
    if wide:
        _, part, width = groups[0].shape
        rows = width // 2
        outs += [((part, width), BF)] * NZ

    def body(ids, *rest):
        ins, given = rest[:count], rest[count : count + len(groups)]
        made = rest[count + len(groups) :]
        for at in range(count):
            made[0][at] = ins[at][...]
        for dz in range(NZ if wide else 0):
            lanes = slice((dz % 2) * rows, (dz % 2 + 1) * rows)
            parts = [group[dz // 2].astype(F32)[:, lanes] for group in given]
            made[-NZ + dz][...] = jnp.concatenate(parts, axis=1).astype(BF)

    made = list(call(body, outs, [ids, *pieces, *groups], after=after))
    return (made[:1] if count else []) + [made[-NZ:]] * wide


def regroup_back(ids, both, after=()):
    part, width = both[0].shape
    rows = width // 2

    def body(ids, *rest):
        ins, outs = rest[:NZ], rest[NZ:]
        for r in range(2):
            lanes = slice(r * rows, (r + 1) * rows)
            for pair in range(NZ // 2):
                parts = [ins[2 * pair + k][...].astype(F32)[:, lanes] for k in range(2)]
                outs[r][pair] = jnp.concatenate(parts, axis=1).astype(BF)

    return call(body, [((NZ // 2, part, width), BF)] * 2, [ids, *both], after=after, flops=EARLY)


def join_weight(ids, blocks):
    part, width = blocks[0].shape
    rows = width // 2

    def body(ids, *rest):
        ins, (wide, tall), joined = rest[:NZ], rest[NZ : NZ + 2], rest[NZ + 2]
        z, x = ids[0], ids[1]
        for dz in range(NZ):
            source = mod(z - dz)
            both = ins[dz][...].astype(F32)
            for r in range(2):
                base = (flip(x, r) * 2 + source // 2) * part
                at = pl.ds(pl.multiple_of(base, 8), part)
                joined[lax.rem(source, 2), at, :] = both[:, r * rows : (r + 1) * rows]
        for half in range(2):
            at = pl.ds(half * 2 * part, 2 * part)
            both = jnp.concatenate([joined[0, at, :], joined[1, at, :]], axis=1)
            wide[at, :] = both.astype(BF)
        for y in range(2):
            tall[pl.ds(y * rows, rows), :] = joined[y].T.astype(BF)

    return call(
        body,
        [((4 * part, 2 * rows), BF), ((2 * rows, 4 * part), BF)],
        [ids, *blocks],
        [pltpu.VMEM((2, 4 * part, rows), F32)],
        flops=EARLY,
    )


def halves(array, axis):
    half = array.shape[axis] // 2
    return lax.slice_in_dim(array, 0, half, axis=axis), lax.slice_in_dim(array, half, 2 * half, axis=axis)


def along_z(piece):
    return [piece] + [over_z(piece, dz) for dz in range(1, NZ)]


def stacked(arrays, rank):
    found = []
    for at, array in enumerate(arrays):
        found += [(at, None)] if len(array.shape) == rank else [(at, k) for k in range(array.shape[0])]
    return found


def corner(ids, from_x, from_y, axis, after=()):
    lists = [stacked(part, 2) for part in (from_x, from_y)]
    piece = from_x[0].shape[-2:]
    half = tuple(extent // 2 if at == axis else extent for at, extent in enumerate(piece))

    def body(ids, *rest):
        ins = rest[: len(from_x)], rest[len(from_x) : -2]
        for k in range(2):
            cut = (slice(None),) * axis + (pl.ds(k * half[axis], half[axis]),)
            for dz, (at, index) in enumerate(lists[k]):
                ref = ins[k][at] if index is None else ins[k][at].at[index]
                rest[-2 + k][dz] = ref[cut]

    return call(body, [((NZ,) + half, BF)] * 2, [ids, *from_x, *from_y], after=after)


def add_diagonal(ids, parts, axis, after=()):
    _, to_x, to_y, at_x, at_y = parts
    half = at_x.shape[axis + 1]

    def body(ids, to_x, to_y, at_x, at_y, out_x, out_y):
        cuts = [(slice(None),) * (axis + 1) + (pl.ds(k * half, half),) for k in range(2)]
        for k, (to, came, out) in enumerate(((to_x, at_x, out_x), (to_y, at_y, out_y))):
            out[cuts[k]] = (to[cuts[k]] + came[...].astype(F32)).astype(BF)
            out[cuts[1 - k]] = to[cuts[1 - k]].astype(BF)

    return call(body, [(to_x.shape, BF)] * 2, [ids, to_x, to_y, at_x, at_y], after=after)


def add_plane(ids, own, from_x, from_y, after=()):
    def body(ids, own, from_x, from_y, *outs):
        for step in range(NZ):
            plane = own[step] + from_x[step].astype(F32) + from_y[step].astype(F32)
            outs[step][...] = plane.astype(outs[step].dtype)

    outs = [(own.shape[1:], BF)] * (NZ - 1) + [(own.shape[1:], F32)]
    return call(body, outs, [ids, own, from_x, from_y], after=after)


def total_of(own, others):
    total = own[...]
    for other in others:
        total = total + other[...].astype(F32)
    return total


def add_all(ids, own, others):
    def body(ids, own, *rest):
        rest[-1][...] = total_of(own, rest[:-1])

    return call(body, [(own.shape, F32)], [ids, own, *others])[0]


def partial_gates(ids, wide, near, from_x, from_y, diagonal, channel_pieces, after=()):
    total, depth = wide.shape
    part = total // 4
    rows = depth // 2
    if channel_pieces:
        own, length = near.shape[-2:]
    else:
        length = near.shape[-1] * 8
    found = [near, from_x, from_y, *diagonal]

    def body(ids, w, *rest):
        ins, (kept, mine, theirs, u, done) = rest[:-5], rest[-5:]
        z, x, y, c = ids[0], ids[1], ids[2], ids[3]

        def lay(dz, carry):
            near, at_x, at_y, diag_a, diag_b = [part.at[dz] for part in ins]
            source = mod(z - dz)
            if channel_pieces:
                half = length // 2
                for other in range(2):
                    row = pl.multiple_of(flip(y, other) * rows + source * 2 * own, 16)
                    for k in range(2):
                        cols = pl.ds(k * half, half)
                        if other:
                            a, b = at_y[:, cols], (diag_a, diag_b)[k][...]
                        else:
                            a, b = near[:, cols], at_x[:, cols]
                        a, b = a.astype(F32), b.astype(F32)
                        pair = jnp.concatenate([jnp.where(x == 0, a, b), jnp.where(x == 0, b, a)], axis=0)
                        u[pl.ds(row, 2 * own), cols] = pair.astype(BF)
            else:
                block = length // 8
                here = pl.ds(pl.multiple_of((source * 2 + x) * block, block), block)
                there = pl.ds(pl.multiple_of((source * 2 + 1 - x) * block, block), block)
                top = pl.multiple_of(y * rows, 16)
                low = pl.multiple_of((1 - y) * rows, 16)
                u[pl.ds(top, rows), here] = near[...]
                u[pl.ds(top, rows), there] = at_x[...]
                u[pl.ds(low, rows), here] = at_y[...]
                u[pl.ds(low, rows // 2), there] = diag_a[...]
                u[pl.ds(pl.multiple_of(low + rows // 2, 16), rows // 2), there] = diag_b[...]
            return carry

        lax.fori_loop(0, NZ, lay, 0)
        keep = pltpu.make_async_copy(u, kept.at[0], done)
        keep.start()
        lane = lax.broadcasted_iota(jnp.int32, (part, WIDE), 1)

        def step(cols, k, carry):
            lasts = []
            for out, core, before in ((mine, c, carry[0]), (theirs, 1 - c, carry[1])):
                rows = pl.ds(pl.multiple_of(core * 2 * part, 16), 2 * part)
                made = jnp.dot(w[rows, :], u[:, cols], preferred_element_type=F32)
                prev = made[:part]
                out[:, cols] = made[part:] + jnp.where(lane == 0, before, pltpu.roll(prev, 1, 1))
                lasts.append(prev[:, WIDE - 1 :])
            return tuple(lasts)

        zero = jnp.zeros((part, 1), F32)
        spans(length, step, (zero, zero), span=WIDE)
        keep.wait()

    return call(
        body,
        [roomy((depth, length), BF), ((part, length), F32), ((part, length), F32)],
        [ids, wide, *found],
        [pltpu.VMEM((depth, length), BF), pltpu.SemaphoreType.DMA],
        after=after,
        flops=2 * total * depth * length,
        far_out=(0,),
    )


def spans(length, step, carry, backward=False, span=SPAN):
    count = length // span

    def run(n, carry):
        k = count - 1 - n if backward else n
        return step(pl.ds(pl.multiple_of(k * span, span), span), k, carry)

    return lax.fori_loop(0, count, run, carry)


def scan_span(forget, driven, carry, backward):
    own, length = driven.shape
    lane = lax.broadcasted_iota(jnp.int32, (own, LANES), 1)
    blocks = [slice(at, at + LANES) for at in range(0, length, LANES)]
    reach, state = [forget[:, cols] for cols in blocks], [driven[:, cols] for cols in blocks]
    by = 1
    while by < LANES:
        shift = LANES - by if backward else by
        inside = lane < LANES - by if backward else lane >= by
        for at in range(len(blocks)):
            r, s = reach[at], state[at]
            state[at] = s + jnp.where(inside, r * pltpu.roll(s, shift, 1), 0.0)
            reach[at] = jnp.where(inside, r * pltpu.roll(r, shift, 1), r)
        by *= 2
    for at in range(len(blocks))[:: -1 if backward else 1]:
        state[at] = state[at] + reach[at] * carry
        carry = state[at][:, :1] if backward else state[at][:, LANES - 1 :]
    return jnp.concatenate(state, axis=1), carry


def squash(value):
    return 1.0 / (1.0 + jnp.exp(-value))


def forward_scan(mine, theirs, bias, cand, forg, outg, cells, result):
    own, length = cells.shape

    def step(cols, k, carry):
        gates = []
        for g in range(3):
            rows = pl.ds(g * own, own)
            gates.append(mine[rows, cols] + theirs[rows, cols] + bias[rows, :])
        candidate, forget, outgate = jnp.tanh(gates[0]), squash(gates[1]), squash(gates[2])
        state, carry = scan_span(forget, (1.0 - forget) * candidate, carry, False)
        cand[:, cols], forg[:, cols], outg[:, cols], cells[:, cols] = candidate, forget, outgate, state
        result(cols, outgate * state)
        return carry

    spans(length, step, jnp.zeros((own, 1), F32))


def backward_scan(grad_of, cand, forg, outg, cells, gate_grad):
    own, length = cells.shape
    lane = lax.broadcasted_iota(jnp.int32, (own, SPAN), 1)

    def step(cols, k, carry):
        adjoint_after, forget_after = carry
        grad, a, f, o, now = grad_of(cols), cand[:, cols], forg[:, cols], outg[:, cols], cells[:, cols]
        later = jnp.where(lane == SPAN - 1, forget_after, pltpu.roll(f, SPAN - 1, 1))
        adjoint, adjoint_first = scan_span(later, grad * o, adjoint_after, True)
        last = cells[:, pl.ds(pl.multiple_of(jnp.maximum(k * SPAN - LANES, 0), LANES), LANES)][:, LANES - 1 :]
        before = jnp.where(lane == 0, jnp.where(k == 0, 0.0, last), pltpu.roll(now, 1, 1))
        away = 1.0 - f
        gate_grad[:, cols] = jnp.concatenate(
            [
                adjoint * away * (1.0 - a * a),
                adjoint * (before - a) * f * away,
                grad * now * o * (1.0 - o),
            ],
            axis=0,
        ).astype(BF)
        return adjoint_first, f[:, :1]

    zero = jnp.zeros((own, 1), F32)
    spans(length, step, (zero, zero), True)


def first_cells(ids, mine, theirs, bias, after=()):
    part, length = mine.shape
    own = part // 3

    def body(ids, mine, theirs, bias, hidden, kept, *rest):
        made, done = rest[:4], rest[4]

        def result(cols, value):
            hidden[:, cols] = value.astype(BF)

        forward_scan(mine, theirs, bias, *made, result)
        copies = [pltpu.make_async_copy(made[at], kept.at[at], done.at[at]) for at in range(4)]
        for copy in copies:
            copy.start()
        for copy in copies:
            copy.wait()

    return call(
        body,
        [((own, length), BF), roomy((own, length), F32)],
        [ids, mine, theirs, bias],
        [pltpu.VMEM((own, length), F32)] * 4 + [pltpu.SemaphoreType.DMA((4,))],
        after=after,
        far_out=(1,),
    )


def first_gate_grad(ids, own, others, saved, after=()):
    channels, length = own.shape

    def body(ids, own, *rest):
        ins, held, gate_grad = rest[: len(others)], rest[-5:-1], rest[-1]

        def grad_of(cols):
            total = own[:, cols]
            for other in ins:
                total = total + other[:, cols].astype(F32)
            return total

        backward_scan(grad_of, *held, gate_grad)

    args = [ids, own, *others, *[saved[at] for at in range(4)]]
    return call(body, [((3 * channels, length), BF)], args, after=after)[0]


def second_cells(ids, mine, theirs, bias, cot_pieces):
    part, length = mine.shape
    own = part // 3
    block = length // 8

    def body(ids, mine, theirs, bias, *rest):
        cots, outs, gate_grad = rest[:NZ], rest[NZ : NZ + 2], rest[NZ + 2]
        grad, cand, forg, outg, cells, made = rest[NZ + 3 :]
        z, x = ids[0], ids[1]
        for dz in range(NZ):
            for dx in range(2):
                i = mod(z - dz) * 2 + flip(x, dx)
                grad[:, pl.ds(pl.multiple_of(i * block, block), block)] = cots[dz][dx]

        def result(cols, value):
            made[:, cols] = value.astype(BF)

        forward_scan(mine, theirs, bias, cand, forg, outg, cells, result)
        for dz in range(NZ):
            for dx in range(2):
                i = mod(z + dz) * 2 + flip(x, dx)
                outs[dx][dz] = made[:, pl.ds(pl.multiple_of(i * block, block), block)]
        backward_scan(lambda cols: grad[:, cols].astype(F32), cand, forg, outg, cells, gate_grad)

    made = call(
        body,
        [((NZ, own, block), BF)] * 2 + [((part, length), BF)],
        [ids, mine, theirs, bias, *cot_pieces],
        [pltpu.VMEM((own, length), BF)] + [pltpu.VMEM((own, length), F32)] * 4 + [pltpu.VMEM((own, length), BF)],
    )
    return made[:2], made[2]


def split_cotangent(ids, cotangent):
    channels, block = cotangent.shape
    own = channels // 8

    def body(ids, cot, *rest):
        outs, wide = rest[:2], rest[2]
        wide[...] = cot[...].astype(F32)
        for dz in range(NZ):
            for dx in range(2):
                i = mod(ids[0] + dz) * 2 + flip(ids[1], dx)
                outs[dx][dz] = wide[pl.ds(pl.multiple_of(i * own, 8), own), :].astype(BF)

    return call(body, [((NZ, own, block), BF)] * 2, [ids, cotangent], [pltpu.VMEM((channels, block), F32)])


def pair_up(ids, first, second, after=()):
    shape = (2,) + first.shape[1:]

    def body(ids, first, second, *outs):
        for at in range(NZ):
            outs[at][0] = first[at]
            outs[at][1] = second[at]

    return call(body, [(shape, BF)] * NZ, [ids, first, second], after=after)


def join_outputs(ids, pieces):
    _, own, block = pieces[0].shape

    def body(ids, *rest):
        ins, out, wide = rest[:NZ], rest[NZ], rest[NZ + 1]
        for dz in range(NZ):
            for dx in range(2):
                i = mod(ids[0] - dz) * 2 + flip(ids[1], dx)
                wide[pl.ds(pl.multiple_of(i * own, 8), own), :] = ins[dz][dx].astype(F32)
        out[...] = wide[...].astype(BF)

    return call(body, [((8 * own, block), BF)], [ids, *pieces], [pltpu.VMEM((8 * own, block), F32)])[0]


def input_parts(ids, tall, mine, theirs, channel_pieces, after=()):
    depth, total = tall.shape
    part, length = mine.shape
    rows = depth // 2
    own = rows // 8
    block = length // 8
    shape = (NZ, own, length) if channel_pieces else (NZ, rows, block)
    half = (NZ, own, length // 2) if channel_pieces else (NZ, rows // 2, block)

    def body(ids, w, mine, theirs, grads, *rest):
        outs, v = rest[:5], rest[5]
        z, x, y, c = ids[0], ids[1], ids[2], ids[3]
        lane = lax.broadcasted_iota(jnp.int32, (part, WIDE), 1)

        def product(cols, k, carry):
            firsts = []
            for given, core, first in ((mine, c, carry[0]), (theirs, 1 - c, carry[1])):
                now = given[:, cols].astype(F32)
                later = jnp.where(lane == WIDE - 1, first, pltpu.roll(now, WIDE - 1, 1))
                at = pl.ds(pl.multiple_of(core * 2 * part, 16), 2 * part)
                grads[at, cols] = jnp.concatenate([later, now], axis=0).astype(BF)
                firsts.append(now[:, :1])
            v[:, cols] = jnp.dot(w[...], grads[:, cols], preferred_element_type=F32)
            return tuple(firsts)

        zero = jnp.zeros((part, 1), F32)
        spans(length, product, (zero, zero), True, WIDE)

        def hand_out(step, carry):
            target = mod(z + 1 + step)

            def piece(dx, dy, k=None):
                i = target * 2 + flip(x, dx)
                if channel_pieces:
                    row = pl.multiple_of(flip(y, dy) * rows + i * own, 8)
                    cols = slice(None) if k is None else pl.ds(k * length // 2, length // 2)
                    return v[pl.ds(row, own), cols]
                cols = pl.ds(pl.multiple_of(i * block, block), block)
                row = flip(y, dy) * rows
                if k is None:
                    return v[pl.ds(pl.multiple_of(row, 8), rows), cols]
                return v[pl.ds(pl.multiple_of(row + k * rows // 2, 8), rows // 2), cols]

            outs[0][step] = piece(0, 0)
            outs[1][step] = piece(1, 0)
            outs[2][step] = piece(0, 1)
            outs[3][step] = piece(1, 1, 0).astype(BF)
            outs[4][step] = piece(1, 1, 1).astype(BF)
            return carry

        lax.fori_loop(0, NZ, hand_out, 0)

    made = call(
        body,
        [((total, length), BF), (shape, F32), (shape, F32), (shape, F32), (half, BF), (half, BF)],
        [ids, tall, mine, theirs],
        [pltpu.VMEM((depth, length), F32)],
        after=after,
        flops=2 * depth * total * length,
    )
    return made[0], made[1:]


def weight_blocks(ids, grads, u, after=()):
    total, length = grads.shape
    depth = u.shape[0]
    part, rows = total // 4, depth // 2

    def body(ids, grads, u, *rest):
        outs, made = rest[:NZ], rest[NZ]
        z, x = ids[0], ids[1]
        contract = (((1,), (1,)), ((), ()))

        def product(y, carry):
            at = pl.ds(pl.multiple_of(y * rows, 16), rows)
            made[y] = lax.dot_general(grads[...], u[at, :], contract, preferred_element_type=F32)
            return carry

        lax.fori_loop(0, 2, product, 0)
        sums = lax.dot_general(jnp.ones((8, length), BF), grads[...], contract, preferred_element_type=F32)
        line = lax.broadcasted_iota(jnp.int32, (8, part), 0)
        tails = []
        for r in range(2):
            bias = jnp.where(flip(x, r) == 0, sums[:, part : 2 * part], sums[:, 3 * part : 4 * part])
            high = bias.astype(BF).astype(F32)
            tail = jnp.where(line == 0, high, jnp.where(line == 1, bias - high, 0.0))
            tails.append(jnp.concatenate([tail, jnp.zeros((8, rows - part), F32)], axis=1))
        for dz in range(NZ):
            source = mod(z - dz)
            both = []
            for r in range(2):
                at = pl.ds(pl.multiple_of((flip(x, r) * 2 + source // 2) * part, 8), part)
                both.append(jnp.concatenate([made[lax.rem(source, 2), at, :], tails[r]], axis=0))
            outs[dz][...] = jnp.concatenate(both, axis=1).astype(BF)

    return call(
        body,
        [((part + 8, 2 * rows), BF)] * NZ,
        [ids, grads, u],
        [pltpu.VMEM((2, total, rows), F32)],
        after=after,
        flops=2 * depth * total * length,
    )


def unpack_weight(ids, groups):
    _, height, width = groups[0].shape
    part, rows = height - 8, width // 2
    own = part // 3
    columns = own * 8

    def body(ids, r0, r1, out, bias, joined):
        z, c = ids[0], ids[3]
        for r, group in enumerate((r0, r1)):
            for pair in range(NZ // 2):
                both = group[pair].astype(F32)
                for k in range(2):
                    i = mod(z + 2 * pair + k) * 2 + flip(c, r)
                    block = both[:, k * rows : (k + 1) * rows]
                    for g in range(3):
                        at = pl.ds(pl.multiple_of(i * own, 8), own)
                        joined[g, at, :] = block[g * own : (g + 1) * own]
                    bias[pl.ds(i, 1), :] = (block[part : part + 1] + block[part + 1 : part + 2])[:, :part]

        def turn(g, carry):
            out[g] = joined[g].T
            return carry

        lax.fori_loop(0, 3, turn, 0)

    grad, bias = call(
        body,
        [((3, rows, columns), F32), ((8, part), F32)],
        [ids, *groups],
        [pltpu.VMEM((3, columns, rows), F32)],
    )
    bias = jnp.transpose(bias.reshape(8, 3, own), (1, 0, 2)).reshape(3, columns)
    return grad, bias


def back_rounds(ids, parts, blocks, axis, after=()):
    blocks = blocks_over_z(blocks, -1)
    parts = [*parts[:3], over_y(parts[3]), over_x(parts[4])]
    sent_x, sent_y = add_diagonal(ids, parts, axis, after=after)
    groups = regroup_back(ids, blocks)
    *planes, own = add_plane(ids, parts[0], over_x(sent_x), over_y(sent_y), after=groups)
    others = [over_z(plane, step + 1) for step, plane in enumerate(planes)]
    return own, others, blocks_over_x(groups, True)


def owned_channels(inputs, first_weight, first_bias, second_weight, second_bias, cotangent):
    tm, mp = lax.axis_index("tm"), lax.axis_index("mp")
    ids = jnp.stack([tm // 2, tm % 2, mp // 2, mp % 2]).astype(jnp.int32)

    *w1, column_1 = pack_weight(ids, first_weight, first_bias)
    near, w1 = regroup(ids, along_z(inputs[0].T), blocks_over_x(w1))
    from_x, from_y = over_x(near), over_y(near)
    wide_1, tall_1 = join_weight(ids, blocks_over_z(w1, 1))
    cot_here, cot_there = split_cotangent(ids, cotangent[0].T)
    diag = corner(ids, [from_x], [from_y], 0)
    (cot_there,) = relay([cot_there], [diag[0]])
    diag = [over_y(diag[0]), over_x(diag[1])]
    cots = pair_up(ids, cot_here, over_x(cot_there))
    *w2, column_2 = pack_weight(ids, second_weight, second_bias)

    cots = [cots[0]] + [over_z(cots[dz], dz) for dz in range(1, NZ)]
    u, mine, theirs = partial_gates(ids, wide_1, near, from_x, from_y, diag, False, after=[*w2, *cots])
    theirs = over_core(theirs)
    hidden, saved = first_cells(ids, mine, theirs, column_1)

    w2 = blocks_over_x(relay(w2, [hidden]))
    near, w2 = regroup(ids, along_z(hidden), w2)
    from_x, from_y = [over_x(near)], [over_y(near)]
    wide_2, tall_2 = join_weight(ids, blocks_over_z(w2, 1))
    diag = corner(ids, from_x, from_y, 1)
    diag = [over_y(diag[0]), over_x(diag[1])]
    h, mine, theirs = partial_gates(ids, wide_2, near, *from_x, *from_y, diag, True)
    outs, gate_grad = second_cells(ids, mine, over_core(theirs), column_2, cots)

    grads, parts = input_parts(ids, tall_2, gate_grad, over_core(gate_grad), True)
    outs = pair_up(ids, outs[0], over_x(outs[1]), after=[grads])
    dw2 = weight_blocks(ids, grads, h[0], after=outs)
    plane, others, dw2 = back_rounds(ids, parts, dw2, 1)
    gate_grad = first_gate_grad(ids, plane, others, saved, after=dw2)

    grads, parts = input_parts(ids, tall_1, gate_grad, over_core(gate_grad), False)
    outs = [outs[0]] + [over_z(outs[dz], dz) for dz in range(1, NZ)]
    dw1 = weight_blocks(ids, grads, u[0])
    second_grad, second_bias_grad = unpack_weight(ids, dw2)
    outputs = join_outputs(ids, outs)
    plane, others, dw1 = back_rounds(ids, parts, dw1, 0, [second_grad, outputs])
    input_grad = add_all(ids, plane, others)
    first_grad, first_bias_grad = unpack_weight(ids, dw1)
    first_grad, second_grad = (jnp.transpose(grad, (1, 0, 2)) for grad in (first_grad, second_grad))
    return (
        outputs.T[None],
        input_grad.T[None],
        first_grad,
        first_bias_grad,
        second_grad,
        second_bias_grad,
    )


def prefix(value, axis, join, neutral, backward):
    count, mine = (lax.axis_size(axis), lax.axis_index(axis))
    pieces = jax.tree.map(lambda part: lax.all_gather(part, axis), value)
    if backward:
        pieces = jax.tree.map(lambda part: part[::-1], pieces)
        mine = count - 1 - mine
    total = jax.tree.map(
        lambda part, zero: jnp.full_like(part, 0) + jnp.asarray(zero, part.dtype), value, neutral
    )

    def hop(position, total):
        longer = join(total, jax.tree.map(lambda part: part[position], pieces))
        return jax.tree.map(lambda new, old: jnp.where(position < mine, new, old), longer, total)

    return lax.fori_loop(0, count - 1, hop, total)


def passed_along(array, axis, by):
    size = lax.axis_size(axis)
    pairs = [(i, i + by) for i in range(size) if 0 <= i + by < size]
    return lax.ppermute(array, axis, pairs)


def affine_join(earlier, later):
    return (earlier[0] * later[0], later[0] * earlier[1] + later[1])


def weight_view(gathered):
    return gathered.reshape(2, gathered.shape[0] // 2, gathered.shape[1] * gathered.shape[2])


def span_prefix(product, offset):
    identity = (jnp.ones_like(product), jnp.zeros_like(offset))
    result = prefix((product, offset), "tm", affine_join, identity, False)
    return result[1]


def span_suffix(product, offset):
    identity = (jnp.ones_like(product), jnp.zeros_like(offset))
    result = prefix((product, offset), "tm", affine_join, identity, True)
    return result[1]


def forward_layer(layer_in, view, bias):
    seq_count, length, channels = layer_in.shape
    prev_row = passed_along(layer_in[:, length - 1 :], "tm", 1)
    previous = jnp.concatenate([prev_row, layer_in[:, : length - 1]], axis=1)
    stacked = jnp.stack([previous, layer_in])
    summed = jnp.einsum(
        "jsck,jkn->scn",
        lax.all_gather(stacked, "mp", axis=3, tiled=True),
        view,
        preferred_element_type=jnp.float32,
    )
    gates = summed.reshape(seq_count, length, 3, channels) + bias
    candidate = jnp.tanh(gates[:, :, 0])
    forget = jax.nn.sigmoid(gates[:, :, 1])
    outgate = jax.nn.sigmoid(gates[:, :, 2])
    product, offset = lax.associative_scan(
        affine_join, (forget, (1.0 - forget) * candidate), axis=1
    )
    carry_in = span_prefix(product[:, length - 1], offset[:, length - 1])
    cells = offset + product * carry_in[:, None]
    cells_prev = jnp.concatenate([carry_in[:, None], cells[:, : length - 1]], axis=1)
    return (outgate * cells, (stacked, candidate, forget, outgate, cells, cells_prev))


def backward_layer(grad_in, saved, view):
    stacked, candidate, forget, outgate, cells, cells_prev = saved
    seq_count, length, channels = grad_in.shape
    driven = grad_in * outgate
    next_forget = jnp.concatenate([forget[:, 1:], jnp.ones_like(forget[:, :1])], axis=1)
    reach, local_adj = lax.associative_scan(
        affine_join, (next_forget[:, ::-1], driven[:, ::-1]), axis=1
    )
    reach = reach[:, ::-1]
    local_adj = local_adj[:, ::-1]
    first_forget = forget[:, 0]
    incoming = span_suffix(first_forget * reach[:, 0], first_forget * local_adj[:, 0])
    adjoint = local_adj + reach * incoming[:, None]
    grad_cand = adjoint * (1.0 - forget) * (1.0 - candidate * candidate)
    grad_forget = adjoint * (cells_prev - candidate) * forget * (1.0 - forget)
    grad_outgate = grad_in * cells * outgate * (1.0 - outgate)
    gate_grad = jnp.stack([grad_cand, grad_forget, grad_outgate], axis=2).astype(jnp.bfloat16)
    flat_grad = gate_grad.reshape(seq_count, length, 3 * channels)
    bias_part = jnp.sum(gate_grad, axis=(0, 1), dtype=jnp.float32)
    back_both = jnp.einsum("scn,jkn->jsck", flat_grad, view, preferred_element_type=jnp.float32)
    from_prev = back_both[0]
    from_current = back_both[1]
    local_grad = from_current + jnp.concatenate(
        [from_prev[:, 1:], jnp.zeros_like(from_prev[:, :1])], axis=1
    )
    tail_rows = from_prev[:, :1]
    shard_grad, tail_shard = (
        lax.psum_scatter(local_grad, "mp", scatter_dimension=2, tiled=True),
        lax.psum_scatter(tail_rows, "mp", scatter_dimension=2, tiled=True),
    )
    tail_next = passed_along(tail_shard, "tm", -1)
    layer_grad = shard_grad + jnp.concatenate(
        [jnp.zeros_like(shard_grad[:, : length - 1]), tail_next], axis=1
    )
    weight_full = jnp.einsum(
        "jsck,scn->jkn",
        lax.all_gather(stacked, "mp", axis=3, tiled=True),
        flat_grad,
        preferred_element_type=jnp.float32,
    )
    weight_full = weight_full.reshape(2 * weight_full.shape[1], 3, channels)
    weight_shard = lax.psum_scatter(weight_full, "tm", scatter_dimension=0, tiled=True)
    bias_grad = lax.psum(bias_part, "tm")
    return (layer_grad, weight_shard, bias_grad)


def per_device(inputs, first_weight, first_bias, second_weight, second_bias, cotangent):
    full_first, full_second = (
        lax.all_gather(first_weight, "tm", axis=0, tiled=True),
        lax.all_gather(second_weight, "tm", axis=0, tiled=True),
    )
    view_first = weight_view(full_first)
    view_second = weight_view(full_second)
    hidden_out, saved_first = forward_layer(inputs, view_first, first_bias)
    hidden = hidden_out.astype(jnp.bfloat16)
    top_out, saved_second = forward_layer(hidden, view_second, second_bias)
    again_first, again_second = (
        lax.all_gather(first_weight, "tm", axis=0, tiled=True),
        lax.all_gather(second_weight, "tm", axis=0, tiled=True),
    )
    back_first = weight_view(again_first)
    back_second = weight_view(again_second)
    hidden_grad, second_weightgrad, second_biasgrad = backward_layer(
        cotangent.astype(jnp.float32), saved_second, back_second
    )
    input_grad, first_weightgrad, first_biasgrad = backward_layer(
        hidden_grad, saved_first, back_first
    )
    return (
        top_out.astype(jnp.bfloat16),
        input_grad,
        first_weightgrad,
        first_biasgrad,
        second_weightgrad,
        second_biasgrad,
    )


def choose(owned):
    def run(inputs, first_weight, *rest):
        sizes = inputs.shape[0] == 1 and inputs.shape[1] == 256 and first_weight.shape == (576, 3, 576)
        plan = owned_channels if owned and sizes else per_device
        return plan(inputs, first_weight, *rest)

    return run


def solution(mesh):
    placed = (
        P(None, "tm", "mp"),
        P("tm", None, "mp"),
        P(None, "mp"),
        P("tm", None, "mp"),
        P(None, "mp"),
        P(None, "tm", "mp"),
    )
    owned = mesh.shape["tm"] == 2 * NZ and mesh.shape["mp"] == 4
    return jax.shard_map(
        choose(owned),
        mesh=mesh,
        in_specs=placed,
        out_specs=(
            P(None, "tm", "mp"),
            P(None, "tm", "mp"),
            P("tm", None, "mp"),
            P(None, "mp"),
            P("tm", None, "mp"),
            P(None, "mp"),
        ),
        check_vma=False,
    )
```

```python
import jax
import jax.numpy as jnp
from jax import lax
from jax.experimental import pallas as pl
from jax.experimental.pallas import tpu as pltpu
from jax.sharding import PartitionSpec as P

BF = jnp.bfloat16
F32 = jnp.float32
LANES = 128
SPAN = 512
WIDE = 2048
MIB = 2**20

NZ = 4


def mod(value):
    return lax.rem(value + 2 * NZ, NZ)


def flip(bit, by):
    return bit if by == 0 else 1 - bit


def moved(array, target):
    pairs = []
    for z in range(NZ):
        for x in range(2):
            for y in range(2):
                for c in range(2):
                    tz, tx, ty, tc = target(z, x, y, c)
                    pairs.append(((z * 2 + x) * 4 + y * 2 + c, (tz * 2 + tx) * 4 + ty * 2 + tc))
    return lax.ppermute(array, ("tm", "mp"), pairs)


def over_x(array):
    return moved(array, lambda z, x, y, c: (z, 1 - x, y, c))


def over_y(array):
    return moved(array, lambda z, x, y, c: (z, x, 1 - y, c))


def over_core(array):
    return moved(array, lambda z, x, y, c: (z, x, y, 1 - c))


def over_z(array, by):
    return moved(array, lambda z, x, y, c: ((z + by) % NZ, x, y, c))


def call(body, outs, args, scratch=(), vmem=28, flops=0, after=(), far_in=(), far_out=()):
    whole = pl.BlockSpec(memory_space=pltpu.VMEM)
    anywhere = pl.BlockSpec(memory_space=pl.ANY)
    moved_bytes = sum(a.size * a.dtype.itemsize for at, a in enumerate(args) if at not in far_in)
    for at, (shape, kind) in enumerate(outs):
        size = 0 if at in far_out else jnp.dtype(kind).itemsize
        for extent in shape:
            size *= extent
        moved_bytes += size
    specs = [pl.BlockSpec(memory_space=pltpu.SMEM)]
    specs += [anywhere if at in far_in else whole for at in range(1, len(args))]
    specs += [anywhere] * len(after)
    count = len(args)

    def run(*refs):
        body(*refs[:count], *refs[count + len(after) :])

    return pl.pallas_call(
        run,
        out_shape=[jax.ShapeDtypeStruct(shape, kind) for shape, kind in outs],
        in_specs=specs,
        out_specs=[anywhere if at in far_out else whole for at in range(len(outs))],
        scratch_shapes=list(scratch),
        compiler_params=pltpu.CompilerParams(vmem_limit_bytes=vmem * MIB),
        cost_estimate=pl.CostEstimate(flops=flops, bytes_accessed=moved_bytes, transcendentals=0),
    )(*args, *after)


ROOMY = 42 * 10**6


def roomy(shape, kind):
    size = jnp.dtype(kind).itemsize
    for extent in shape:
        size *= extent
    return ((-(-ROOMY // size),) + shape, kind)


EARLY = 10**11
SOON = 10**10


def relay(arrays, after, flops=0):
    anywhere = pl.BlockSpec(memory_space=pl.ANY)
    count = len(arrays)

    def body(*refs):
        pass

    return pl.pallas_call(
        body,
        out_shape=[jax.ShapeDtypeStruct(array.shape, array.dtype) for array in arrays],
        in_specs=[anywhere] * (count + len(after)),
        out_specs=[anywhere] * count,
        input_output_aliases={at: at for at in range(count)},
        cost_estimate=pl.CostEstimate(flops=flops, bytes_accessed=0, transcendentals=0),
    )(*arrays, *after)


def pack_weight(ids, weight, bias, along=None, after=()):
    rows, gates, columns = weight.shape
    own = columns // 8
    extra = [] if along is None else [along]

    def body(ids, w, bias, *rest):
        outs, column = rest[len(extra) : len(extra) + 2], rest[len(extra) + 2]
        turned, upright = rest[-2:]
        if extra:
            rest[-3][...] = rest[0][...]
        z, x, c = ids[0], ids[1], ids[3]
        mine = pl.ds(pl.multiple_of((z * 2 + x) * own, 8), own)
        for g in range(gates):
            upright[...] = jnp.broadcast_to(bias[g : g + 1, :], (8, columns)).T
            column[pl.ds(g * own, own), :] = upright[mine, :1]

        def turn(g, carry):
            turned[g] = w[g].astype(F32).T
            return carry

        lax.fori_loop(0, gates, turn, 0)
        for r in range(2):
            for pair in range(NZ // 2):
                both = []
                for dz in (2 * pair, 2 * pair + 1):
                    at = pl.ds(pl.multiple_of((mod(z + dz) * 2 + flip(c, r)) * own, 8), own)
                    both.append(jnp.concatenate([turned[g, at, :] for g in range(gates)], axis=0))
                outs[r][pair] = jnp.concatenate(both, axis=1).astype(BF)

    return call(
        body,
        [((NZ // 2, gates * own, 2 * rows), BF)] * 2
        + [((gates * own, 1), F32)]
        + [(a.shape, a.dtype) for a in extra],
        [ids, jnp.transpose(weight, (1, 0, 2)), bias, *extra],
        [pltpu.VMEM((gates, columns, rows), F32), pltpu.VMEM((columns, 8), F32)],
        after=after,
    )


def blocks_over_x(groups, back=False):
    def to(r):
        if back:
            return lambda z, x, y, c: (z, c, y, x ^ r)
        return lambda z, x, y, c: (z, c ^ r, y, x)

    return [moved(groups[r], to(r)) for r in range(2)]


def blocks_over_z(both, sign):
    return [both[0]] + [over_z(both[dz], sign * dz) for dz in range(1, NZ)]


def regroup(ids, pieces, groups, after=()):
    count, wide = len(pieces), len(groups) > 0
    outs = [((count,) + pieces[0].shape, BF)] if count else []
    if wide:
        _, part, width = groups[0].shape
        rows = width // 2
        outs += [((part, width), BF)] * NZ

    def body(ids, *rest):
        ins, given = rest[:count], rest[count : count + len(groups)]
        made = rest[count + len(groups) :]
        for at in range(count):
            made[0][at] = ins[at][...]
        for dz in range(NZ if wide else 0):
            lanes = slice((dz % 2) * rows, (dz % 2 + 1) * rows)
            parts = [group[dz // 2].astype(F32)[:, lanes] for group in given]
            made[-NZ + dz][...] = jnp.concatenate(parts, axis=1).astype(BF)

    made = list(call(body, outs, [ids, *pieces, *groups], after=after))
    return (made[:1] if count else []) + [made[-NZ:]] * wide


def regroup_back(ids, both, after=()):
    part, width = both[0].shape
    rows = width // 2

    def body(ids, *rest):
        ins, outs = rest[:NZ], rest[NZ:]
        for r in range(2):
            lanes = slice(r * rows, (r + 1) * rows)
            for pair in range(NZ // 2):
                parts = [ins[2 * pair + k][...].astype(F32)[:, lanes] for k in range(2)]
                outs[r][pair] = jnp.concatenate(parts, axis=1).astype(BF)

    return call(body, [((NZ // 2, part, width), BF)] * 2, [ids, *both], after=after, flops=EARLY)


def join_weight(ids, blocks):
    part, width = blocks[0].shape
    rows = width // 2

    def body(ids, *rest):
        ins, (wide, tall), joined = rest[:NZ], rest[NZ : NZ + 2], rest[NZ + 2]
        z, x = ids[0], ids[1]
        for dz in range(NZ):
            source = mod(z - dz)
            both = ins[dz][...].astype(F32)
            for r in range(2):
                base = (flip(x, r) * 2 + source // 2) * part
                at = pl.ds(pl.multiple_of(base, 8), part)
                joined[lax.rem(source, 2), at, :] = both[:, r * rows : (r + 1) * rows]
        for half in range(2):
            at = pl.ds(half * 2 * part, 2 * part)
            both = jnp.concatenate([joined[0, at, :], joined[1, at, :]], axis=1)
            wide[at, :] = both.astype(BF)
        for y in range(2):
            tall[pl.ds(y * rows, rows), :] = joined[y].T.astype(BF)

    return call(
        body,
        [((4 * part, 2 * rows), BF), ((2 * rows, 4 * part), BF)],
        [ids, *blocks],
        [pltpu.VMEM((2, 4 * part, rows), F32)],
        flops=EARLY,
    )


def halves(array, axis):
    half = array.shape[axis] // 2
    return lax.slice_in_dim(array, 0, half, axis=axis), lax.slice_in_dim(array, half, 2 * half, axis=axis)


def along_z(piece):
    return [piece] + [over_z(piece, dz) for dz in range(1, NZ)]


def stacked(arrays, rank):
    found = []
    for at, array in enumerate(arrays):
        found += [(at, None)] if len(array.shape) == rank else [(at, k) for k in range(array.shape[0])]
    return found


def corner(ids, from_x, from_y, axis, after=()):
    lists = [stacked(part, 2) for part in (from_x, from_y)]
    piece = from_x[0].shape[-2:]
    half = tuple(extent // 2 if at == axis else extent for at, extent in enumerate(piece))

    def body(ids, *rest):
        ins = rest[: len(from_x)], rest[len(from_x) : -2]
        for k in range(2):
            cut = (slice(None),) * axis + (pl.ds(k * half[axis], half[axis]),)
            for dz, (at, index) in enumerate(lists[k]):
                ref = ins[k][at] if index is None else ins[k][at].at[index]
                rest[-2 + k][dz] = ref[cut]

    return call(body, [((NZ,) + half, BF)] * 2, [ids, *from_x, *from_y], after=after)


def add_diagonal(ids, parts, axis, after=()):
    _, to_x, to_y, at_x, at_y = parts
    half = at_x.shape[axis + 1]

    def body(ids, to_x, to_y, at_x, at_y, out_x, out_y):
        cuts = [(slice(None),) * (axis + 1) + (pl.ds(k * half, half),) for k in range(2)]
        for k, (to, came, out) in enumerate(((to_x, at_x, out_x), (to_y, at_y, out_y))):
            out[cuts[k]] = (to[cuts[k]] + came[...].astype(F32)).astype(BF)
            out[cuts[1 - k]] = to[cuts[1 - k]].astype(BF)

    return call(body, [(to_x.shape, BF)] * 2, [ids, to_x, to_y, at_x, at_y], after=after)


def add_plane(ids, own, from_x, from_y, after=()):
    def body(ids, own, from_x, from_y, *outs):
        for step in range(NZ):
            plane = own[step] + from_x[step].astype(F32) + from_y[step].astype(F32)
            outs[step][...] = plane.astype(outs[step].dtype)

    outs = [(own.shape[1:], BF)] * (NZ - 1) + [(own.shape[1:], F32)]
    return call(body, outs, [ids, own, from_x, from_y], after=after)


def total_of(own, others):
    total = own[...]
    for other in others:
        total = total + other[...].astype(F32)
    return total


def add_all(ids, own, others):
    def body(ids, own, *rest):
        rest[-1][...] = total_of(own, rest[:-1])

    return call(body, [(own.shape, F32)], [ids, own, *others])[0]


def partial_gates(ids, wide, near, from_x, from_y, diagonal, channel_pieces, after=()):
    total, depth = wide.shape
    part = total // 4
    rows = depth // 2
    if channel_pieces:
        own, length = near.shape[-2:]
    else:
        length = near.shape[-1] * 8
    found = [near, from_x, from_y, *diagonal]

    def body(ids, w, *rest):
        ins, (kept, mine, theirs, u, done) = rest[:-5], rest[-5:]
        z, x, y, c = ids[0], ids[1], ids[2], ids[3]

        def lay(dz, carry):
            near, at_x, at_y, diag_a, diag_b = [part.at[dz] for part in ins]
            source = mod(z - dz)
            if channel_pieces:
                half = length // 2
                for other in range(2):
                    row = pl.multiple_of(flip(y, other) * rows + source * 2 * own, 16)
                    for k in range(2):
                        cols = pl.ds(k * half, half)
                        if other:
                            a, b = at_y[:, cols], (diag_a, diag_b)[k][...]
                        else:
                            a, b = near[:, cols], at_x[:, cols]
                        a, b = a.astype(F32), b.astype(F32)
                        pair = jnp.concatenate([jnp.where(x == 0, a, b), jnp.where(x == 0, b, a)], axis=0)
                        u[pl.ds(row, 2 * own), cols] = pair.astype(BF)
            else:
                block = length // 8
                here = pl.ds(pl.multiple_of((source * 2 + x) * block, block), block)
                there = pl.ds(pl.multiple_of((source * 2 + 1 - x) * block, block), block)
                top = pl.multiple_of(y * rows, 16)
                low = pl.multiple_of((1 - y) * rows, 16)
                u[pl.ds(top, rows), here] = near[...]
                u[pl.ds(top, rows), there] = at_x[...]
                u[pl.ds(low, rows), here] = at_y[...]
                u[pl.ds(low, rows // 2), there] = diag_a[...]
                u[pl.ds(pl.multiple_of(low + rows // 2, 16), rows // 2), there] = diag_b[...]
            return carry

        lax.fori_loop(0, NZ, lay, 0)
        keep = pltpu.make_async_copy(u, kept.at[0], done)
        keep.start()
        lane = lax.broadcasted_iota(jnp.int32, (part, WIDE), 1)

        def step(cols, k, carry):
            lasts = []
            for out, core, before in ((mine, c, carry[0]), (theirs, 1 - c, carry[1])):
                rows = pl.ds(pl.multiple_of(core * 2 * part, 16), 2 * part)
                made = jnp.dot(w[rows, :], u[:, cols], preferred_element_type=F32)
                prev = made[:part]
                out[:, cols] = made[part:] + jnp.where(lane == 0, before, pltpu.roll(prev, 1, 1))
                lasts.append(prev[:, WIDE - 1 :])
            return tuple(lasts)

        zero = jnp.zeros((part, 1), F32)
        spans(length, step, (zero, zero), span=WIDE)
        keep.wait()

    return call(
        body,
        [roomy((depth, length), BF), ((part, length), F32), ((part, length), F32)],
        [ids, wide, *found],
        [pltpu.VMEM((depth, length), BF), pltpu.SemaphoreType.DMA],
        after=after,
        flops=2 * total * depth * length,
        far_out=(0,),
    )


def spans(length, step, carry, backward=False, span=SPAN):
    count = length // span

    def run(n, carry):
        k = count - 1 - n if backward else n
        return step(pl.ds(pl.multiple_of(k * span, span), span), k, carry)

    return lax.fori_loop(0, count, run, carry)


def scan_span(forget, driven, carry, backward):
    own, length = driven.shape
    lane = lax.broadcasted_iota(jnp.int32, (own, LANES), 1)
    blocks = [slice(at, at + LANES) for at in range(0, length, LANES)]
    reach, state = [forget[:, cols] for cols in blocks], [driven[:, cols] for cols in blocks]
    by = 1
    while by < LANES:
        shift = LANES - by if backward else by
        inside = lane < LANES - by if backward else lane >= by
        for at in range(len(blocks)):
            r, s = reach[at], state[at]
            state[at] = s + jnp.where(inside, r * pltpu.roll(s, shift, 1), 0.0)
            reach[at] = jnp.where(inside, r * pltpu.roll(r, shift, 1), r)
        by *= 2
    for at in range(len(blocks))[:: -1 if backward else 1]:
        state[at] = state[at] + reach[at] * carry
        carry = state[at][:, :1] if backward else state[at][:, LANES - 1 :]
    return jnp.concatenate(state, axis=1), carry


def squash(value):
    return 1.0 / (1.0 + jnp.exp(-value))


def forward_scan(mine, theirs, bias, cand, forg, outg, cells, result):
    own, length = cells.shape

    def step(cols, k, carry):
        gates = []
        for g in range(3):
            rows = pl.ds(g * own, own)
            gates.append(mine[rows, cols] + theirs[rows, cols] + bias[rows, :])
        candidate, forget, outgate = jnp.tanh(gates[0]), squash(gates[1]), squash(gates[2])
        state, carry = scan_span(forget, (1.0 - forget) * candidate, carry, False)
        cand[:, cols], forg[:, cols], outg[:, cols], cells[:, cols] = candidate, forget, outgate, state
        result(cols, outgate * state)
        return carry

    spans(length, step, jnp.zeros((own, 1), F32))


def backward_scan(grad_of, cand, forg, outg, cells, gate_grad):
    own, length = cells.shape
    lane = lax.broadcasted_iota(jnp.int32, (own, SPAN), 1)

    def step(cols, k, carry):
        adjoint_after, forget_after = carry
        grad, a, f, o, now = grad_of(cols), cand[:, cols], forg[:, cols], outg[:, cols], cells[:, cols]
        later = jnp.where(lane == SPAN - 1, forget_after, pltpu.roll(f, SPAN - 1, 1))
        adjoint, adjoint_first = scan_span(later, grad * o, adjoint_after, True)
        last = cells[:, pl.ds(pl.multiple_of(jnp.maximum(k * SPAN - LANES, 0), LANES), LANES)][:, LANES - 1 :]
        before = jnp.where(lane == 0, jnp.where(k == 0, 0.0, last), pltpu.roll(now, 1, 1))
        away = 1.0 - f
        gate_grad[:, cols] = jnp.concatenate(
            [
                adjoint * away * (1.0 - a * a),
                adjoint * (before - a) * f * away,
                grad * now * o * (1.0 - o),
            ],
            axis=0,
        ).astype(BF)
        return adjoint_first, f[:, :1]

    zero = jnp.zeros((own, 1), F32)
    spans(length, step, (zero, zero), True)


def first_cells(ids, mine, theirs, bias, after=()):
    part, length = mine.shape
    own = part // 3

    def body(ids, mine, theirs, bias, hidden, kept, *rest):
        made, done = rest[:4], rest[4]

        def result(cols, value):
            hidden[:, cols] = value.astype(BF)

        forward_scan(mine, theirs, bias, *made, result)
        copies = [pltpu.make_async_copy(made[at], kept.at[at], done.at[at]) for at in range(4)]
        for copy in copies:
            copy.start()
        for copy in copies:
            copy.wait()

    return call(
        body,
        [((own, length), BF), roomy((own, length), F32)],
        [ids, mine, theirs, bias],
        [pltpu.VMEM((own, length), F32)] * 4 + [pltpu.SemaphoreType.DMA((4,))],
        after=after,
        far_out=(1,),
    )


def first_gate_grad(ids, own, others, saved, after=()):
    channels, length = own.shape

    def body(ids, own, *rest):
        ins, held, gate_grad = rest[: len(others)], rest[-5:-1], rest[-1]

        def grad_of(cols):
            total = own[:, cols]
            for other in ins:
                total = total + other[:, cols].astype(F32)
            return total

        backward_scan(grad_of, *held, gate_grad)

    args = [ids, own, *others, *[saved[at] for at in range(4)]]
    return call(body, [((3 * channels, length), BF)], args, after=after)[0]


def second_cells(ids, mine, theirs, bias, cot_pieces):
    part, length = mine.shape
    own = part // 3
    block = length // 8

    def body(ids, mine, theirs, bias, *rest):
        cots, outs, gate_grad = rest[:NZ], rest[NZ : NZ + 2], rest[NZ + 2]
        grad, cand, forg, outg, cells, made = rest[NZ + 3 :]
        z, x = ids[0], ids[1]
        for dz in range(NZ):
            for dx in range(2):
                i = mod(z - dz) * 2 + flip(x, dx)
                grad[:, pl.ds(pl.multiple_of(i * block, block), block)] = cots[dz][dx]

        def result(cols, value):
            made[:, cols] = value.astype(BF)

        forward_scan(mine, theirs, bias, cand, forg, outg, cells, result)
        for dz in range(NZ):
            for dx in range(2):
                i = mod(z + dz) * 2 + flip(x, dx)
                outs[dx][dz] = made[:, pl.ds(pl.multiple_of(i * block, block), block)]
        backward_scan(lambda cols: grad[:, cols].astype(F32), cand, forg, outg, cells, gate_grad)

    made = call(
        body,
        [((NZ, own, block), BF)] * 2 + [((part, length), BF)],
        [ids, mine, theirs, bias, *cot_pieces],
        [pltpu.VMEM((own, length), BF)] + [pltpu.VMEM((own, length), F32)] * 4 + [pltpu.VMEM((own, length), BF)],
    )
    return made[:2], made[2]


def split_cotangent(ids, cotangent):
    channels, block = cotangent.shape
    own = channels // 8

    def body(ids, cot, *rest):
        outs, wide = rest[:2], rest[2]
        wide[...] = cot[...].astype(F32)
        for dz in range(NZ):
            for dx in range(2):
                i = mod(ids[0] + dz) * 2 + flip(ids[1], dx)
                outs[dx][dz] = wide[pl.ds(pl.multiple_of(i * own, 8), own), :].astype(BF)

    return call(body, [((NZ, own, block), BF)] * 2, [ids, cotangent], [pltpu.VMEM((channels, block), F32)])


def pair_up(ids, first, second, after=()):
    shape = (2,) + first.shape[1:]

    def body(ids, first, second, *outs):
        for at in range(NZ):
            outs[at][0] = first[at]
            outs[at][1] = second[at]

    return call(body, [(shape, BF)] * NZ, [ids, first, second], after=after)


def join_outputs(ids, pieces):
    _, own, block = pieces[0].shape

    def body(ids, *rest):
        ins, out, wide = rest[:NZ], rest[NZ], rest[NZ + 1]
        for dz in range(NZ):
            for dx in range(2):
                i = mod(ids[0] - dz) * 2 + flip(ids[1], dx)
                wide[pl.ds(pl.multiple_of(i * own, 8), own), :] = ins[dz][dx].astype(F32)
        out[...] = wide[...].astype(BF)

    return call(body, [((8 * own, block), BF)], [ids, *pieces], [pltpu.VMEM((8 * own, block), F32)])[0]


def input_parts(ids, tall, mine, theirs, channel_pieces, after=()):
    depth, total = tall.shape
    part, length = mine.shape
    rows = depth // 2
    own = rows // 8
    block = length // 8
    shape = (NZ, own, length) if channel_pieces else (NZ, rows, block)
    half = (NZ, own, length // 2) if channel_pieces else (NZ, rows // 2, block)

    def body(ids, w, mine, theirs, grads, *rest):
        outs, v = rest[:5], rest[5]
        z, x, y, c = ids[0], ids[1], ids[2], ids[3]
        lane = lax.broadcasted_iota(jnp.int32, (part, WIDE), 1)

        def product(cols, k, carry):
            firsts = []
            for given, core, first in ((mine, c, carry[0]), (theirs, 1 - c, carry[1])):
                now = given[:, cols].astype(F32)
                later = jnp.where(lane == WIDE - 1, first, pltpu.roll(now, WIDE - 1, 1))
                at = pl.ds(pl.multiple_of(core * 2 * part, 16), 2 * part)
                grads[at, cols] = jnp.concatenate([later, now], axis=0).astype(BF)
                firsts.append(now[:, :1])
            v[:, cols] = jnp.dot(w[...], grads[:, cols], preferred_element_type=F32)
            return tuple(firsts)

        zero = jnp.zeros((part, 1), F32)
        spans(length, product, (zero, zero), True, WIDE)

        def hand_out(step, carry):
            target = mod(z + 1 + step)

            def piece(dx, dy, k=None):
                i = target * 2 + flip(x, dx)
                if channel_pieces:
                    row = pl.multiple_of(flip(y, dy) * rows + i * own, 8)
                    cols = slice(None) if k is None else pl.ds(k * length // 2, length // 2)
                    return v[pl.ds(row, own), cols]
                cols = pl.ds(pl.multiple_of(i * block, block), block)
                row = flip(y, dy) * rows
                if k is None:
                    return v[pl.ds(pl.multiple_of(row, 8), rows), cols]
                return v[pl.ds(pl.multiple_of(row + k * rows // 2, 8), rows // 2), cols]

            outs[0][step] = piece(0, 0)
            outs[1][step] = piece(1, 0)
            outs[2][step] = piece(0, 1)
            outs[3][step] = piece(1, 1, 0).astype(BF)
            outs[4][step] = piece(1, 1, 1).astype(BF)
            return carry

        lax.fori_loop(0, NZ, hand_out, 0)

    made = call(
        body,
        [((total, length), BF), (shape, F32), (shape, F32), (shape, F32), (half, BF), (half, BF)],
        [ids, tall, mine, theirs],
        [pltpu.VMEM((depth, length), F32)],
        after=after,
        flops=2 * depth * total * length,
    )
    return made[0], made[1:]


def weight_blocks(ids, grads, u, after=()):
    total, length = grads.shape
    depth = u.shape[0]
    part, rows = total // 4, depth // 2

    def body(ids, grads, u, *rest):
        outs, made = rest[:NZ], rest[NZ]
        z, x = ids[0], ids[1]
        contract = (((1,), (1,)), ((), ()))

        def product(y, carry):
            at = pl.ds(pl.multiple_of(y * rows, 16), rows)
            made[y] = lax.dot_general(grads[...], u[at, :], contract, preferred_element_type=F32)
            return carry

        lax.fori_loop(0, 2, product, 0)
        sums = lax.dot_general(jnp.ones((8, length), BF), grads[...], contract, preferred_element_type=F32)
        line = lax.broadcasted_iota(jnp.int32, (8, part), 0)
        tails = []
        for r in range(2):
            bias = jnp.where(flip(x, r) == 0, sums[:, part : 2 * part], sums[:, 3 * part : 4 * part])
            high = bias.astype(BF).astype(F32)
            tail = jnp.where(line == 0, high, jnp.where(line == 1, bias - high, 0.0))
            tails.append(jnp.concatenate([tail, jnp.zeros((8, rows - part), F32)], axis=1))
        for dz in range(NZ):
            source = mod(z - dz)
            both = []
            for r in range(2):
                at = pl.ds(pl.multiple_of((flip(x, r) * 2 + source // 2) * part, 8), part)
                both.append(jnp.concatenate([made[lax.rem(source, 2), at, :], tails[r]], axis=0))
            outs[dz][...] = jnp.concatenate(both, axis=1).astype(BF)

    return call(
        body,
        [((part + 8, 2 * rows), BF)] * NZ,
        [ids, grads, u],
        [pltpu.VMEM((2, total, rows), F32)],
        after=after,
        flops=2 * depth * total * length,
    )


def unpack_weight(ids, groups):
    _, height, width = groups[0].shape
    part, rows = height - 8, width // 2
    own = part // 3
    columns = own * 8

    def body(ids, r0, r1, out, bias, joined):
        z, c = ids[0], ids[3]
        for r, group in enumerate((r0, r1)):
            for pair in range(NZ // 2):
                both = group[pair].astype(F32)
                for k in range(2):
                    i = mod(z + 2 * pair + k) * 2 + flip(c, r)
                    block = both[:, k * rows : (k + 1) * rows]
                    for g in range(3):
                        at = pl.ds(pl.multiple_of(i * own, 8), own)
                        joined[g, at, :] = block[g * own : (g + 1) * own]
                    bias[pl.ds(i, 1), :] = (block[part : part + 1] + block[part + 1 : part + 2])[:, :part]

        def turn(g, carry):
            out[g] = joined[g].T
            return carry

        lax.fori_loop(0, 3, turn, 0)

    grad, bias = call(
        body,
        [((3, rows, columns), F32), ((8, part), F32)],
        [ids, *groups],
        [pltpu.VMEM((3, columns, rows), F32)],
    )
    bias = jnp.transpose(bias.reshape(8, 3, own), (1, 0, 2)).reshape(3, columns)
    return grad, bias


def back_rounds(ids, parts, blocks, axis, after=()):
    blocks = blocks_over_z(blocks, -1)
    parts = [*parts[:3], over_y(parts[3]), over_x(parts[4])]
    sent_x, sent_y = add_diagonal(ids, parts, axis, after=after)
    groups = regroup_back(ids, blocks)
    *planes, own = add_plane(ids, parts[0], over_x(sent_x), over_y(sent_y), after=groups)
    others = [over_z(plane, step + 1) for step, plane in enumerate(planes)]
    return own, others, blocks_over_x(groups, True)


def owned_channels(inputs, first_weight, first_bias, second_weight, second_bias, cotangent):
    tm, mp = lax.axis_index("tm"), lax.axis_index("mp")
    ids = jnp.stack([tm // 2, tm % 2, mp // 2, mp % 2]).astype(jnp.int32)

    *w1, column_1 = pack_weight(ids, first_weight, first_bias)
    near, w1 = regroup(ids, along_z(inputs[0].T), blocks_over_x(w1))
    from_x, from_y = over_x(near), over_y(near)
    wide_1, tall_1 = join_weight(ids, blocks_over_z(w1, 1))
    cot_here, cot_there = split_cotangent(ids, cotangent[0].T)
    diag = corner(ids, [from_x], [from_y], 0)
    (cot_there,) = relay([cot_there], [diag[0]])
    diag = [over_y(diag[0]), over_x(diag[1])]
    cots = pair_up(ids, cot_here, over_x(cot_there))
    *w2, column_2 = pack_weight(ids, second_weight, second_bias)

    cots = [cots[0]] + [over_z(cots[dz], dz) for dz in range(1, NZ)]
    u, mine, theirs = partial_gates(ids, wide_1, near, from_x, from_y, diag, False, after=[*w2, *cots])
    theirs = over_core(theirs)
    hidden, saved = first_cells(ids, mine, theirs, column_1)

    w2 = blocks_over_x(relay(w2, [hidden]))
    near, w2 = regroup(ids, along_z(hidden), w2)
    from_x, from_y = [over_x(near)], [over_y(near)]
    wide_2, tall_2 = join_weight(ids, blocks_over_z(w2, 1))
    diag = corner(ids, from_x, from_y, 1)
    diag = [over_y(diag[0]), over_x(diag[1])]
    h, mine, theirs = partial_gates(ids, wide_2, near, *from_x, *from_y, diag, True)
    outs, gate_grad = second_cells(ids, mine, over_core(theirs), column_2, cots)

    grads, parts = input_parts(ids, tall_2, gate_grad, over_core(gate_grad), True)
    outs = pair_up(ids, outs[0], over_x(outs[1]), after=[grads])
    dw2 = weight_blocks(ids, grads, h[0], after=outs)
    plane, others, dw2 = back_rounds(ids, parts, dw2, 1)
    gate_grad = first_gate_grad(ids, plane, others, saved, after=dw2)

    grads, parts = input_parts(ids, tall_1, gate_grad, over_core(gate_grad), False)
    outs = [outs[0]] + [over_z(outs[dz], dz) for dz in range(1, NZ)]
    dw1 = weight_blocks(ids, grads, u[0])
    second_grad, second_bias_grad = unpack_weight(ids, dw2)
    outputs = join_outputs(ids, outs)
    plane, others, dw1 = back_rounds(ids, parts, dw1, 0, [second_grad, outputs])
    input_grad = add_all(ids, plane, others)
    first_grad, first_bias_grad = unpack_weight(ids, dw1)
    first_grad, second_grad = (jnp.transpose(grad, (1, 0, 2)) for grad in (first_grad, second_grad))
    return (
        outputs.T[None],
        input_grad.T[None],
        first_grad,
        first_bias_grad,
        second_grad,
        second_bias_grad,
    )


def prefix(value, axis, join, neutral, backward):
    count, mine = (lax.axis_size(axis), lax.axis_index(axis))
    pieces = jax.tree.map(lambda part: lax.all_gather(part, axis), value)
    if backward:
        pieces = jax.tree.map(lambda part: part[::-1], pieces)
        mine = count - 1 - mine
    total = jax.tree.map(
        lambda part, zero: jnp.full_like(part, 0) + jnp.asarray(zero, part.dtype), value, neutral
    )

    def hop(position, total):
        longer = join(total, jax.tree.map(lambda part: part[position], pieces))
        return jax.tree.map(lambda new, old: jnp.where(position < mine, new, old), longer, total)

    return lax.fori_loop(0, count - 1, hop, total)


def passed_along(array, axis, by):
    size = lax.axis_size(axis)
    pairs = [(i, i + by) for i in range(size) if 0 <= i + by < size]
    return lax.ppermute(array, axis, pairs)


def affine_join(earlier, later):
    return (earlier[0] * later[0], later[0] * earlier[1] + later[1])


def weight_view(gathered):
    return gathered.reshape(2, gathered.shape[0] // 2, gathered.shape[1] * gathered.shape[2])


def span_prefix(product, offset):
    identity = (jnp.ones_like(product), jnp.zeros_like(offset))
    result = prefix((product, offset), "tm", affine_join, identity, False)
    return result[1]


def span_suffix(product, offset):
    identity = (jnp.ones_like(product), jnp.zeros_like(offset))
    result = prefix((product, offset), "tm", affine_join, identity, True)
    return result[1]


def forward_layer(layer_in, view, bias):
    seq_count, length, channels = layer_in.shape
    prev_row = passed_along(layer_in[:, length - 1 :], "tm", 1)
    previous = jnp.concatenate([prev_row, layer_in[:, : length - 1]], axis=1)
    stacked = jnp.stack([previous, layer_in])
    summed = jnp.einsum(
        "jsck,jkn->scn",
        lax.all_gather(stacked, "mp", axis=3, tiled=True),
        view,
        preferred_element_type=jnp.float32,
    )
    gates = summed.reshape(seq_count, length, 3, channels) + bias
    candidate = jnp.tanh(gates[:, :, 0])
    forget = jax.nn.sigmoid(gates[:, :, 1])
    outgate = jax.nn.sigmoid(gates[:, :, 2])
    product, offset = lax.associative_scan(
        affine_join, (forget, (1.0 - forget) * candidate), axis=1
    )
    carry_in = span_prefix(product[:, length - 1], offset[:, length - 1])
    cells = offset + product * carry_in[:, None]
    cells_prev = jnp.concatenate([carry_in[:, None], cells[:, : length - 1]], axis=1)
    return (outgate * cells, (stacked, candidate, forget, outgate, cells, cells_prev))


def backward_layer(grad_in, saved, view):
    stacked, candidate, forget, outgate, cells, cells_prev = saved
    seq_count, length, channels = grad_in.shape
    driven = grad_in * outgate
    next_forget = jnp.concatenate([forget[:, 1:], jnp.ones_like(forget[:, :1])], axis=1)
    reach, local_adj = lax.associative_scan(
        affine_join, (next_forget[:, ::-1], driven[:, ::-1]), axis=1
    )
    reach = reach[:, ::-1]
    local_adj = local_adj[:, ::-1]
    first_forget = forget[:, 0]
    incoming = span_suffix(first_forget * reach[:, 0], first_forget * local_adj[:, 0])
    adjoint = local_adj + reach * incoming[:, None]
    grad_cand = adjoint * (1.0 - forget) * (1.0 - candidate * candidate)
    grad_forget = adjoint * (cells_prev - candidate) * forget * (1.0 - forget)
    grad_outgate = grad_in * cells * outgate * (1.0 - outgate)
    gate_grad = jnp.stack([grad_cand, grad_forget, grad_outgate], axis=2).astype(jnp.bfloat16)
    flat_grad = gate_grad.reshape(seq_count, length, 3 * channels)
    bias_part = jnp.sum(gate_grad, axis=(0, 1), dtype=jnp.float32)
    back_both = jnp.einsum("scn,jkn->jsck", flat_grad, view, preferred_element_type=jnp.float32)
    from_prev = back_both[0]
    from_current = back_both[1]
    local_grad = from_current + jnp.concatenate(
        [from_prev[:, 1:], jnp.zeros_like(from_prev[:, :1])], axis=1
    )
    tail_rows = from_prev[:, :1]
    shard_grad, tail_shard = (
        lax.psum_scatter(local_grad, "mp", scatter_dimension=2, tiled=True),
        lax.psum_scatter(tail_rows, "mp", scatter_dimension=2, tiled=True),
    )
    tail_next = passed_along(tail_shard, "tm", -1)
    layer_grad = shard_grad + jnp.concatenate(
        [jnp.zeros_like(shard_grad[:, : length - 1]), tail_next], axis=1
    )
    weight_full = jnp.einsum(
        "jsck,scn->jkn",
        lax.all_gather(stacked, "mp", axis=3, tiled=True),
        flat_grad,
        preferred_element_type=jnp.float32,
    )
    weight_full = weight_full.reshape(2 * weight_full.shape[1], 3, channels)
    weight_shard = lax.psum_scatter(weight_full, "tm", scatter_dimension=0, tiled=True)
    bias_grad = lax.psum(bias_part, "tm")
    return (layer_grad, weight_shard, bias_grad)


def per_device(inputs, first_weight, first_bias, second_weight, second_bias, cotangent):
    full_first, full_second = (
        lax.all_gather(first_weight, "tm", axis=0, tiled=True),
        lax.all_gather(second_weight, "tm", axis=0, tiled=True),
    )
    view_first = weight_view(full_first)
    view_second = weight_view(full_second)
    hidden_out, saved_first = forward_layer(inputs, view_first, first_bias)
    hidden = hidden_out.astype(jnp.bfloat16)
    top_out, saved_second = forward_layer(hidden, view_second, second_bias)
    again_first, again_second = (
        lax.all_gather(first_weight, "tm", axis=0, tiled=True),
        lax.all_gather(second_weight, "tm", axis=0, tiled=True),
    )
    back_first = weight_view(again_first)
    back_second = weight_view(again_second)
    hidden_grad, second_weightgrad, second_biasgrad = backward_layer(
        cotangent.astype(jnp.float32), saved_second, back_second
    )
    input_grad, first_weightgrad, first_biasgrad = backward_layer(
        hidden_grad, saved_first, back_first
    )
    return (
        top_out.astype(jnp.bfloat16),
        input_grad,
        first_weightgrad,
        first_biasgrad,
        second_weightgrad,
        second_biasgrad,
    )


def choose(owned):
    def run(inputs, first_weight, *rest):
        sizes = inputs.shape[0] == 1 and inputs.shape[1] == 256 and first_weight.shape == (576, 3, 576)
        plan = owned_channels if owned and sizes else per_device
        return plan(inputs, first_weight, *rest)

    return run


def solution(mesh):
    placed = (
        P(None, "tm", "mp"),
        P("tm", None, "mp"),
        P(None, "mp"),
        P("tm", None, "mp"),
        P(None, "mp"),
        P(None, "tm", "mp"),
    )
    owned = mesh.shape["tm"] == 2 * NZ and mesh.shape["mp"] == 4
    return jax.shard_map(
        choose(owned),
        mesh=mesh,
        in_specs=placed,
        out_specs=(
            P(None, "tm", "mp"),
            P(None, "tm", "mp"),
            P("tm", None, "mp"),
            P(None, "mp"),
            P("tm", None, "mp"),
            P(None, "mp"),
        ),
        check_vma=False,
    )
```
